32 devices in a mesh: dp: 8 (over z, y), mp: 4 (over x, core).
Axes of the slice: x: 2, y: 2, z: 4, core: 2. Of those that a mesh axis runs over, the one named last changes fastest.
Arguments:
- post_stream: float32 [32768, 512], P(('dp', 'mp')), may hold values from -6 to 6
- pre_stream: float32 [32768, 512], P(('dp', 'mp')), may hold values from -6 to 6
- seq_lengths: int32 [8, 13], P('dp'), may hold values from 1 to 2048, 4096 in all within a row
- qkv_weight: bfloat16 [512, 3, 512], P(None, None, 'mp'), may hold values from -0.25 to 0.25
- query_bias: bfloat16 [512], P('mp'), may hold values from -3 to 3
- value_bias: bfloat16 [512], P('mp'), may hold values from -3 to 3
- out_weight: bfloat16 [512, 512], P('mp'), may hold values from -0.75 to 0.75
- out_bias: bfloat16 [512], replicated, may hold values from -2 to 2
- norm1_gain: bfloat16 [512], replicated, may hold values from 0.5 to 1.5
- norm1_shift: bfloat16 [512], replicated, may hold values from -2 to 2
- up_weight: bfloat16 [512, 2048], P(None, 'mp'), may hold values from -0.25 to 0.25
- up_bias: bfloat16 [2048], P('mp'), may hold values from -3 to 3
- down_weight: bfloat16 [2048, 512], P('mp'), may hold values from -0.1875 to 0.1875
- down_bias: bfloat16 [512], replicated, may hold values from -2 to 2
- norm2_gain: bfloat16 [512], replicated, may hold values from 0.5 to 1.5
- norm2_shift: bfloat16 [512], replicated, may hold values from -2 to 2
- post_cotan: float32 [32768, 512], P(('dp', 'mp')), may hold values from -6 to 6
- pre_cotan: float32 [32768, 512], P(('dp', 'mp')), may hold values from -6 to 6
Outputs:
- post_out: float32 [32768, 512], P(('dp', 'mp'))
- pre_out: float32 [32768, 512], P(('dp', 'mp'))
- post_grad: float32 [32768, 512], P(('dp', 'mp'))
- qkv_weight_grad: float32 [512, 3, 512], P(None, None, 'mp')
- query_bias_grad: float32 [512], P('mp')
- value_bias_grad: float32 [512], P('mp')
- out_weight_grad: float32 [512, 512], P('mp')
- out_bias_grad: float32 [512], replicated
- norm1_gain_grad: float32 [512], replicated
- norm1_shift_grad: float32 [512], replicated
- up_weight_grad: float32 [512, 2048], P(None, 'mp')
- up_bias_grad: float32 [2048], P('mp')
- down_weight_grad: float32 [2048, 512], P('mp')
- down_bias_grad: float32 [512], replicated
- norm2_gain_grad: float32 [512], replicated
- norm2_shift_grad: float32 [512], replicated
The draws below stay inside these ranges and needn't reach their ends.
Inputs may be any that keep to these rules, and one draw needn't show every extreme that they name: `seq_lengths`: row g serves group g: its first 12 entries are the lengths of the sequences packed in order from the group's first position, its last entry the number of padded positions at the end; each row sums to 4096, and its largest entry is 2048.
All inputs are finite; a program needn't handle non-finite values.
Results may differ from the reference program's by a relative error of at most 0.011.
The reference program's roundings to bfloat16 on the way count: a program that leaves them out, or rounds other values in their place, can miss the bound.
Values may be sent and summed in bfloat16 or wider, within the bound.
A program may use at most 192 MiB of HBM per device.

```python
import math
import jax
import jax.numpy as jnp
import numpy as np
from jax import lax

D = 512
HEADS = 8
HEAD_DIM = 64
FF = 2048
SEQS = 12
GROUP_TOK = 4096
TOKENS = 32768
N_DP = 8


def block_levels(own_key, dims, shards, low, top_value):
    loudness, own = 1.0, jax.random.fold_in(own_key, 6)
    for axis_at, shards_of in shards:
        steps = jnp.exp(jax.random.uniform(jax.random.fold_in(own, axis_at), (shards_of,), jnp.float32, low / len(shards), top_value / len(shards)))
        loudness = loudness * jnp.repeat(steps, dims[axis_at] // shards_of).reshape([-1 if axis == axis_at else 1 for axis in range(len(dims))])
    return loudness


def split_up(amount, total, bound, slope):
    portions = [(1 << 20) // math.isqrt(grade ** slope) + 1 for grade in range(2, amount + 1)]
    surplus, given = total - bound - (amount - 1), [1] * (amount - 1)
    while surplus > 0:
        free = [i for i in range(amount - 1) if given[i] < bound]
        pool, remaining = sum([portions[i] for i in free]), surplus
        for i in free:
            extra = min(bound - given[i], max(1, remaining * portions[i] // pool), surplus)
            given[i] = given[i] + extra
            surplus = surplus - extra
    return np.array([bound] + given)


def ragged(rng, amount, total, bound, skew):
    if amount == 2:
        one = jax.random.randint(rng, (), max(1, total - bound), min(bound, total - 1) + 1)
        return jnp.stack([one, total - one])
    sizes = jnp.asarray(split_up(amount, total, bound, skew), jnp.int32)
    pairs = (amount - 1) // 2
    donor, taker = sizes[1:1 + 2 * pairs:2], sizes[2:2 + 2 * pairs:2]
    room = jnp.minimum(donor - 1, bound - taker)
    shifted = jax.random.randint(jax.random.fold_in(rng, 1), (pairs,), 0, 1 << 20) % (room + 1)
    sizes = sizes.at[1:1 + 2 * pairs:2].set(donor - shifted).at[2:2 + 2 * pairs:2].set(taker + shifted)
    return sizes[jax.random.permutation(jax.random.fold_in(rng, 2), amount)]


def noise(stream_key, extent, width, limit, split=(), held_as=jnp.bfloat16):
    entries = jax.random.normal(stream_key, extent, jnp.float32) * width
    if len(split) > 0:
        entries = block_levels(stream_key, extent, split, -0.22, 0.18) * entries
    return jnp.clip(entries, min=-limit, max=limit).astype(held_as)


def setup_inputs(seed: int = 0) -> dict:
    streams_of = jax.random.split(jax.random.key(seed), 19)
    return {
        "post_stream": noise(streams_of[0], (TOKENS, D), 1.0, 6.0, ((0, 32),), jnp.float32),
        "pre_stream": noise(streams_of[1], (TOKENS, D), 1.0, 6.0, ((0, 32),), jnp.float32),
        "seq_lengths": jax.vmap(lambda own: ragged(own, SEQS + 1, GROUP_TOK, GROUP_TOK // 2, 2))(jax.random.split(streams_of[2], N_DP)).reshape((N_DP, SEQS + 1)).astype(jnp.int32),
        "qkv_weight": noise(streams_of[3], (D, 3, D), D ** -0.5, 0.25, ((2, 4),)),
        "query_bias": noise(streams_of[4], (D,), 0.5, 3.0, ((0, 4),)),
        "value_bias": noise(streams_of[5], (D,), 0.5, 3.0, ((0, 4),)),
        "out_weight": noise(streams_of[6], (D, D), (D // 8) ** -0.5, 0.75, ((0, 4),)),
        "out_bias": noise(streams_of[7], (D,), 0.3, 2.0),
        "norm1_gain": jnp.clip(1.0 + 0.1 * jax.random.normal(streams_of[8], (D,), jnp.float32), 0.5, 1.5).astype(jnp.bfloat16),
        "norm1_shift": noise(streams_of[9], (D,), 0.3, 2.0),
        "up_weight": noise(streams_of[10], (D, FF), D ** -0.5, 0.25, ((1, 4),)),
        "up_bias": noise(streams_of[11], (FF,), 0.5, 3.0, ((0, 4),)),
        "down_weight": noise(streams_of[12], (FF, D), (FF // 2) ** -0.5, 0.1875, ((0, 4),)),
        "down_bias": noise(streams_of[13], (D,), 0.3, 2.0),
        "norm2_gain": jnp.clip(1.0 + 0.1 * jax.random.normal(streams_of[14], (D,), jnp.float32), 0.5, 1.5).astype(jnp.bfloat16),
        "norm2_shift": noise(streams_of[15], (D,), 0.3, 2.0),
        "post_cotan": noise(streams_of[16], (TOKENS, D), 1.0, 6.0, ((0, 32),), jnp.float32),
        "pre_cotan": noise(streams_of[17], (TOKENS, D), 1.0, 6.0, ((0, 32),), jnp.float32),
    }


EPSILON = 1e-05
PRECISE = lax.Precision.HIGHEST
MASKED = -1e+30

@jax.custom_vjp
def low(v):
    return lax.optimization_barrier(v.astype(jnp.bfloat16)).astype(jnp.float32)

@jax.custom_vjp
def low_back(v):
    return v

def low_keep(v):
    return (low(v), None)

def low_pass(kept, grad):
    return (grad,)

def back_keep(v):
    return (v, None)

def back_low(kept, grad):
    return (low(grad),)
low.defvjp(low_keep, low_pass)
low_back.defvjp(back_keep, back_low)

def gelu_tanh(value):
    return jax.nn.gelu(value, approximate=True)

def segment_ids(length_row):
    bounds = jnp.cumsum(length_row[:SEQS], dtype=jnp.int32)
    places = jnp.arange(GROUP_TOK, dtype=jnp.int32)
    segment = lax.optimization_barrier(jnp.sum((places[None, :] >= bounds[:, None]).astype(jnp.int32), axis=0, dtype=jnp.int32))
    return jnp.where(places >= bounds[SEQS - 1], SEQS + places, segment)

def block_mask(segment, start, block_rows):
    query_segment = lax.dynamic_slice_in_dim(segment, start, block_rows, 0)
    query_place = start + jnp.arange(block_rows, dtype=jnp.int32)
    key_place = jnp.arange(segment.shape[0], dtype=jnp.int32)
    return (query_segment[:, None] == segment[None, :]) & (key_place[None, :] <= query_place[:, None])

def layer_norm(summed, norm_gain, norm_shift):
    center = summed - lax.optimization_barrier(jnp.mean(summed, axis=-1, keepdims=True))
    inverse = lax.rsqrt(lax.optimization_barrier(jnp.mean(center * center, axis=-1, keepdims=True)) + EPSILON)
    return center * inverse * norm_gain + norm_shift

def attend_group(shaped, segment):
    query = shaped[:, 0]
    keys = shaped[:, 1]
    values = shaped[:, 2]
    block_rows = min(512, GROUP_TOK)
    starts = jnp.arange(GROUP_TOK // block_rows, dtype=jnp.int32) * block_rows

    def one_block(start):
        query_block = lax.dynamic_slice_in_dim(query, start, block_rows, 0)
        raw = jnp.einsum('qhd,khd->hqk', query_block, keys, precision=PRECISE) * HEAD_DIM ** (-0.5)
        allowed = block_mask(segment, start, block_rows)
        scores = low_back(jnp.where(allowed[None], raw, MASKED))
        attention = low(jax.nn.softmax(scores, axis=-1))
        return jnp.einsum('hqk,khd->qhd', attention, values, precision=PRECISE)
    blocks = lax.map(jax.checkpoint(one_block), starts)
    return blocks.reshape(GROUP_TOK, HEADS, HEAD_DIM)

def forward(post_stream, qkv_weight, query_bias, value_bias, out_weight, out_bias, norm1_gain, norm1_shift, up_weight, up_bias, down_weight, down_bias, norm2_gain, norm2_shift, pre_stream, segment):
    total_rows = post_stream.shape[0]
    tokens_low = low(post_stream)
    projected = jnp.dot(tokens_low, qkv_weight.reshape(D, 3 * D), precision=PRECISE).reshape(total_rows, 3, D)
    bias_stack = jnp.stack([query_bias, jnp.zeros_like(query_bias), value_bias])
    qkv_low = low(low_back(projected + bias_stack[None]))
    shaped = qkv_low.reshape(GROUP_TOK, 3, HEADS, HEAD_DIM)
    attended = attend_group(shaped, segment).reshape(total_rows, D)
    attended = low_back(low(attended))
    branch = low_back(jnp.dot(attended, out_weight, precision=PRECISE) + out_bias)
    mid = layer_norm(post_stream + branch, norm1_gain, norm1_shift)
    pre_mid = pre_stream + branch
    pre_act = low_back(jnp.dot(low(mid), up_weight, precision=PRECISE) + up_bias)
    hidden = low(gelu_tanh(pre_act))
    ffn = low_back(jnp.dot(hidden, down_weight, precision=PRECISE) + down_bias)
    return (layer_norm(mid + ffn, norm2_gain, norm2_shift), pre_mid + ffn)

def reference(post_stream, pre_stream, seq_lengths, qkv_weight, query_bias, value_bias, out_weight, out_bias, norm1_gain, norm1_shift, up_weight, up_bias, down_weight, down_bias, norm2_gain, norm2_shift, post_cotan, pre_cotan):
    segments = jax.vmap(segment_ids)(seq_lengths)
    weights = (qkv_weight.astype(jnp.float32), query_bias.astype(jnp.float32), value_bias.astype(jnp.float32), out_weight.astype(jnp.float32), out_bias.astype(jnp.float32), norm1_gain.astype(jnp.float32), norm1_shift.astype(jnp.float32), up_weight.astype(jnp.float32), up_bias.astype(jnp.float32), down_weight.astype(jnp.float32), down_bias.astype(jnp.float32), norm2_gain.astype(jnp.float32), norm2_shift.astype(jnp.float32))
    post_groups = post_stream.reshape(N_DP, GROUP_TOK, D)
    pre_groups = pre_stream.reshape(N_DP, GROUP_TOK, D)
    post_cotans = post_cotan.reshape(N_DP, GROUP_TOK, D)
    pre_cotans = pre_cotan.reshape(N_DP, GROUP_TOK, D)

    def one_group(totals, packed):
        post_value, pre_value, segment, post_back, pre_back = packed

        def run_layer(post_piece, qkv_value, query_value, value_value, out_value, out_shift, gain_one, shift_one, up_value, up_shift, down_value, down_shift, gain_two, shift_two):
            return forward(post_piece, qkv_value, query_value, value_value, out_value, out_shift, gain_one, shift_one, up_value, up_shift, down_value, down_shift, gain_two, shift_two, pre_value, segment)
        outputs, pullback = jax.vjp(run_layer, post_value, *weights)
        grads = pullback((post_back, pre_back))
        totals = tuple((total + grad for total, grad in zip(totals, grads[1:])))
        return (totals, (outputs[0], outputs[1], grads[0]))
    zeros = tuple((jnp.zeros_like(weight) for weight in weights))
    sums, stacked = lax.scan(one_group, zeros, (post_groups, pre_groups, segments, post_cotans, pre_cotans))
    post_out = stacked[0].reshape(TOKENS, D)
    pre_out = stacked[1].reshape(TOKENS, D)
    post_grad = stacked[2].reshape(TOKENS, D)
    return (post_out, pre_out, post_grad, sums[0], sums[1], sums[2], sums[3], sums[4], sums[5], sums[6], sums[7], sums[8], sums[9], sums[10], sums[11], sums[12])
```

```python
import functools

import jax
import jax.numpy as jnp
from jax import lax
from jax.experimental import pallas as pl
from jax.experimental.pallas import tpu as pltpu
from jax.sharding import PartitionSpec as P

HEAD_DIM = 64
EPSILON = 1e-05
MASKED = -1e30
MP = 4
TILE = 256
MESH = pl.DeviceIdType.MESH
BF16 = jnp.bfloat16
F32 = jnp.float32
ANY = pl.BlockSpec(memory_space=pl.ANY)
VMEM = pl.BlockSpec(memory_space=pltpu.VMEM)
NT = (((1,), (1,)), ((), ()))
TN = (((0,), (0,)), ((), ()))
SQRT_2_OVER_PI = 0.7978845608028654


def ds(start, size):
    return pl.ds(pl.multiple_of(start, size), size)


def mp_peers():
    me = lax.axis_index("mp")
    sib = me + 1 - 2 * (me % 2)
    across = (me + 2) % MP
    diagonal = (sib + 2) % MP
    return me, sib, across, diagonal


def greet(devices):
    barrier = pltpu.get_barrier_semaphore()
    for device in devices:
        pl.semaphore_signal(barrier, inc=1, device_id=device, device_id_type=MESH)
    pl.semaphore_wait(barrier, len(devices))


def remote(src, dst, send_sem, recv_sem, device):
    return pltpu.make_async_remote_copy(
        src_ref=src,
        dst_ref=dst,
        send_sem=send_sem,
        recv_sem=recv_sem,
        device_id=device,
        device_id_type=MESH,
    )


def dot(a, b, dims=(((1,), (0,)), ((), ()))):
    return lax.dot_general(a, b, dims, preferred_element_type=F32)


def dma_sems(*shape):
    return pltpu.SemaphoreType.DMA(shape)


def project_kernel(
    post, w, prm,
    tok_t_out, q_out, k_out, v_out, kt_out, vt_out,
    stage, tok, tok_t, q_s, k_s, v_s, kt_s, vt_s,
    in_sem, send_x, recv_x, send_c, recv_c, send_f, recv_f, out_sem,
):
    me, sib, across, diagonal = mp_peers()
    dp = lax.axis_index("dp")
    rows = post.shape[0]
    width = post.shape[1]
    chunk = TILE
    count = rows // chunk
    loads = [
        pltpu.make_async_copy(post.at[pl.ds(c * chunk, chunk)], stage.at[pl.ds(c * chunk, chunk)], in_sem.at[c])
        for c in range(count)
    ]
    for load in loads:
        load.start()
    greet([(dp, sib), (dp, across)])

    def piece(owner, c):
        return ds(owner * rows + c * chunk, chunk)

    def to_across(c):
        here = piece(me, c)
        return remote(tok.at[here], tok.at[here], send_x.at[c], recv_x.at[c], (dp, across))

    def to_sibling(c):
        here = piece(me, c)
        return remote(tok.at[here], tok.at[here], send_c.at[c], recv_c.at[c], (dp, sib))

    def forward(c):
        here = piece(across, c)
        return remote(tok.at[here], tok.at[here], send_f.at[c], recv_f.at[c], (dp, sib))

    def arrived(owner, sem, c):
        here = piece(owner, c)
        return pltpu.make_async_copy(tok.at[here], tok.at[here], sem.at[c])

    for c in range(count):
        loads[c].wait()
        tok[piece(me, c)] = stage[pl.ds(c * chunk, chunk)].astype(BF16)
        to_across(c).start()
        to_sibling(c).start()

    query_bias = prm[0:1, 0:128]
    value_bias = prm[0:1, 256:384]

    def project(owner, c):
        here = piece(owner, c)
        block = tok[here]
        tok_t[:, here] = block.T
        query = (dot(block, w[0]) + query_bias).astype(BF16)
        q_s[here] = (query.astype(F32) * HEAD_DIM ** (-0.5)).astype(BF16)
        keys = dot(block, w[1]).astype(BF16)
        k_s[here] = keys
        kt_s[:, here] = keys.T
        values = (dot(block, w[2]) + value_bias).astype(BF16)
        v_s[here] = values
        vt_s[:, here] = values.T

    def outs(g, owner):
        here = ds(owner * rows, rows)
        return [
            pltpu.make_async_copy(tok_t.at[:, here], tok_t_out.at[:, here], out_sem.at[g, 0]),
            pltpu.make_async_copy(q_s.at[here], q_out.at[here], out_sem.at[g, 1]),
            pltpu.make_async_copy(k_s.at[here], k_out.at[here], out_sem.at[g, 2]),
            pltpu.make_async_copy(v_s.at[here], v_out.at[here], out_sem.at[g, 3]),
            pltpu.make_async_copy(kt_s.at[:, here], kt_out.at[:, here], out_sem.at[g, 4]),
            pltpu.make_async_copy(vt_s.at[:, here], vt_out.at[:, here], out_sem.at[g, 5]),
        ]

    def own_step(c, _):
        project(me, c)
        return 0

    lax.fori_loop(0, count, own_step, 0)
    for copy in outs(0, me):
        copy.start()

    def sibling_step(c, _):
        arrived(sib, recv_c, c).wait()
        project(sib, c)
        return 0

    lax.fori_loop(0, count, sibling_step, 0)
    for copy in outs(1, sib):
        copy.start()

    def across_step(c, _):
        arrived(across, recv_x, c).wait()
        forward(c).start()
        project(across, c)
        arrived(diagonal, recv_f, c).wait()
        project(diagonal, c)
        return 0

    lax.fori_loop(0, count, across_step, 0)
    for copy in outs(2, across) + outs(3, diagonal):
        copy.start()
    for c in range(count):
        to_across(c).wait_send()
        to_sibling(c).wait_send()
        forward(c).wait_send()
    for g, owner in enumerate((me, sib, across, diagonal)):
        for copy in outs(g, owner):
            copy.wait()


def gather_and_project(post_stream, qkv3, prm):
    rows, width = post_stream.shape
    group = rows * MP
    local = qkv3.shape[2]
    count = rows // TILE
    tall = jax.ShapeDtypeStruct((group, local), BF16)
    wide = jax.ShapeDtypeStruct((local, group), BF16)
    return pl.pallas_call(
        project_kernel,
        out_shape=(jax.ShapeDtypeStruct((width, group), BF16), tall, tall, tall, wide, wide),
        in_specs=[ANY, VMEM, VMEM],
        out_specs=(ANY,) * 6,
        scratch_shapes=[
            pltpu.VMEM((rows, width), F32),
            pltpu.VMEM((group, width), BF16),
            pltpu.VMEM((width, group), BF16),
            pltpu.VMEM((group, local), BF16),
            pltpu.VMEM((group, local), BF16),
            pltpu.VMEM((group, local), BF16),
            pltpu.VMEM((local, group), BF16),
            pltpu.VMEM((local, group), BF16),
            dma_sems(count), dma_sems(count), dma_sems(count), dma_sems(count),
            dma_sems(count), dma_sems(count), dma_sems(count), dma_sems(4, 6),
        ],
        compiler_params=pltpu.CompilerParams(
            collective_id=0, has_side_effects=True, vmem_limit_bytes=40 << 20
        ),
        cost_estimate=pl.CostEstimate(flops=2 * group * width * 3 * local, bytes_accessed=12 << 20, transcendentals=0),
        name="gather_project",
    )(post_stream, qkv3, prm)


def first_of_segment(lengths, place):
    bound = jnp.int32(0)
    start = jnp.zeros_like(place)
    for s in range(lengths.shape[0] - 1):
        bound = bound + lengths[s]
        start = jnp.where(place >= bound, bound, start)
    return jnp.where(place >= bound, place, start)


def head_masked(block, h):
    lane = lax.broadcasted_iota(jnp.int32, block.shape, 1)
    return jnp.where((lane >= h * HEAD_DIM) & (lane < (h + 1) * HEAD_DIM), block, jnp.zeros_like(block))


def attend_kernel(lengths, q_ref, k_ref, vt_ref, att_ref, lse_ref):
    i = pl.program_id(0)
    base = i * TILE
    heads = q_ref.shape[1] // HEAD_DIM
    place = base + lax.broadcasted_iota(jnp.int32, (1, TILE), 1)
    start = first_of_segment(lengths, place)
    low = first_of_segment(lengths, base) // TILE
    query = q_ref[...]
    queries = [head_masked(query, h) for h in range(heads)]

    def tile(j, carry, diagonal):
        here = ds(j * TILE, TILE)
        keys = k_ref[here]
        values_t = vt_ref[:, here]
        key_place = lax.broadcasted_iota(jnp.int32, (TILE, TILE), 0)
        allowed = key_place >= start - j * TILE
        if diagonal:
            allowed = allowed & (key_place <= place - j * TILE)
        result = []
        for h in range(heads):
            top, total, acc = carry[h]
            score = jnp.where(allowed, dot(keys, queries[h], NT), MASKED)
            new_top = jnp.maximum(top, jnp.max(score, axis=0, keepdims=True))
            alpha = jnp.exp(top - new_top)
            prob = jnp.exp(score - new_top)
            total = total * alpha + jnp.sum(prob, axis=0, keepdims=True)
            acc = acc * alpha + dot(values_t[h * HEAD_DIM : (h + 1) * HEAD_DIM], prob.astype(BF16))
            result.append((new_top, total, acc))
        return tuple(result)

    init = tuple(
        (
            jnp.full((1, TILE), MASKED, F32),
            jnp.zeros((1, TILE), F32),
            jnp.zeros((HEAD_DIM, TILE), F32),
        )
        for _ in range(heads)
    )
    carry = tile(i, init, True)
    carry = lax.fori_loop(low, i, lambda j, c: tile(j, c, False), carry)
    out_t = jnp.concatenate([acc / total for _, total, acc in carry], axis=0)
    att_ref[...] = out_t.T.astype(BF16)
    for h in range(heads):
        top, total, _ = carry[h]
        lse_ref[0, h : h + 1, :] = top + jnp.log(total)


def attend(lengths, q, k, vt):
    group, local = q.shape
    count = group // TILE
    return pl.pallas_call(
        attend_kernel,
        grid_spec=pltpu.PrefetchScalarGridSpec(
            num_scalar_prefetch=1,
            grid=(count,),
            in_specs=[
                pl.BlockSpec((TILE, local), lambda i, n: (i, 0)),
                pl.BlockSpec((group, local), lambda i, n: (0, 0)),
                pl.BlockSpec((local, group), lambda i, n: (0, 0)),
            ],
            out_specs=[
                pl.BlockSpec((TILE, local), lambda i, n: (i, 0)),
                pl.BlockSpec((1, 8, TILE), lambda i, n: (i, 0, 0)),
            ],
        ),
        out_shape=(
            jax.ShapeDtypeStruct((group, local), BF16),
            jax.ShapeDtypeStruct((count, 8, TILE), F32),
        ),
        compiler_params=pltpu.CompilerParams(vmem_limit_bytes=32 << 20),
        cost_estimate=pl.CostEstimate(flops=12 << 30, bytes_accessed=4 << 20, transcendentals=8 << 20),
        name="attend",
    )(lengths, q, k, vt)


def attend_back_kernel(
    lengths, q_ref, do_ref, o_ref, lse_ref, k_ref, v_ref, kt_ref,
    dq_ref, dk_ref, dv_ref, dk_acc, dv_acc,
):
    i = pl.program_id(0)
    base = i * TILE
    heads = q_ref.shape[1] // HEAD_DIM

    @pl.when(i == 0)
    def _():
        dk_acc[...] = jnp.zeros_like(dk_acc)
        dv_acc[...] = jnp.zeros_like(dv_acc)

    place = base + lax.broadcasted_iota(jnp.int32, (1, TILE), 1)
    start = first_of_segment(lengths, place)
    low = first_of_segment(lengths, base) // TILE
    query = q_ref[...]
    grad = do_ref[...]
    inner = (grad.astype(F32) * o_ref[...].astype(F32)).T
    queries = [head_masked(query, h) for h in range(heads)]
    grads = [head_masked(grad, h) for h in range(heads)]
    delta = [
        jnp.sum(inner[h * HEAD_DIM : (h + 1) * HEAD_DIM], axis=0, keepdims=True) for h in range(heads)
    ]
    lse = [lse_ref[0, h : h + 1, :] for h in range(heads)]

    def tile(j, carry, diagonal):
        here = ds(j * TILE, TILE)
        keys = k_ref[here]
        values = v_ref[here]
        keys_t = kt_ref[:, here]
        key_place = lax.broadcasted_iota(jnp.int32, (TILE, TILE), 0)
        allowed = key_place >= start - j * TILE
        if diagonal:
            allowed = allowed & (key_place <= place - j * TILE)
        result = []
        dv = jnp.zeros((TILE, heads * HEAD_DIM), F32)
        dk = jnp.zeros((TILE, heads * HEAD_DIM), F32)
        for h in range(heads):
            score = jnp.where(allowed, dot(keys, queries[h], NT), MASKED)
            prob = jnp.exp(score - lse[h])
            upstream = dot(values, grads[h], NT)
            score_grad = (prob * (upstream - delta[h])).astype(BF16)
            dv = dv + dot(prob.astype(BF16), grads[h])
            dk = dk + dot(score_grad, queries[h])
            result.append(carry[h] + dot(keys_t[h * HEAD_DIM : (h + 1) * HEAD_DIM], score_grad))
        dv_acc[here] += dv
        dk_acc[here] += dk
        return tuple(result)

    carry = tuple(jnp.zeros((HEAD_DIM, TILE), F32) for _ in range(heads))
    carry = tile(i, carry, True)
    carry = lax.fori_loop(low, i, lambda j, c: tile(j, c, False), carry)
    dq_t = jnp.concatenate(carry, axis=0) * HEAD_DIM ** (-0.5)
    dq_ref[...] = dq_t.T.astype(BF16)

    @pl.when(i == pl.num_programs(0) - 1)
    def _():
        dk_ref[...] = dk_acc[...].astype(BF16)
        dv_ref[...] = dv_acc[...].astype(BF16)


def attend_back(lengths, q, k, v, kt, att, lse, att_grad):
    group, local = q.shape
    count = group // TILE
    block = pl.BlockSpec((TILE, local), lambda i, n: (i, 0))
    whole = pl.BlockSpec((group, local), lambda i, n: (0, 0))
    shape = jax.ShapeDtypeStruct((group, local), BF16)
    return pl.pallas_call(
        attend_back_kernel,
        grid_spec=pltpu.PrefetchScalarGridSpec(
            num_scalar_prefetch=1,
            grid=(count,),
            in_specs=[
                block, block, block,
                pl.BlockSpec((1, 8, TILE), lambda i, n: (i, 0, 0)),
                whole, whole,
                pl.BlockSpec((local, group), lambda i, n: (0, 0)),
            ],
            out_specs=[block, whole, whole],
            scratch_shapes=[pltpu.VMEM((group, local), F32), pltpu.VMEM((group, local), F32)],
        ),
        out_shape=(shape, shape, shape),
        compiler_params=pltpu.CompilerParams(vmem_limit_bytes=32 << 20),
        cost_estimate=pl.CostEstimate(flops=30 << 30, bytes_accessed=9 << 20, transcendentals=8 << 20),
        name="attend_back",
    )(lengths, q, att_grad, att, lse, k, v, kt)


def center_and_scale(summed):
    width = summed.shape[1]
    center = summed - jnp.sum(summed, axis=1, keepdims=True) * (1.0 / width)
    inverse = lax.rsqrt(jnp.sum(center * center, axis=1, keepdims=True) * (1.0 / width) + EPSILON)
    return center * inverse, inverse


def norm_backward(cotangent, normed, inverse, gain):
    width = normed.shape[1]
    scaled = cotangent * gain
    mean = jnp.sum(scaled, axis=1, keepdims=True) * (1.0 / width)
    along = jnp.sum(scaled * normed, axis=1, keepdims=True) * (1.0 / width)
    return inverse * (scaled - mean - normed * along)


def gelu_and_slope(value):
    square = value * value
    inner = value * (SQRT_2_OVER_PI + (SQRT_2_OVER_PI * 0.044715) * square)
    half = 0.5 + 0.5 * jnp.tanh(inner)
    rise = value * (2.0 * SQRT_2_OVER_PI + (6.0 * SQRT_2_OVER_PI * 0.044715) * square)
    return value * half, half * (1.0 + (1.0 - half) * rise)


def column_sum(block):
    return jnp.sum(block, axis=0, keepdims=True)


def middle_kernel(
    att, post, pre, post_cot, pre_cot, up_own, down_own, out_own, up_across, down_across, out_across, prm,
    post_out, pre_out, sum1_out, att_grad_out, keep_out, give_out, small_out,
    post_b, pre_b, post_cot_b, pre_cot_b, att_in, w_up, w_down, w_out, prm_all,
    mid_low, hidden, act_grad, ffn_grad, branch_grad, att_grad_b, slope_b,
    post_out_b, pre_out_b, sum1_b, send_b, recv_b, keep_b, give_b,
    in_sem, own_sem, weight_sem, send_w, recv_w, send_p, recv_p,
    send_a, recv_a, send_g, recv_g, send_r, recv_r, out_sem,
):
    me, sib, across, diagonal = mp_peers()
    dp = lax.axis_index("dp")
    rows, width = post.shape
    chunk = TILE
    count = rows // chunk
    local = att.shape[1]
    hid = up_own.shape[1]
    peers = (sib, across, diagonal)

    def stream(c):
        here = pl.ds(c * chunk, chunk)
        return [
            pltpu.make_async_copy(src.at[here], dst.at[here], in_sem.at[c, n])
            for n, (src, dst) in enumerate(
                ((post, post_b), (pre, pre_b), (post_cot, post_cot_b), (pre_cot, pre_cot_b))
            )
        ]

    def own_attended():
        return pltpu.make_async_copy(
            att.at[ds(me * rows, rows)], att_in.at[:, ds(me * local, local)], own_sem.at[0]
        )

    def local_weights():
        copies = []
        for n, (owner, parts) in enumerate(
            ((me, (up_own, down_own, out_own)), (across, (up_across, down_across, out_across)))
        ):
            places = (w_up.at[owner], w_down.at[owner], w_out.at[ds(owner * local, local)])
            copies += [
                pltpu.make_async_copy(src, dst, weight_sem.at[n, k])
                for k, (src, dst) in enumerate(zip(parts, places))
            ]
        return copies

    def sent_weights():
        copies = []
        for n, (owner, parts) in enumerate(
            ((me, (up_own, down_own, out_own)), (across, (up_across, down_across, out_across)))
        ):
            places = (w_up.at[owner], w_down.at[owner], w_out.at[ds(owner * local, local)])
            copies += [
                remote(src, dst, send_w.at[n, k], recv_w.at[n, k], (dp, sib))
                for k, (src, dst) in enumerate(zip(parts, places))
            ]
        return copies

    def arriving_weights():
        copies = []
        for n, owner in enumerate((sib, diagonal)):
            places = (w_up.at[owner], w_down.at[owner], w_out.at[ds(owner * local, local)])
            copies += [pltpu.make_async_copy(p, p, recv_w.at[n, k]) for k, p in enumerate(places)]
        return copies

    def sent_prm(n):
        return remote(prm, prm_all.at[me], send_p.at[n], recv_p.at[n], (dp, peers[n]))

    def sent_attended(n, c):
        peer = peers[n]
        return remote(
            att.at[ds(peer * rows + c * chunk, chunk)],
            att_in.at[ds(c * chunk, chunk), ds(me * local, local)],
            send_a.at[n, c],
            recv_a.at[n, c],
            (dp, peer),
        )

    def arriving_attended(n, c):
        place = att_in.at[ds(c * chunk, chunk), ds(peers[n] * local, local)]
        return pltpu.make_async_copy(place, place, recv_a.at[n, c])

    def sent_grad(n, c):
        peer = peers[n]
        return remote(
            att_grad_b.at[ds(c * chunk, chunk), ds(peer * local, local)],
            att_grad_out.at[ds(me * rows + c * chunk, chunk)],
            send_g.at[n, c],
            recv_g.at[n, c],
            (dp, peer),
        )

    def arriving_grad(n, c):
        place = att_grad_out.at[ds(peers[n] * rows + c * chunk, chunk)]
        return pltpu.make_async_copy(place, place, recv_g.at[n, c])

    def own_grad(c):
        return pltpu.make_async_copy(
            att_grad_b.at[ds(c * chunk, chunk), ds(me * local, local)],
            att_grad_out.at[ds(me * rows + c * chunk, chunk)],
            out_sem.at[c, 3],
        )

    def stored(c):
        here = ds(c * chunk, chunk)
        return [
            pltpu.make_async_copy(src.at[here], dst.at[here], out_sem.at[c, n])
            for n, (src, dst) in enumerate(((post_out_b, post_out), (pre_out_b, pre_out), (sum1_b, sum1_out)))
        ]

    for copy in stream(0) + [own_attended()] + local_weights():
        copy.start()
    greet([(dp, peer) for peer in peers])
    for n in range(3):
        sent_prm(n).start()
    for c in range(count):
        for n in (2, 1, 0):
            sent_attended(n, c).start()
    for copy in sent_weights():
        copy.start()
    for c in range(1, count):
        for copy in stream(c):
            copy.start()
    prm_all[ds(me, 1)] = prm[...][None]
    small_out[...] = jnp.zeros_like(small_out)
    own_attended().wait()
    for n in range(3):
        arrived = prm_all.at[peers[n]]
        pltpu.make_async_copy(arrived, arrived, recv_p.at[n]).wait()
    for copy in local_weights() + arriving_weights():
        copy.wait()

    out_bias, gain1, shift1 = prm[1:2], prm[2:3], prm[3:4]
    down_bias, gain2, shift2 = prm[4:5], prm[5:6], prm[6:7]

    def block_step(c, _):
        here = ds(c * chunk, chunk)
        for n in range(3):
            arriving_attended(n, c).wait()
        for n in range(4):
            pltpu.make_async_copy(post_b.at[here], post_b.at[here], in_sem.at[c, n]).wait()
        branch = dot(att_in[here], w_out[...]) + out_bias
        normed1, inverse1 = center_and_scale(post_b[here] + branch)
        mid = normed1 * gain1 + shift1
        pre_mid = pre_b[here] + branch
        low = mid.astype(BF16)
        mid_low[here] = low
        ffn = jnp.zeros((chunk, width), F32)
        for f in range(MP):
            pre_act = dot(low, w_up[f]) + prm_all[f, 7:8]
            value, slope = gelu_and_slope(pre_act)
            value = value.astype(BF16)
            hidden[f, here] = value
            slope_b[f] = slope
            ffn = ffn + dot(value, w_down[f])
        ffn = ffn + down_bias
        normed2, inverse2 = center_and_scale(mid + ffn)
        post_out_b[here] = normed2 * gain2 + shift2
        pre_out_b[here] = pre_mid + ffn
        cot = post_cot_b[here]
        small_out[4:5] += column_sum(cot * normed2)
        small_out[5:6] += column_sum(cot)
        sum2_grad = norm_backward(cot, normed2, inverse2, gain2)
        grad = (sum2_grad + pre_cot_b[here]).astype(BF16)
        ffn_grad[here] = grad
        small_out[3:4] += column_sum(grad.astype(F32))
        mid_grad = sum2_grad
        for f in range(MP):
            back = (dot(grad, w_down[f], NT) * slope_b[f]).astype(BF16)
            act_grad[f, here] = back
            small_out[8 + f : 9 + f] += column_sum(back.astype(F32))
            mid_grad = mid_grad + dot(back, w_up[f], NT)
        small_out[1:2] += column_sum(mid_grad * normed1)
        small_out[2:3] += column_sum(mid_grad)
        sum1 = norm_backward(mid_grad, normed1, inverse1, gain1)
        sum1_b[here] = sum1
        grad1 = (sum1 + pre_cot_b[here]).astype(BF16)
        branch_grad[here] = grad1
        small_out[0:1] += column_sum(grad1.astype(F32))
        att_grad_b[here] = dot(grad1, w_out[...], NT).astype(BF16)
        for n in (2, 1, 0):
            sent_grad(n, c).start()
        own_grad(c).start()
        for copy in stored(c):
            copy.start()
        return 0

    lax.fori_loop(0, count, block_step, 0)

    def weight_grads(s):
        up = dot(mid_low[...], act_grad[s], TN)
        down = dot(hidden[s], ffn_grad[...], TN)
        out = dot(att_in[:, ds(s * local, local)], branch_grad[...], TN)
        return up, down, out

    def sent_sums(n):
        return remote(send_b.at[n], recv_b.at[n], send_r.at[n], recv_r.at[n], (dp, sib))

    spans = (pl.ds(0, width), pl.ds(width, hid), pl.ds(width + hid, local))
    for n, owner in enumerate((diagonal, sib)):
        for span, part in zip(spans, weight_grads(owner)):
            send_b[n, span] = part.astype(BF16)
        sent_sums(n).start()
    for span, part in zip(spans, weight_grads(across)):
        keep_b[span] = part
    sent_sums(0).wait_recv()
    give_b[...] = (keep_b[...] + recv_b[0].astype(F32)).astype(BF16)
    give = pltpu.make_async_copy(give_b, give_out, own_sem.at[1])
    give.start()
    for span, part in zip(spans, weight_grads(me)):
        keep_b[span] = part
    sent_sums(1).wait_recv()
    keep_b[...] = keep_b[...] + recv_b[1].astype(F32)
    keep = pltpu.make_async_copy(keep_b, keep_out, own_sem.at[2])
    keep.start()
    for c in range(count):
        for copy in stored(c) + [own_grad(c)]:
            copy.wait()
        for n in range(3):
            sent_attended(n, c).wait_send()
            sent_grad(n, c).wait_send()
            arriving_grad(n, c).wait()
    for copy in sent_weights():
        copy.wait_send()
    for n in range(3):
        sent_prm(n).wait_send()
    for n in range(2):
        sent_sums(n).wait_send()
    give.wait()
    keep.wait()


def middle(att, post, pre, post_cot, pre_cot, own, across, prm):
    rows, width = post.shape
    local = att.shape[1]
    up, down, out = own
    hid = up.shape[1]
    count = rows // TILE
    tall = width + hid + local
    f32 = jax.ShapeDtypeStruct((rows, width), F32)
    return pl.pallas_call(
        middle_kernel,
        out_shape=(
            f32, f32, f32,
            jax.ShapeDtypeStruct(att.shape, BF16),
            jax.ShapeDtypeStruct((tall, width), F32),
            jax.ShapeDtypeStruct((tall, width), BF16),
            jax.ShapeDtypeStruct((16, width), F32),
        ),
        in_specs=[ANY] * 11 + [VMEM],
        out_specs=(ANY,) * 6 + (VMEM,),
        scratch_shapes=[
            pltpu.VMEM((rows, width), F32),
            pltpu.VMEM((rows, width), F32),
            pltpu.VMEM((rows, width), F32),
            pltpu.VMEM((rows, width), F32),
            pltpu.VMEM((rows, MP * local), BF16),
            pltpu.VMEM((MP, width, hid), BF16),
            pltpu.VMEM((MP, hid, width), BF16),
            pltpu.VMEM((MP * local, width), BF16),
            pltpu.VMEM((MP,) + prm.shape, F32),
            pltpu.VMEM((rows, width), BF16),
            pltpu.VMEM((MP, rows, hid), BF16),
            pltpu.VMEM((MP, rows, hid), BF16),
            pltpu.VMEM((rows, width), BF16),
            pltpu.VMEM((rows, width), BF16),
            pltpu.VMEM((rows, MP * local), BF16),
            pltpu.VMEM((MP, TILE, hid), F32),
            pltpu.VMEM((rows, width), F32),
            pltpu.VMEM((rows, width), F32),
            pltpu.VMEM((rows, width), F32),
            pltpu.VMEM((2, tall, width), BF16),
            pltpu.VMEM((2, tall, width), BF16),
            pltpu.VMEM((tall, width), F32),
            pltpu.VMEM((tall, width), BF16),
            dma_sems(count, 4), dma_sems(3), dma_sems(2, 3), dma_sems(2, 3), dma_sems(2, 3),
            dma_sems(3), dma_sems(3), dma_sems(3, count), dma_sems(3, count),
            dma_sems(3, count), dma_sems(3, count), dma_sems(2), dma_sems(2), dma_sems(count, 4),
        ],
        compiler_params=pltpu.CompilerParams(
            collective_id=1, has_side_effects=True, vmem_limit_bytes=60 << 20
        ),
        cost_estimate=pl.CostEstimate(flops=15 << 30, bytes_accessed=20 << 20, transcendentals=4 << 20),
        name="middle",
    )(att, post, pre, post_cot, pre_cot, up, down, out, *across, prm)


def tail_kernel(
    dp_size,
    dq, dk, dv, tok_t, w, sum1, keep, given, small,
    post_out, qkv_out, up_out, down_out, out_out, small_out,
    grads, tok_b, sum1_b, given_b, mine, far, send_far, recv_far, pass_far, land_far, send_near, recv_near,
    acc, flight, full, land, small_flight, small_land,
    in_sem, near_send, near_recv, far_send, far_recv, hop_send, hop_recv,
    step_send, step_recv, small_send, small_recv, out_sem,
):
    me, sib, across, diagonal = mp_peers()
    dp = lax.axis_index("dp")
    rows, width = sum1.shape
    local = dq.shape[1]
    chunk = TILE
    count = rows // chunk
    hid = up_out.shape[1]
    bits = dp_size.bit_length() - 1
    partners = [dp + (1 << b) - 2 * (1 << b) * ((dp // (1 << b)) % 2) for b in range(bits)]
    upper = [(dp // (1 << b)) % 2 for b in range(bits)]

    loads = [
        pltpu.make_async_copy(src, grads.at[n], in_sem.at[n]) for n, src in enumerate((dq, dk, dv))
    ] + [
        pltpu.make_async_copy(tok_t, tok_b, in_sem.at[3]),
        pltpu.make_async_copy(sum1, sum1_b, in_sem.at[4]),
        pltpu.make_async_copy(keep, acc.at[pl.ds(0, keep.shape[0])], in_sem.at[5]),
        pltpu.make_async_copy(given, given_b, in_sem.at[6]),
    ]
    for load in loads:
        load.start()
    greet([(dp, sib), (dp, across)] + [(p, me) for p in partners])

    pieces = ((0, width), (width, hid), (width + hid, local), (width + hid + local, 3 * width // 4))

    def plan(piece):
        start, size = piece
        sizes = []
        for b in range(bits):
            halved = size % 32 == 0
            sizes.append((b, size, halved))
            if halved:
                size //= 2
        return sizes

    offsets = {}
    for n, piece in enumerate(pieces):
        base = jnp.int32(piece[0])
        for b, size, halved in plan(piece):
            if halved:
                half = size // 2
                offsets[n, b] = (base + (1 - upper[b]) * half, base + upper[b] * half, half)
                base = base + upper[b] * half
            else:
                offsets[n, b] = (base, base, size)

    def reduce_copy(n, b):
        given_at, kept_at, size = offsets[n, b]
        return remote(
            flight.at[ds16(given_at, size)], land.at[b, ds16(given_at, size)],
            step_send.at[0, n, b], step_recv.at[0, n, b], (partners[b], me),
        )

    def reduce_start(n, b):
        given_at, kept_at, size = offsets[n, b]
        here = ds16(given_at, size)
        flight[here] = acc[here].astype(BF16)
        reduce_copy(n, b).start()

    def reduce_finish(n, b):
        given_at, kept_at, size = offsets[n, b]
        copy = reduce_copy(n, b)
        copy.wait_recv()
        here = ds16(kept_at, size)
        if plan(pieces[n])[b][2]:
            acc[here] = acc[here] + land[b, here].astype(F32)
        else:
            acc[here] = flight[here].astype(F32) + land[b, here].astype(F32)
        copy.wait_send()

    def spread_copy(n, b):
        given_at, kept_at, size = offsets[n, b]
        here = ds16(kept_at, size)
        return remote(full.at[here], full.at[here], step_send.at[1, n, b], step_recv.at[1, n, b], (partners[b], me))

    def spread_done(n, b):
        given_at, kept_at, size = offsets[n, b]
        there = ds16(given_at, size)
        copy = pltpu.make_async_copy(full.at[there], full.at[there], step_recv.at[1, n, b])
        copy.wait()

    def stage(n, t):
        if t <= bits:
            if t > 0:
                reduce_finish(n, t - 1)
            if t < bits:
                reduce_start(n, t)
                return
            _, kept_at, size = offsets[n, bits - 1]
            here = ds16(kept_at, size)
            full[here] = acc[here].astype(BF16)
            t = bits
        order = [b for b in range(bits - 1, -1, -1) if plan(pieces[n])[b][2]]
        k = t - bits
        if k > 0:
            spread_done(n, order[k - 1])
            spread_copy(n, order[k - 1]).wait_send()
        if k < len(order):
            spread_copy(n, order[k]).start()

    def last_stage(n):
        return bits + sum(1 for _, _, halved in plan(pieces[n]) if halved)

    small_peers = [(dp, sib), (dp, across)] + [(p, me) for p in partners]

    def small_copy(s):
        return remote(small_flight.at[s], small_land.at[s], small_send.at[s], small_recv.at[s], small_peers[s])

    def small_stage(s):
        if s > 0:
            small_copy(s - 1).wait()
            small_out[...] = small_out[...] + small_land[s - 1]
        if s < len(small_peers):
            small_flight[s] = small_out[...]
            small_copy(s).start()

    def part(owner, c):
        here = ds(owner * rows + c * chunk, chunk)
        return (
            dot(grads[0, here], w[0], NT) + dot(grads[1, here], w[1], NT) + dot(grads[2, here], w[2], NT)
        )

    def far_copy(c):
        return remote(send_far.at[c], recv_far.at[c], far_send.at[c], far_recv.at[c], (dp, sib))

    def hop_copy(c):
        return remote(pass_far.at[c], land_far.at[c], hop_send.at[c], hop_recv.at[c], (dp, across))

    def near_copy(c):
        return remote(send_near.at[c], recv_near.at[c], near_send.at[c], near_recv.at[c], (dp, sib))

    loads[5].wait()
    loads[6].wait()
    own = pl.ds(0, given_b.shape[0])
    acc[own] = acc[own] + given_b[...].astype(F32)
    stage(0, 0)
    for n in range(3):
        loads[n].wait()

    def far_step(c, _):
        send_far[c] = part(diagonal, c).astype(BF16)
        far_copy(c).start()
        far[c] = part(across, c)
        return 0

    def hop_step(c, _):
        far_copy(c).wait_recv()
        pass_far[c] = (far[c] + recv_far[c].astype(F32)).astype(BF16)
        hop_copy(c).start()
        return 0

    def near_step(c, _):
        send_near[c] = part(sib, c).astype(BF16)
        near_copy(c).start()
        mine[c] = part(me, c)
        return 0

    lax.fori_loop(0, count, far_step, 0)
    stage(1, 0)
    lax.fori_loop(0, count, hop_step, 0)
    stage(2, 0)
    lax.fori_loop(0, count, near_step, 0)
    small_out[...] = small[...]
    query_sum = column_sum(grads[0].astype(F32))
    value_sum = column_sum(grads[2].astype(F32))
    small_out[ds1(12 + me), :] = jnp.concatenate(
        [query_sum, value_sum, jnp.zeros((1, width - 2 * local), F32)], axis=1
    )
    small_stage(0)
    loads[3].wait()
    base = pieces[3][0]
    third = width // 4
    for n in range(3):
        block = dot(tok_b[...], grads[n])
        for s in range(4):
            acc[pl.ds(base + n * third, third), pl.ds(s * local, local)] = block[s * third : (s + 1) * third]
    stage(3, 0)

    last = max(last_stage(n) for n in range(len(pieces)))
    for t in range(1, last + 1):
        for n in range(len(pieces)):
            if t <= last_stage(n):
                stage(n, t)
        if t <= len(small_peers):
            small_stage(t)
        if t == last // 2:
            loads[4].wait()
            for c in range(count):
                near_copy(c).wait()
                mine[c] = mine[c] + recv_near[c].astype(F32)
    for t in range(last + 1, len(small_peers) + 1):
        small_stage(t)

    outs = []
    up_out[...] = full[pl.ds(0, width)].astype(F32)
    down_out[...] = full[pl.ds(width, hid)].astype(F32)
    out_out[...] = full[pl.ds(width + hid, local)].astype(F32)
    for n in range(3):
        for s in range(4):
            qkv_out[n, pl.ds(s * third, third)] = full[
                pl.ds(base + n * third, third), pl.ds(s * local, local)
            ].astype(F32)
    for c in range(count):
        far_copy(c).wait_send()
        hop_copy(c).wait()
        here = pl.ds(c * chunk, chunk)
        sum1_b[here] = sum1_b[here] + mine[c] + land_far[c].astype(F32)
        out = pltpu.make_async_copy(sum1_b.at[here], post_out.at[here], out_sem.at[c])
        out.start()
        outs.append(out)
    for out in outs:
        out.wait()


def ds16(start, size):
    return pl.ds(pl.multiple_of(start, 16), size)


def ds1(start):
    return pl.ds(start, 1)


def tail(dp_size, dq, dk, dv, tok_t, w, sum1, keep, given, small):
    rows, width = sum1.shape
    group, local = dq.shape
    tall = keep.shape[0]
    hid = tall - width - local
    count = rows // TILE
    bits = dp_size.bit_length() - 1
    assert 1 << bits == dp_size
    total = tall + 3 * width // 4
    blocks = (count, TILE, width)
    steps = bits + 2
    return pl.pallas_call(
        functools.partial(tail_kernel, dp_size),
        out_shape=(
            jax.ShapeDtypeStruct((rows, width), F32),
            jax.ShapeDtypeStruct((3, width, local), F32),
            jax.ShapeDtypeStruct((width, hid), F32),
            jax.ShapeDtypeStruct((hid, width), F32),
            jax.ShapeDtypeStruct((local, width), F32),
            jax.ShapeDtypeStruct(small.shape, F32),
        ),
        in_specs=[ANY] * 4 + [VMEM] + [ANY] * 3 + [VMEM],
        out_specs=(ANY,) + (VMEM,) * 5,
        scratch_shapes=[
            pltpu.VMEM((3, group, local), BF16),
            pltpu.VMEM((width, group), BF16),
            pltpu.VMEM((rows, width), F32),
            pltpu.VMEM((tall, width), BF16),
            pltpu.VMEM(blocks, F32),
            pltpu.VMEM(blocks, F32),
            pltpu.VMEM(blocks, BF16),
            pltpu.VMEM(blocks, BF16),
            pltpu.VMEM(blocks, BF16),
            pltpu.VMEM(blocks, BF16),
            pltpu.VMEM(blocks, BF16),
            pltpu.VMEM(blocks, BF16),
            pltpu.VMEM((total, width), F32),
            pltpu.VMEM((total, width), BF16),
            pltpu.VMEM((total, width), BF16),
            pltpu.VMEM((bits, total, width), BF16),
            pltpu.VMEM((steps,) + small.shape, F32),
            pltpu.VMEM((steps,) + small.shape, F32),
            dma_sems(7), dma_sems(count), dma_sems(count), dma_sems(count), dma_sems(count),
            dma_sems(count), dma_sems(count), dma_sems(2, 4, bits), dma_sems(2, 4, bits),
            dma_sems(steps), dma_sems(steps), dma_sems(count),
        ],
        compiler_params=pltpu.CompilerParams(
            collective_id=2, has_side_effects=True, vmem_limit_bytes=60 << 20
        ),
        cost_estimate=pl.CostEstimate(flops=4 << 30, bytes_accessed=20 << 20, transcendentals=0),
        name="tail",
    )(dq, dk, dv, tok_t, w, sum1, keep, given, small)


def body(
    dp_size,
    post_stream,
    pre_stream,
    seq_lengths,
    qkv_weight,
    query_bias,
    value_bias,
    out_weight,
    out_bias,
    norm1_gain,
    norm1_shift,
    up_weight,
    up_bias,
    down_weight,
    down_bias,
    norm2_gain,
    norm2_shift,
    post_cotan,
    pre_cotan,
):
    local = out_weight.shape[0]
    lengths = seq_lengths[0]
    qkv3 = jnp.transpose(qkv_weight, (1, 0, 2))
    pad = jnp.zeros_like(query_bias)
    prm = jnp.stack(
        [
            jnp.concatenate([query_bias, pad, value_bias, pad]),
            out_bias, norm1_gain, norm1_shift, down_bias, norm2_gain, norm2_shift, up_bias,
        ]
    ).astype(F32)
    tok_t, q, k, v, kt, vt = gather_and_project(post_stream, qkv3, prm)
    across = [(m, (m + 2) % MP) for m in range(MP)]
    own = (up_weight, down_weight, out_weight)
    own, _ = lax.optimization_barrier((own, tok_t))
    far = [lax.ppermute(part, "mp", across) for part in own]
    att, lse = attend(lengths, q, k, vt)
    post_out, pre_out, sum1, att_grad, keep, give, small = middle(
        att, post_stream, pre_stream, post_cotan, pre_cotan, own, far, prm
    )
    given = lax.ppermute(give, "mp", across)
    dq, dk, dv = attend_back(lengths, q, k, v, kt, att, lse, att_grad)
    post_grad, qkv_grad, up_grad, down_grad, out_grad, small = tail(
        dp_size, dq, dk, dv, tok_t, qkv3, sum1, keep, given, small
    )
    me = lax.axis_index("mp")
    own_row = lax.dynamic_slice_in_dim(small, 12 + me, 1, 0)[0]
    return (
        post_out,
        pre_out,
        post_grad,
        jnp.transpose(qkv_grad, (1, 0, 2)),
        own_row[:local],
        own_row[local : 2 * local],
        out_grad,
        small[0],
        small[1],
        small[2],
        up_grad,
        lax.dynamic_slice_in_dim(small, 8 + me, 1, 0)[0],
        down_grad,
        small[3],
        small[4],
        small[5],
    )


def solution(mesh):
    tokens = P(("dp", "mp"), None)
    vector = P()
    return jax.shard_map(
        functools.partial(body, mesh.shape["dp"]),
        mesh=mesh,
        in_specs=(
            tokens, tokens, P("dp", None), P(None, None, "mp"), P("mp"), P("mp"), P("mp", None),
            vector, vector, vector, P(None, "mp"), P("mp"), P("mp", None), vector, vector, vector,
            tokens, tokens,
        ),
        out_specs=(
            tokens, tokens, tokens, P(None, None, "mp"), P("mp"), P("mp"), P("mp", None),
            vector, vector, vector, P(None, "mp"), P("mp"), P("mp", None), vector, vector, vector,
        ),
        check_vma=False,
    )
```

```python
import functools

import jax
import jax.numpy as jnp
from jax import lax
from jax.experimental import pallas as pl
from jax.experimental.pallas import tpu as pltpu
from jax.sharding import PartitionSpec as P

HEAD_DIM = 64
EPSILON = 1e-05
MASKED = -1e30
MP = 4
TILE = 256
MESH = pl.DeviceIdType.MESH
BF16 = jnp.bfloat16
F32 = jnp.float32
ANY = pl.BlockSpec(memory_space=pl.ANY)
VMEM = pl.BlockSpec(memory_space=pltpu.VMEM)
SMEM = pl.BlockSpec(memory_space=pltpu.SMEM)
NT = (((1,), (1,)), ((), ()))
TN = (((0,), (0,)), ((), ()))
SQRT_2_OVER_PI = 0.7978845608028654


def ds(start, size):
    return pl.ds(pl.multiple_of(start, size), size)


def mp_peers():
    me = lax.axis_index("mp")
    sib = me + 1 - 2 * (me % 2)
    across = (me + 2) % MP
    diagonal = (sib + 2) % MP
    return me, sib, across, diagonal


def greet(devices):
    barrier = pltpu.get_barrier_semaphore()
    for device in devices:
        pl.semaphore_signal(barrier, inc=1, device_id=device, device_id_type=MESH)
    pl.semaphore_wait(barrier, len(devices))


def remote(src, dst, send_sem, recv_sem, device):
    return pltpu.make_async_remote_copy(
        src_ref=src,
        dst_ref=dst,
        send_sem=send_sem,
        recv_sem=recv_sem,
        device_id=device,
        device_id_type=MESH,
    )


def dot(a, b, dims=(((1,), (0,)), ((), ()))):
    return lax.dot_general(a, b, dims, preferred_element_type=F32)


def column_sum(block):
    return jnp.sum(block, axis=0, keepdims=True)


def as_row(vector):
    return vector[...].astype(F32).reshape(1, vector.shape[0])


def dma_sems(*shape):
    return pltpu.SemaphoreType.DMA(shape)


def first_of_segment(bounds, place):
    start = jnp.zeros_like(place)
    for bound in bounds:
        start = jnp.where(place >= bound, bound, start)
    return jnp.where(place >= bounds[-1], place, start)


def head_masked(block, h):
    lane = lax.broadcasted_iota(jnp.int32, block.shape, 1)
    return jnp.where((lane >= h * HEAD_DIM) & (lane < (h + 1) * HEAD_DIM), block, jnp.zeros_like(block))


def project_kernel(
    lengths, post, w_any, query_bias_ref, value_bias_ref, up, down, out,
    tok_t_out, q_out, k_out, v_out, kt_out, vt_out, starts, limits, own_out,
    stage, w, own_b, tok, tok_t, q_s, k_s, v_s, kt_s, vt_s,
    w_sem, in_sem, send_x, recv_x, send_c, recv_c, send_f, recv_f, out_sem,
):
    me, sib, across, diagonal = mp_peers()
    dp = lax.axis_index("dp")
    rows = post.shape[0]
    width = post.shape[1]
    chunk = TILE
    count = rows // chunk
    heads = w.shape[2] // HEAD_DIM
    hid = up.shape[1]
    packs = []
    for n, (src, start) in enumerate(((up, 0), (down, width), (out, width + hid))):
        packs.append(pltpu.make_async_copy(src, own_b.at[pl.ds(start, src.shape[0])], w_sem.at[1 + n]))
    packed = pltpu.make_async_copy(own_b, own_out, w_sem.at[4])
    w_load = pltpu.make_async_copy(w_any, w, w_sem.at[0])
    loads = [
        pltpu.make_async_copy(post.at[pl.ds(c * chunk, chunk)], stage.at[pl.ds(c * chunk, chunk)], in_sem.at[c])
        for c in range(count)
    ]
    for load in loads + [w_load] + packs:
        load.start()
    greet([(dp, sib), (dp, across)])

    def piece(owner, c):
        return ds(owner * rows + c * chunk, chunk)

    def to_across(c):
        here = piece(me, c)
        return remote(tok.at[here], tok.at[here], send_x.at[c], recv_x.at[c], (dp, across))

    def to_sibling(c):
        here = piece(me, c)
        return remote(tok.at[here], tok.at[here], send_c.at[c], recv_c.at[c], (dp, sib))

    def forward(c):
        here = piece(across, c)
        return remote(tok.at[here], tok.at[here], send_f.at[c], recv_f.at[c], (dp, sib))

    def arrived(owner, sem, c):
        here = piece(owner, c)
        return pltpu.make_async_copy(tok.at[here], tok.at[here], sem.at[c])

    for c in range(count):
        loads[c].wait()
        tok[piece(me, c)] = stage[pl.ds(c * chunk, chunk)].astype(BF16)
        to_across(c).start()
        to_sibling(c).start()

    query_bias = as_row(query_bias_ref)
    value_bias = as_row(value_bias_ref)

    def project(owner, c):
        here = piece(owner, c)
        block = tok[here]
        tok_t[:, here] = block.T
        query = (dot(block, w[0]) + query_bias).astype(BF16)
        query = (query.astype(F32) * HEAD_DIM ** (-0.5)).astype(BF16)
        for h in range(heads):
            q_s[owner * count + c, pl.ds(h * TILE, TILE)] = head_masked(query, h)
        keys = dot(block, w[1]).astype(BF16)
        k_s[here] = keys
        kt_s[:, here] = keys.T
        values = (dot(block, w[2]) + value_bias).astype(BF16)
        v_s[here] = values
        vt_s[:, here] = values.T

    def outs(g, owner):
        here = ds(owner * rows, rows)
        return [
            pltpu.make_async_copy(tok_t.at[:, here], tok_t_out.at[:, here], out_sem.at[g, 0]),
            pltpu.make_async_copy(
                q_s.at[pl.ds(owner * count, count)], q_out.at[pl.ds(owner * count, count)], out_sem.at[g, 1]
            ),
            pltpu.make_async_copy(k_s.at[here], k_out.at[here], out_sem.at[g, 2]),
            pltpu.make_async_copy(v_s.at[here], v_out.at[here], out_sem.at[g, 3]),
            pltpu.make_async_copy(kt_s.at[:, here], kt_out.at[:, here], out_sem.at[g, 4]),
            pltpu.make_async_copy(vt_s.at[:, here], vt_out.at[:, here], out_sem.at[g, 5]),
        ]

    w_load.wait()
    bounds = [lengths[0, 0]]
    for s in range(1, lengths.shape[1] - 1):
        bounds.append(bounds[-1] + lengths[0, s])
    for i in range(starts.shape[0]):
        place = i * TILE + lax.broadcasted_iota(jnp.int32, (1, starts.shape[2]), 1) % TILE
        starts[i] = jnp.broadcast_to(first_of_segment(bounds, place), starts.shape[1:])
        limits[0, i] = first_of_segment(bounds, jnp.int32(i * TILE)) // TILE
        last = first_of_segment(bounds, jnp.int32(i * TILE + TILE - 1))
        limits[1, i] = jnp.minimum((last + TILE - 1) // TILE, i)

    def own_step(c, _):
        project(me, c)
        return 0

    lax.fori_loop(0, count, own_step, 0)
    for copy in outs(0, me):
        copy.start()
    for pack in packs:
        pack.wait()
    packed.start()

    def sibling_step(c, _):
        arrived(sib, recv_c, c).wait()
        project(sib, c)
        return 0

    lax.fori_loop(0, count, sibling_step, 0)
    for copy in outs(1, sib):
        copy.start()

    def across_step(c, _):
        arrived(across, recv_x, c).wait()
        forward(c).start()
        project(across, c)
        arrived(diagonal, recv_f, c).wait()
        project(diagonal, c)
        return 0

    lax.fori_loop(0, count, across_step, 0)
    for copy in outs(2, across) + outs(3, diagonal):
        copy.start()
    for c in range(count):
        to_across(c).wait_send()
        to_sibling(c).wait_send()
        forward(c).wait_send()
    for g, owner in enumerate((me, sib, across, diagonal)):
        for copy in outs(g, owner):
            copy.wait()
    packed.wait()


def gather_and_project(lengths, post_stream, qkv3, query_bias, value_bias, own):
    rows, width = post_stream.shape
    group = rows * MP
    local = qkv3.shape[2]
    count = rows // TILE
    tall = jax.ShapeDtypeStruct((group, local), BF16)
    wide = jax.ShapeDtypeStruct((local, group), BF16)
    blocks = group // TILE
    across = TILE * (local // HEAD_DIM)
    return pl.pallas_call(
        project_kernel,
        out_shape=(
            jax.ShapeDtypeStruct((width, group), BF16),
            jax.ShapeDtypeStruct((blocks, across, local), BF16),
            tall, tall, wide, wide,
            jax.ShapeDtypeStruct((blocks, 8, across), jnp.int32),
            jax.ShapeDtypeStruct((2, blocks), jnp.int32),
            jax.ShapeDtypeStruct((sum(part.shape[0] for part in own), width), BF16),
        ),
        in_specs=[SMEM, ANY, ANY, VMEM, VMEM, ANY, ANY, ANY],
        out_specs=(ANY,) * 6 + (VMEM, SMEM, ANY),
        scratch_shapes=[
            pltpu.VMEM((rows, width), F32),
            pltpu.VMEM(qkv3.shape, BF16),
            pltpu.VMEM((sum(part.shape[0] for part in own), width), BF16),
            pltpu.VMEM((group, width), BF16),
            pltpu.VMEM((width, group), BF16),
            pltpu.VMEM((blocks, across, local), BF16),
            pltpu.VMEM((group, local), BF16),
            pltpu.VMEM((group, local), BF16),
            pltpu.VMEM((local, group), BF16),
            pltpu.VMEM((local, group), BF16),
            dma_sems(5), dma_sems(count), dma_sems(count), dma_sems(count), dma_sems(count),
            dma_sems(count), dma_sems(count), dma_sems(count), dma_sems(4, 6),
        ],
        compiler_params=pltpu.CompilerParams(
            collective_id=0, has_side_effects=True, vmem_limit_bytes=60 << 20
        ),
        cost_estimate=pl.CostEstimate(flops=2 * group * width * 3 * local, bytes_accessed=12 << 20, transcendentals=0),
        name="gather_project",
    )(lengths, post_stream, qkv3, query_bias, value_bias, *own)


UNROLL = 8


def list_tiles(limits, tiles, counts, blocks):
    spare = jnp.int32(blocks * 65536)
    tiles[0] = spare
    tiles[1] = spare

    def put(code, first, last, at):
        def step(j, at):
            tiles[at] = code + j
            return at + 1

        return lax.fori_loop(first, last, step, at)

    def diagonal(i, at):
        tiles[at] = i * 65536 + i * 257
        return at + 1

    def edge_row(i, at):
        return put(i * 65536 + i * 256, limits[0, i], limits[1, i], at)

    def whole_row(i, at):
        return put(i * 65536 + i * 256, jnp.maximum(limits[0, i], limits[1, i]), i, at)

    at = jnp.int32(2)
    for kind, row in enumerate((diagonal, edge_row, whole_row)):
        at = lax.fori_loop(0, blocks, row, at)
        counts[kind] = (at - 2 + (1 if kind < 2 else 2) + UNROLL - 1) // UNROLL
    for u in range(2 * UNROLL + 2):
        tiles[at + u] = spare


def for_tiles(tiles, counts, heads, products, probabilities, sums):
    for kind in range(3):

        def step(n, _):
            codes = [tiles[n * UNROLL + u] for u in range(UNROLL + 2)]
            entries = [(code // 65536, (code // 256) % 256, code % 256) for code in codes]
            for u in range(UNROLL):
                for h in range(heads):
                    if products is not None:
                        products(u % 2, h, *entries[u + 2])
                    sums(u % 2, h, *entries[u])
                    probabilities((u + 1) % 2, h, kind, *entries[u + 1])
            return 0

        lax.fori_loop(counts[kind - 1] if kind else 0, counts[kind], step, 0)


def masked_score(score, kind, starts, i, j, lanes):
    if kind == 2:
        return score
    keys, queries = score.shape
    score = score.reshape(keys // 8, 8, queries)
    row = 8 * lax.broadcasted_iota(jnp.int32, score.shape, 0)
    key = lax.broadcasted_iota(jnp.int32, (8, queries), 0) + j * TILE
    allowed = (key - starts[i, :, lanes])[None] >= -row
    if kind == 0:
        query = lax.broadcasted_iota(jnp.int32, (8, queries), 1) + i * TILE
        allowed = allowed & ((key - query)[None] <= -row)
    return jnp.where(allowed, score, MASKED).reshape(keys, queries)


def tile_limit(blocks):
    return blocks * (blocks + 1) // 2 + 4 * UNROLL


def attend_kernel(
    limits, starts_ref, q_ref, k_ref, vt_ref, att_ref, lse_ref, tiles, counts,
    queries, k, vt, top, total, acc, scores, probs, alphas, att_b, sem, out_sem,
):
    blocks, wide, local = queries.shape
    heads = local // HEAD_DIM
    one = pl.ds(0, 1)
    loads = [
        pltpu.make_async_copy(src, dst, sem.at[n])
        for n, (src, dst) in enumerate(((q_ref, queries), (k_ref, k), (vt_ref, vt)))
    ]
    for load in loads:
        load.start()
    list_tiles(limits, tiles, counts, blocks)
    top[...] = jnp.full_like(top, MASKED)
    total[...] = jnp.zeros_like(total)
    acc[...] = jnp.zeros_like(acc)
    for load in loads:
        load.wait()

    def products(b, h, slot, i, j):
        lanes = pl.ds(h * TILE, TILE)
        scores[b, :, lanes] = dot(k[ds(j * TILE, TILE)], queries[i, lanes], NT)

    def probabilities(b, h, kind, slot, i, j):
        lanes = pl.ds(h * TILE, TILE)
        score = scores[b, :, lanes]
        score = masked_score(score, kind, starts_ref, i, j, lanes)
        old = top[slot, one, lanes]
        new = jnp.maximum(old, jnp.max(score, axis=0, keepdims=True))
        top[slot, one, lanes] = new
        alpha = jnp.exp(old - new)
        prob = jnp.exp(score - new)
        total[slot, one, lanes] = total[slot, one, lanes] * alpha + jnp.sum(prob, axis=0, keepdims=True)
        probs[b, :, lanes] = prob.astype(BF16)
        alphas[b, one, lanes] = alpha

    def sums(b, h, slot, i, j):
        lanes = pl.ds(h * TILE, TILE)
        values_t = vt[pl.ds(h * HEAD_DIM, HEAD_DIM), ds(j * TILE, TILE)]
        acc[slot, :, lanes] = acc[slot, :, lanes] * alphas[b, one, lanes] + dot(values_t, probs[b, :, lanes])

    for_tiles(tiles, counts, heads, products, probabilities, sums)

    def finish(i, _):
        lse_ref[i, one] = top[i, one] + jnp.log(total[i, one])
        out_t = acc[i] / total[i, one]
        here = ds(i * TILE, TILE)
        parts = [out_t[:, h * TILE : (h + 1) * TILE] for h in range(heads)]
        att_b[here] = jnp.concatenate(parts, axis=0).T.astype(BF16)
        pltpu.make_async_copy(att_b.at[here], att_ref.at[here], out_sem.at[i]).start()
        return 0

    lax.fori_loop(0, blocks, finish, 0, unroll=4)
    for i in range(blocks):
        here = pl.ds(i * TILE, TILE)
        pltpu.make_async_copy(att_b.at[here], att_ref.at[here], out_sem.at[i]).wait()


def attend(limits, starts, queries, k, vt):
    group, local = k.shape
    blocks, wide, _ = queries.shape
    return pl.pallas_call(
        attend_kernel,
        in_specs=[SMEM, VMEM, ANY, ANY, ANY],
        out_specs=[ANY, VMEM, SMEM, SMEM],
        out_shape=(
            jax.ShapeDtypeStruct((group, local), BF16),
            jax.ShapeDtypeStruct((blocks, 8, wide), F32),
            jax.ShapeDtypeStruct((tile_limit(blocks),), jnp.int32),
            jax.ShapeDtypeStruct((3,), jnp.int32),
        ),
        scratch_shapes=[
            pltpu.VMEM((blocks, wide, local), BF16),
            pltpu.VMEM((group, local), BF16),
            pltpu.VMEM((local, group), BF16),
            pltpu.VMEM((blocks + 1, 8, wide), F32),
            pltpu.VMEM((blocks + 1, 8, wide), F32),
            pltpu.VMEM((blocks + 1, HEAD_DIM, wide), F32),
            pltpu.VMEM((2, TILE, wide), F32),
            pltpu.VMEM((2, TILE, wide), BF16),
            pltpu.VMEM((2, 8, wide), F32),
            pltpu.VMEM((group, local), BF16),
            dma_sems(3), dma_sems(blocks),
        ],
        compiler_params=pltpu.CompilerParams(vmem_limit_bytes=60 << 20),
        cost_estimate=pl.CostEstimate(flops=12 << 30, bytes_accessed=4 << 20, transcendentals=8 << 20),
        name="attend",
    )(limits, starts, queries, k, vt)


def attend_back_kernel(
    tiles, counts, starts_ref, lse, q_ref, do_ref, o_ref, k_ref, v_ref, kt_ref, post_mid, pre_mid,
    dq_ref, dk_ref, dv_ref, post_out, pre_out,
    queries, do, o, k, v, kt, grads, delta, dq_acc, dk_acc, dv_acc,
    probs, score_grads, passed_b, out_b, sem, out_sem,
):
    blocks, wide, local = queries.shape
    heads = local // HEAD_DIM
    one = pl.ds(0, 1)
    loads = [
        pltpu.make_async_copy(src, dst, sem.at[n])
        for n, (src, dst) in enumerate(((do_ref, do), (o_ref, o), (q_ref, queries), (k_ref, k), (v_ref, v), (kt_ref, kt)))
    ]
    passed_in = [
        pltpu.make_async_copy(src, passed_b.at[n], sem.at[6 + n]) for n, src in enumerate((post_mid, pre_mid))
    ]
    passed_out = [
        pltpu.make_async_copy(passed_b.at[n], dst, sem.at[8 + n]) for n, dst in enumerate((post_out, pre_out))
    ]
    for load in loads + passed_in:
        load.start()
    dq_acc[...] = jnp.zeros_like(dq_acc)
    dk_acc[...] = jnp.zeros_like(dk_acc)
    dv_acc[...] = jnp.zeros_like(dv_acc)
    for load in loads[:2]:
        load.wait()

    def prepare(i, _):
        here = ds(i * TILE, TILE)
        block = do[here]
        for h in range(heads):
            grads[i, pl.ds(h * TILE, TILE)] = head_masked(block, h)
        along = (block.astype(F32) * o[here].astype(F32)).T
        parts = [column_sum(along[h * HEAD_DIM : (h + 1) * HEAD_DIM]) for h in range(heads)]
        delta[i, one] = jnp.concatenate(parts, axis=1)
        return 0

    lax.fori_loop(0, blocks, prepare, 0, unroll=4)
    for load in loads[2:]:
        load.wait()
    for copy_in, copy_out in zip(passed_in, passed_out):
        copy_in.wait()
        copy_out.start()

    def probabilities(b, h, kind, slot, i, j):
        lanes = pl.ds(h * TILE, TILE)
        here = ds(j * TILE, TILE)
        score = dot(k[here], queries[i, lanes], NT)
        score = masked_score(score, kind, starts_ref, i, j, lanes)
        rise = dot(v[here], grads[i, lanes], NT)
        prob = jnp.exp(score - lse[i, one, lanes])
        probs[b, :, lanes] = prob.astype(BF16)
        score_grads[b, :, lanes] = (prob * (rise - delta[i, one, lanes])).astype(BF16)

    def sums(b, h, slot, i, j):
        lanes = pl.ds(h * TILE, TILE)
        spot = ds(jnp.where(slot == blocks, blocks, j) * TILE, TILE)
        if h == 0:
            dv_acc[spot] += dot(probs[b], grads[i])
        else:
            dk_acc[spot] += dot(score_grads[b], queries[i])
        keys_t = kt[pl.ds(h * HEAD_DIM, HEAD_DIM), ds(j * TILE, TILE)]
        dq_acc[slot, :, lanes] += dot(keys_t, score_grads[b, :, lanes])

    for_tiles(tiles, counts, heads, None, probabilities, sums)

    outs = (dq_ref, dk_ref, dv_ref)

    def out_copy(n, i):
        here = ds(i * TILE, TILE)
        return pltpu.make_async_copy(out_b.at[n, here], outs[n].at[here], out_sem.at[n, i])

    def finish(i, _):
        here = ds(i * TILE, TILE)
        dq_t = dq_acc[i] * HEAD_DIM ** (-0.5)
        parts = [dq_t[:, h * TILE : (h + 1) * TILE] for h in range(heads)]
        out_b[0, here] = jnp.concatenate(parts, axis=0).T.astype(BF16)
        out_b[1, here] = dk_acc[here].astype(BF16)
        out_b[2, here] = dv_acc[here].astype(BF16)
        for n in range(3):
            out_copy(n, i).start()
        return 0

    lax.fori_loop(0, blocks, finish, 0, unroll=4)
    for i in range(blocks):
        for n in range(3):
            out_copy(n, i).wait()
    for copy in passed_out:
        copy.wait()


def attend_back(tiles, counts, starts, lse, queries, k, v, kt, att, att_grad, post_mid, pre_mid):
    group, local = k.shape
    blocks, wide, _ = queries.shape
    shape = jax.ShapeDtypeStruct((group, local), BF16)
    tall = pltpu.VMEM((group, local), BF16)
    return pl.pallas_call(
        attend_back_kernel,
        in_specs=[SMEM, SMEM, VMEM, VMEM] + [ANY] * 8,
        out_specs=[ANY] * 5,
        out_shape=(shape, shape, shape, jax.ShapeDtypeStruct(post_mid.shape, F32), jax.ShapeDtypeStruct(pre_mid.shape, F32)),
        scratch_shapes=[
            pltpu.VMEM((blocks, wide, local), BF16),
            tall, tall, tall, tall,
            pltpu.VMEM((local, group), BF16),
            pltpu.VMEM((blocks, wide, local), BF16),
            pltpu.VMEM((blocks, 8, wide), F32),
            pltpu.VMEM((blocks + 1, HEAD_DIM, wide), F32),
            pltpu.VMEM((group + TILE, local), F32),
            pltpu.VMEM((group + TILE, local), F32),
            pltpu.VMEM((2, TILE, wide), BF16),
            pltpu.VMEM((2, TILE, wide), BF16),
            pltpu.VMEM((2,) + post_mid.shape, F32),
            pltpu.VMEM((3, group, local), BF16),
            dma_sems(10), dma_sems(3, blocks),
        ],
        compiler_params=pltpu.CompilerParams(vmem_limit_bytes=60 << 20),
        cost_estimate=pl.CostEstimate(flops=30 << 30, bytes_accessed=9 << 20, transcendentals=8 << 20),
        name="attend_back",
    )(tiles, counts, starts, lse, queries, att_grad, att, k, v, kt, post_mid, pre_mid)


def center_and_scale(summed):
    width = summed.shape[1]
    center = summed - jnp.sum(summed, axis=1, keepdims=True) * (1.0 / width)
    inverse = lax.rsqrt(jnp.sum(center * center, axis=1, keepdims=True) * (1.0 / width) + EPSILON)
    return center * inverse, inverse


def norm_backward(cotangent, normed, inverse, gain):
    width = normed.shape[1]
    scaled = cotangent * gain
    mean = jnp.sum(scaled, axis=1, keepdims=True) * (1.0 / width)
    along = jnp.sum(scaled * normed, axis=1, keepdims=True) * (1.0 / width)
    return inverse * (scaled - mean - normed * along)


def gelu_and_slope(value):
    square = value * value
    inner = value * (SQRT_2_OVER_PI + (SQRT_2_OVER_PI * 0.044715) * square)
    half = 0.5 + 0.5 * jnp.tanh(inner)
    rise = value * (2.0 * SQRT_2_OVER_PI + (6.0 * SQRT_2_OVER_PI * 0.044715) * square)
    return value * half, half * (1.0 + (1.0 - half) * rise)


def middle_kernel(
    att, post, pre, post_cot, pre_cot, own, far, out_bias_ref, gain1_ref, shift1_ref, down_bias_ref, gain2_ref, shift2_ref, up_bias_ref,
    post_out, pre_out, sum1_out, att_grad_out, keep_out, give_out, small_out,
    post_b, pre_b, post_cot_b, pre_cot_b, att_in, w_up, w_down, w_out, up_bias, up_bias_all,
    mid_low, hidden, act_grad, ffn_grad, branch_grad, att_grad_b, slope_b,
    post_out_b, pre_out_b, sum1_b, send_b, recv_b, keep_b, give_b,
    in_sem, own_sem, weight_sem, send_w, recv_w, send_p, recv_p,
    send_a, recv_a, send_g, recv_g, send_r, recv_r, out_sem,
):
    me, sib, across, diagonal = mp_peers()
    dp = lax.axis_index("dp")
    rows, width = post.shape
    chunk = TILE
    count = rows // chunk
    local = att.shape[1]
    hid = w_up.shape[2]
    spans = (pl.ds(0, width), pl.ds(width, hid), pl.ds(width + hid, local))
    peers = (sib, across, diagonal)

    def stream(c):
        here = pl.ds(c * chunk, chunk)
        return [
            pltpu.make_async_copy(src.at[here], dst.at[here], in_sem.at[c, n])
            for n, (src, dst) in enumerate(
                ((post, post_b), (pre, pre_b), (post_cot, post_cot_b), (pre_cot, pre_cot_b))
            )
        ]

    def own_attended():
        return pltpu.make_async_copy(
            att.at[ds(me * rows, rows)], att_in.at[:, ds(me * local, local)], own_sem.at[0]
        )

    def local_weights():
        copies = []
        for n, (owner, packed) in enumerate(((me, own), (across, far))):
            places = (w_up.at[owner], w_down.at[owner], w_out.at[ds(owner * local, local)])
            copies += [
                pltpu.make_async_copy(packed.at[span], dst, weight_sem.at[n, k])
                for k, (span, dst) in enumerate(zip(spans, places))
            ]
        return copies

    def sent_weights():
        copies = []
        for n, (owner, packed) in enumerate(((me, own), (across, far))):
            places = (w_up.at[owner], w_down.at[owner], w_out.at[ds(owner * local, local)])
            copies += [
                remote(packed.at[span], dst, send_w.at[n, k], recv_w.at[n, k], (dp, sib))
                for k, (span, dst) in enumerate(zip(spans, places))
            ]
        return copies

    def arriving_weights():
        copies = []
        for n, owner in enumerate((sib, diagonal)):
            places = (w_up.at[owner], w_down.at[owner], w_out.at[ds(owner * local, local)])
            copies += [pltpu.make_async_copy(p, p, recv_w.at[n, k]) for k, p in enumerate(places)]
        return copies

    def sent_prm(n):
        return remote(up_bias, up_bias_all.at[me], send_p.at[n], recv_p.at[n], (dp, peers[n]))

    def sent_attended(n, c):
        peer = peers[n]
        return remote(
            att.at[ds(peer * rows + c * chunk, chunk)],
            att_in.at[ds(c * chunk, chunk), ds(me * local, local)],
            send_a.at[n, c],
            recv_a.at[n, c],
            (dp, peer),
        )

    def arriving_attended(n, c):
        place = att_in.at[ds(c * chunk, chunk), ds(peers[n] * local, local)]
        return pltpu.make_async_copy(place, place, recv_a.at[n, c])

    def sent_grad(n, c):
        peer = peers[n]
        return remote(
            att_grad_b.at[ds(c * chunk, chunk), ds(peer * local, local)],
            att_grad_out.at[ds(me * rows + c * chunk, chunk)],
            send_g.at[n, c],
            recv_g.at[n, c],
            (dp, peer),
        )

    def arriving_grad(n, c):
        place = att_grad_out.at[ds(peers[n] * rows + c * chunk, chunk)]
        return pltpu.make_async_copy(place, place, recv_g.at[n, c])

    def own_grad(c):
        return pltpu.make_async_copy(
            att_grad_b.at[ds(c * chunk, chunk), ds(me * local, local)],
            att_grad_out.at[ds(me * rows + c * chunk, chunk)],
            out_sem.at[c, 3],
        )

    def stored(c):
        here = ds(c * chunk, chunk)
        return [
            pltpu.make_async_copy(src.at[here], dst.at[here], out_sem.at[c, n])
            for n, (src, dst) in enumerate(((post_out_b, post_out), (pre_out_b, pre_out), (sum1_b, sum1_out)))
        ]

    for copy in stream(0) + [own_attended()] + local_weights():
        copy.start()
    up_bias[...] = jnp.broadcast_to(as_row(up_bias_ref), up_bias.shape)
    greet([(dp, peer) for peer in peers])
    for n in range(3):
        sent_prm(n).start()
    for c in range(count):
        for n in (2, 1, 0):
            sent_attended(n, c).start()
    for copy in sent_weights():
        copy.start()
    for c in range(1, count):
        for copy in stream(c):
            copy.start()
    up_bias_all[ds(me, 1)] = up_bias[...][None]
    small_out[...] = jnp.zeros_like(small_out)
    own_attended().wait()
    for n in range(3):
        arrived = up_bias_all.at[peers[n]]
        pltpu.make_async_copy(arrived, arrived, recv_p.at[n]).wait()
    for copy in local_weights() + arriving_weights():
        copy.wait()

    out_bias, gain1, shift1 = as_row(out_bias_ref), as_row(gain1_ref), as_row(shift1_ref)
    down_bias, gain2, shift2 = as_row(down_bias_ref), as_row(gain2_ref), as_row(shift2_ref)

    def block_step(c, _):
        here = ds(c * chunk, chunk)
        for n in range(3):
            arriving_attended(n, c).wait()
        for n in range(4):
            pltpu.make_async_copy(post_b.at[here], post_b.at[here], in_sem.at[c, n]).wait()
        branch = dot(att_in[here], w_out[...]) + out_bias
        normed1, inverse1 = center_and_scale(post_b[here] + branch)
        mid = normed1 * gain1 + shift1
        pre_mid = pre_b[here] + branch
        low = mid.astype(BF16)
        mid_low[here] = low
        ffn = jnp.zeros((chunk, width), F32)
        for f in range(MP):
            pre_act = dot(low, w_up[f]) + up_bias_all[f, 0:1]
            value, slope = gelu_and_slope(pre_act)
            value = value.astype(BF16)
            hidden[f, here] = value
            slope_b[f] = slope
            ffn = ffn + dot(value, w_down[f])
        ffn = ffn + down_bias
        normed2, inverse2 = center_and_scale(mid + ffn)
        post_out_b[here] = normed2 * gain2 + shift2
        pre_out_b[here] = pre_mid + ffn
        cot = post_cot_b[here]
        small_out[4:5] += column_sum(cot * normed2)
        small_out[5:6] += column_sum(cot)
        sum2_grad = norm_backward(cot, normed2, inverse2, gain2)
        grad = (sum2_grad + pre_cot_b[here]).astype(BF16)
        ffn_grad[here] = grad
        small_out[3:4] += column_sum(grad.astype(F32))
        mid_grad = sum2_grad
        for f in range(MP):
            back = (dot(grad, w_down[f], NT) * slope_b[f]).astype(BF16)
            act_grad[f, here] = back
            small_out[8 + f : 9 + f] += column_sum(back.astype(F32))
            mid_grad = mid_grad + dot(back, w_up[f], NT)
        small_out[1:2] += column_sum(mid_grad * normed1)
        small_out[2:3] += column_sum(mid_grad)
        sum1 = norm_backward(mid_grad, normed1, inverse1, gain1)
        sum1_b[here] = sum1
        grad1 = (sum1 + pre_cot_b[here]).astype(BF16)
        branch_grad[here] = grad1
        small_out[0:1] += column_sum(grad1.astype(F32))
        att_grad_b[here] = dot(grad1, w_out[...], NT).astype(BF16)
        for n in (2, 1, 0):
            sent_grad(n, c).start()
        own_grad(c).start()
        for copy in stored(c):
            copy.start()
        return 0

    lax.fori_loop(0, count, block_step, 0)

    def weight_grads(s):
        up = dot(mid_low[...], act_grad[s], TN)
        down = dot(hidden[s], ffn_grad[...], TN)
        out = dot(att_in[:, ds(s * local, local)], branch_grad[...], TN)
        return up, down, out

    def sent_sums(n):
        return remote(send_b.at[n], recv_b.at[n], send_r.at[n], recv_r.at[n], (dp, sib))

    for n, owner in enumerate((diagonal, sib)):
        for span, part in zip(spans, weight_grads(owner)):
            send_b[n, span] = part.astype(BF16)
        sent_sums(n).start()
    for span, part in zip(spans, weight_grads(across)):
        keep_b[span] = part
    sent_sums(0).wait_recv()
    give_b[...] = (keep_b[...] + recv_b[0].astype(F32)).astype(BF16)
    give = pltpu.make_async_copy(give_b, give_out, own_sem.at[1])
    give.start()
    for span, part in zip(spans, weight_grads(me)):
        keep_b[span] = part
    sent_sums(1).wait_recv()
    keep_b[...] = keep_b[...] + recv_b[1].astype(F32)
    keep = pltpu.make_async_copy(keep_b, keep_out, own_sem.at[2])
    keep.start()
    for c in range(count):
        for copy in stored(c) + [own_grad(c)]:
            copy.wait()
        for n in range(3):
            sent_attended(n, c).wait_send()
            sent_grad(n, c).wait_send()
            arriving_grad(n, c).wait()
    for copy in sent_weights():
        copy.wait_send()
    for n in range(3):
        sent_prm(n).wait_send()
    for n in range(2):
        sent_sums(n).wait_send()
    give.wait()
    keep.wait()


def middle(att, post, pre, post_cot, pre_cot, own, far, vectors):
    rows, width = post.shape
    local = att.shape[1]
    tall = own.shape[0]
    hid = tall - width - local
    count = rows // TILE
    f32 = jax.ShapeDtypeStruct((rows, width), F32)
    return pl.pallas_call(
        middle_kernel,
        out_shape=(
            f32, f32, f32,
            jax.ShapeDtypeStruct(att.shape, BF16),
            jax.ShapeDtypeStruct((tall, width), F32),
            jax.ShapeDtypeStruct((tall, width), BF16),
            jax.ShapeDtypeStruct((16, width), F32),
        ),
        in_specs=[ANY] * 7 + [VMEM] * len(vectors),
        out_specs=(ANY,) * 6 + (VMEM,),
        scratch_shapes=[
            pltpu.VMEM((rows, width), F32),
            pltpu.VMEM((rows, width), F32),
            pltpu.VMEM((rows, width), F32),
            pltpu.VMEM((rows, width), F32),
            pltpu.VMEM((rows, MP * local), BF16),
            pltpu.VMEM((MP, width, hid), BF16),
            pltpu.VMEM((MP, hid, width), BF16),
            pltpu.VMEM((MP * local, width), BF16),
            pltpu.VMEM((8, hid), F32),
            pltpu.VMEM((MP, 8, hid), F32),
            pltpu.VMEM((rows, width), BF16),
            pltpu.VMEM((MP, rows, hid), BF16),
            pltpu.VMEM((MP, rows, hid), BF16),
            pltpu.VMEM((rows, width), BF16),
            pltpu.VMEM((rows, width), BF16),
            pltpu.VMEM((rows, MP * local), BF16),
            pltpu.VMEM((MP, TILE, hid), F32),
            pltpu.VMEM((rows, width), F32),
            pltpu.VMEM((rows, width), F32),
            pltpu.VMEM((rows, width), F32),
            pltpu.VMEM((2, tall, width), BF16),
            pltpu.VMEM((2, tall, width), BF16),
            pltpu.VMEM((tall, width), F32),
            pltpu.VMEM((tall, width), BF16),
            dma_sems(count, 4), dma_sems(3), dma_sems(2, 3), dma_sems(2, 3), dma_sems(2, 3),
            dma_sems(3), dma_sems(3), dma_sems(3, count), dma_sems(3, count),
            dma_sems(3, count), dma_sems(3, count), dma_sems(2), dma_sems(2), dma_sems(count, 4),
        ],
        compiler_params=pltpu.CompilerParams(
            collective_id=1, has_side_effects=True, vmem_limit_bytes=60 << 20
        ),
        cost_estimate=pl.CostEstimate(flops=15 << 30, bytes_accessed=20 << 20, transcendentals=4 << 20),
        name="middle",
    )(att, post, pre, post_cot, pre_cot, own, far, *vectors)


ROW_TIME = 0.0209
HOP_TIME = 2.5


def sum_plan(dp_size, width, hid, local):
    bits = dp_size.bit_length() - 1
    near_first = tuple(range(bits))
    swapped = (1, 0) + near_first[2:] if bits > 1 else near_first
    far_first = near_first[2:] + near_first[:2]
    half, sixth = width // 2, 3 * width // 8
    rows = [
        (half, near_first, 1.0), (half, near_first, 1.0), (hid // 2, swapped, 1.0), (hid // 2, far_first, 1.0),
        (local, far_first, 1.0), (sixth, near_first, 6.0), (sixth, swapped, 6.0),
    ]
    pieces, start = [], 0
    for size, order, ready in rows:
        steps = []
        left = size
        for b in order:
            halved = left % 32 == 0
            steps.append((b, left, halved))
            left = left // 2 if halved else left
        pieces.append((start, size, ready, steps))
        start += size
    return pieces, start


def plan_length(steps):
    return len(steps) + sum(halved for _, _, halved in steps)


def step_times(pieces, bits):
    free = [0.0] * bits
    waiting = [(ready, n, 0) for n, (_, _, ready, _) in enumerate(pieces)]
    times = []
    while waiting:
        now, n, t = min(waiting)
        waiting.remove((now, n, t))
        times.append((now, n, t))
        steps = pieces[n][3]
        if t == plan_length(steps):
            continue
        back = [s for s in reversed(steps) if s[2]]
        b, size, halved = steps[t] if t < len(steps) else back[t - len(steps)]
        cost = (size // 2 if halved else size) * ROW_TIME * (2 if b == 2 else 1)
        free[b] = max(now, free[b]) + cost
        waiting.append((free[b] + HOP_TIME, n, t + 1))
    return times


def tail_kernel(
    dp_size,
    dq, dk, dv, tok_t, w, sum1, keep, given, small,
    post_out, full_out, small_out,
    grads, tok_b, sum1_b, given_b, mine, far, send_far, recv_far, pass_far, land_far, send_near, recv_near,
    acc, flight, full, land, small_flight, small_land,
    in_sem, near_send, near_recv, far_send, far_recv, hop_send, hop_recv,
    step_send, step_recv, small_send, small_recv, out_sem, full_sem,
):
    me, sib, across, diagonal = mp_peers()
    dp = lax.axis_index("dp")
    rows, width = sum1.shape
    local = dq.shape[1]
    chunk = TILE
    count = rows // chunk
    tall = keep.shape[0]
    hid = tall - width - local
    bits = dp_size.bit_length() - 1
    partners = [dp + (1 << b) - 2 * (1 << b) * ((dp // (1 << b)) % 2) for b in range(bits)]
    upper = [(dp // (1 << b)) % 2 for b in range(bits)]
    pieces, total = sum_plan(dp_size, width, hid, local)

    loads = [
        pltpu.make_async_copy(src, grads.at[n], in_sem.at[n]) for n, src in enumerate((dq, dk, dv))
    ] + [
        pltpu.make_async_copy(tok_t, tok_b, in_sem.at[3]),
        pltpu.make_async_copy(keep, acc.at[pl.ds(0, tall)], in_sem.at[5]),
        pltpu.make_async_copy(given, given_b, in_sem.at[6]),
        pltpu.make_async_copy(sum1, sum1_b, in_sem.at[4]),
    ]
    for n in (4, 5, 0, 1, 2, 3, 6):
        loads[n].start()
    greet([(dp, sib), (dp, across)] + [(p, me) for p in partners])

    offsets = {}
    for n, (base, _, _, steps) in enumerate(pieces):
        base = jnp.int32(base)
        for t, (b, size, halved) in enumerate(steps):
            if halved:
                half = size // 2
                offsets[n, t] = (base + (1 - upper[b]) * half, base + upper[b] * half, half)
                base = base + upper[b] * half
            else:
                offsets[n, t] = (base, base, size)

    def reduce_copy(n, t):
        given_at, _, size = offsets[n, t]
        here = ds16(given_at, size)
        return remote(
            flight.at[here], land.at[t, here],
            step_send.at[0, n, t], step_recv.at[0, n, t], (partners[pieces[n][3][t][0]], me),
        )

    def reduce_start(n, t):
        given_at, _, size = offsets[n, t]
        here = ds16(given_at, size)
        flight[here] = acc[here].astype(BF16)
        reduce_copy(n, t).start()

    def reduce_finish(n, t):
        _, kept_at, size = offsets[n, t]
        copy = reduce_copy(n, t)
        copy.wait_recv()
        here = ds16(kept_at, size)
        if pieces[n][3][t][2]:
            acc[here] = acc[here] + land[t, here].astype(F32)
        else:
            acc[here] = flight[here].astype(F32) + land[t, here].astype(F32)
        copy.wait_send()

    def spread_copy(n, t):
        _, kept_at, size = offsets[n, t]
        here = ds16(kept_at, size)
        return remote(
            full.at[here], full.at[here],
            step_send.at[1, n, t], step_recv.at[1, n, t], (partners[pieces[n][3][t][0]], me),
        )

    def spread_done(n, t):
        given_at, _, size = offsets[n, t]
        there = ds16(given_at, size)
        pltpu.make_async_copy(full.at[there], full.at[there], step_recv.at[1, n, t]).wait()
        spread_copy(n, t).wait_send()

    def full_copy(n):
        here = pl.ds(pieces[n][0], pieces[n][1])
        return pltpu.make_async_copy(full.at[here], full_out.at[here], full_sem.at[n])

    def stage(n, t):
        steps = pieces[n][3]
        back = [s for s in range(len(steps) - 1, -1, -1) if steps[s][2]]
        if 0 < t <= len(steps):
            reduce_finish(n, t - 1)
        if t < len(steps):
            reduce_start(n, t)
            return
        if t == len(steps):
            _, kept_at, size = offsets[n, len(steps) - 1]
            here = ds16(kept_at, size)
            full[here] = acc[here].astype(BF16)
        else:
            spread_done(n, back[t - len(steps) - 1])
        if t < plan_length(steps):
            spread_copy(n, back[t - len(steps)]).start()
        else:
            full_copy(n).start()

    small_peers = [(dp, sib), (dp, across)] + [(p, me) for p in partners]

    def small_copy(s):
        return remote(small_flight.at[s], small_land.at[s], small_send.at[s], small_recv.at[s], small_peers[s])

    def small_stage(s):
        if s == 0:
            small_out[...] = small[...]
            query_sum = column_sum(grads[0].astype(F32))
            value_sum = column_sum(grads[2].astype(F32))
            small_out[ds1(12 + me), :] = jnp.concatenate(
                [query_sum, value_sum, jnp.zeros((1, width - 2 * local), F32)], axis=1
            )
        else:
            small_copy(s - 1).wait()
            small_out[...] = small_out[...] + small_land[s - 1]
        if s < len(small_peers):
            small_flight[s] = small_out[...]
            small_copy(s).start()

    def part(owner, c):
        here = ds(owner * rows + c * chunk, chunk)
        return (
            dot(grads[0, here], w[0], NT) + dot(grads[1, here], w[1], NT) + dot(grads[2, here], w[2], NT)
        )

    def far_copy(c):
        return remote(send_far.at[c], recv_far.at[c], far_send.at[c], far_recv.at[c], (dp, sib))

    def hop_copy(c):
        return remote(pass_far.at[c], land_far.at[c], hop_send.at[c], hop_recv.at[c], (dp, across))

    def near_copy(c):
        return remote(send_near.at[c], recv_near.at[c], near_send.at[c], near_recv.at[c], (dp, sib))

    def post_copy(c):
        here = pl.ds(c * chunk, chunk)
        return pltpu.make_async_copy(sum1_b.at[here], post_out.at[here], out_sem.at[c])

    def far_step(c):
        if c == 0:
            for n in range(3):
                loads[n].wait()
        send_far[c] = part(diagonal, c).astype(BF16)
        far_copy(c).start()
        far[c] = part(across, c)

    def hop_step(c):
        far_copy(c).wait_recv()
        pass_far[c] = (far[c] + recv_far[c].astype(F32)).astype(BF16)
        hop_copy(c).start()

    def near_step(c):
        send_near[c] = part(sib, c).astype(BF16)
        near_copy(c).start()
        mine[c] = part(me, c)

    def near_add(c):
        near_copy(c).wait_recv()
        mine[c] = mine[c] + recv_near[c].astype(F32)

    def post_step(c):
        if c == 0:
            loads[6].wait()
        hop_copy(c).wait_recv()
        here = pl.ds(c * chunk, chunk)
        sum1_b[here] = sum1_b[here] + mine[c] + land_far[c].astype(F32)
        post_copy(c).start()

    def own_sums(_):
        loads[4].wait()
        loads[5].wait()
        own = pl.ds(0, tall)
        acc[own] = acc[own] + given_b[...].astype(F32)

    def weight_step(_):
        loads[3].wait()
        third = width // 4
        for n in range(3):
            block = dot(tok_b[...], grads[n])
            for s in range(4):
                acc[pl.ds(tall + n * third, third), pl.ds(s * local, local)] = block[s * third : (s + 1) * third]

    events = [(now, 5, stage, (n, t)) for now, n, t in step_times(pieces, bits)]
    events += [(0.9, 0, own_sums, (0,)), (5.9, 0, weight_step, (0,))]
    for c in range(count):
        events.append((1.5 + 0.7 * c, 1, far_step, (c,)))
        events.append((2.9 + 0.7 * c, 2, hop_step, (c,)))
        events.append((6.5 + 0.7 * c, 3, near_step, (c,)))
        events.append((11.0 + 0.7 * c, 3, near_add, (c,)))
        events.append((12.5 + 5.3 * c, 6, post_step, (c,)))
    for s in range(len(small_peers) + 1):
        events.append((9.5 + 3.5 * s, 4, small_stage, (s,)))
    for _, _, act, where in sorted(events, key=lambda event: event[:2] + (event[3],)):
        act(*where)

    for c in range(count):
        far_copy(c).wait_send()
        hop_copy(c).wait_send()
        near_copy(c).wait_send()
        post_copy(c).wait()
    for n in range(len(pieces)):
        full_copy(n).wait()


def ds16(start, size):
    return pl.ds(pl.multiple_of(start, 16), size)


def ds1(start):
    return pl.ds(start, 1)


def tail(dp_size, dq, dk, dv, tok_t, w, sum1, keep, given, small):
    rows, width = sum1.shape
    group, local = dq.shape
    tall = keep.shape[0]
    hid = tall - width - local
    count = rows // TILE
    bits = dp_size.bit_length() - 1
    assert 1 << bits == dp_size
    pieces, total = sum_plan(dp_size, width, hid, local)
    blocks = (count, TILE, width)
    steps = bits + 2
    return pl.pallas_call(
        functools.partial(tail_kernel, dp_size),
        out_shape=(
            jax.ShapeDtypeStruct((rows, width), F32),
            jax.ShapeDtypeStruct((total, width), BF16),
            jax.ShapeDtypeStruct(small.shape, F32),
        ),
        in_specs=[ANY] * 4 + [VMEM] + [ANY] * 3 + [VMEM],
        out_specs=(ANY, ANY, VMEM),
        scratch_shapes=[
            pltpu.VMEM((3, group, local), BF16),
            pltpu.VMEM((width, group), BF16),
            pltpu.VMEM((rows, width), F32),
            pltpu.VMEM((tall, width), BF16),
            pltpu.VMEM(blocks, F32),
            pltpu.VMEM(blocks, F32),
            pltpu.VMEM(blocks, BF16),
            pltpu.VMEM(blocks, BF16),
            pltpu.VMEM(blocks, BF16),
            pltpu.VMEM(blocks, BF16),
            pltpu.VMEM(blocks, BF16),
            pltpu.VMEM(blocks, BF16),
            pltpu.VMEM((total, width), F32),
            pltpu.VMEM((total, width), BF16),
            pltpu.VMEM((total, width), BF16),
            pltpu.VMEM((bits, total, width), BF16),
            pltpu.VMEM((steps,) + small.shape, F32),
            pltpu.VMEM((steps,) + small.shape, F32),
            dma_sems(7), dma_sems(count), dma_sems(count), dma_sems(count), dma_sems(count),
            dma_sems(count), dma_sems(count), dma_sems(2, len(pieces), bits), dma_sems(2, len(pieces), bits),
            dma_sems(steps), dma_sems(steps), dma_sems(count), dma_sems(len(pieces)),
        ],
        compiler_params=pltpu.CompilerParams(
            collective_id=2, has_side_effects=True, vmem_limit_bytes=60 << 20
        ),
        cost_estimate=pl.CostEstimate(flops=4 << 30, bytes_accessed=20 << 20, transcendentals=0),
        name="tail",
    )(dq, dk, dv, tok_t, w, sum1, keep, given, small)


def finish_kernel(
    post_sum, full, small,
    post_grad, qkv_grad, up_grad, down_grad, out_grad,
    query_grad, value_grad, out_bias, gain1, shift1, up_bias, down_bias, gain2, shift2,
    post_b, full_b, grad_b, qkv_b, sem, out_sem,
):
    me = lax.axis_index("mp")
    total, width = full.shape
    local = query_grad.shape[0]
    hid = down_grad.shape[0]
    tall = width + hid + local
    third = width // 4
    post_in = pltpu.make_async_copy(post_sum, post_b, sem.at[0])
    post = pltpu.make_async_copy(post_b, post_grad, sem.at[5])
    post_in.start()
    spans = ((0, width, up_grad), (width, hid, down_grad), (width + hid, local, out_grad), (tall, total - tall, None))
    loads = []
    for n, (start, size, _) in enumerate(spans):
        here = pl.ds(start, size)
        loads.append(pltpu.make_async_copy(full.at[here], full_b.at[here], sem.at[1 + n]))
        loads[-1].start()
    for row, vector in enumerate((out_bias, gain1, shift1, down_bias, gain2, shift2)):
        vector[...] = small[row]
    own = small[pl.ds(12 + me, 1), :]
    query_grad[...] = own[0, :local]
    value_grad[...] = own[0, local : 2 * local]
    up_bias[...] = small[pl.ds(8 + me, 1), :][0]
    stores = []
    post_in.wait()
    post.start()
    for n, (start, size, dst) in enumerate(spans):
        loads[n].wait()
        here = pl.ds(start, size)
        if dst is not None:
            grad_b[here] = full_b[here].astype(F32)
            stores.append(pltpu.make_async_copy(grad_b.at[here], dst, out_sem.at[n]))
        else:
            for m in range(3):
                for s in range(4):
                    qkv_b[m, pl.ds(s * third, third)] = full_b[
                        pl.ds(start + m * third, third), pl.ds(s * local, local)
                    ].astype(F32)
            stores.append(pltpu.make_async_copy(qkv_b, qkv_grad, out_sem.at[n]))
        stores[-1].start()
    for store in stores + [post]:
        store.wait()


def finish(post_sum, full, small, hid, local):
    rows, width = post_sum.shape
    total = full.shape[0]
    vector = lambda size: jax.ShapeDtypeStruct((size,), F32)
    return pl.pallas_call(
        finish_kernel,
        out_shape=(
            jax.ShapeDtypeStruct((rows, width), F32),
            jax.ShapeDtypeStruct((3, width, local), F32),
            jax.ShapeDtypeStruct((width, hid), F32),
            jax.ShapeDtypeStruct((hid, width), F32),
            jax.ShapeDtypeStruct((local, width), F32),
            vector(local), vector(local), vector(width), vector(width), vector(width),
            vector(hid), vector(width), vector(width), vector(width),
        ),
        in_specs=[ANY, ANY, VMEM],
        out_specs=(ANY,) * 5 + (VMEM,) * 9,
        scratch_shapes=[
            pltpu.VMEM((rows, width), F32),
            pltpu.VMEM((total, width), BF16),
            pltpu.VMEM((total, width), F32),
            pltpu.VMEM((3, width, local), F32),
            dma_sems(6), dma_sems(4),
        ],
        compiler_params=pltpu.CompilerParams(vmem_limit_bytes=60 << 20),
        name="results",
    )(post_sum, full, small)


def body(
    dp_size,
    post_stream,
    pre_stream,
    seq_lengths,
    qkv_weight,
    query_bias,
    value_bias,
    out_weight,
    out_bias,
    norm1_gain,
    norm1_shift,
    up_weight,
    up_bias,
    down_weight,
    down_bias,
    norm2_gain,
    norm2_shift,
    post_cotan,
    pre_cotan,
):
    local = out_weight.shape[0]
    hid = down_weight.shape[0]
    qkv3 = jnp.transpose(qkv_weight, (1, 0, 2))
    tok_t, queries, k, v, kt, vt, starts, limits, own = gather_and_project(
        seq_lengths, post_stream, qkv3, query_bias, value_bias, (up_weight, down_weight, out_weight)
    )
    across = [(m, (m + 2) % MP) for m in range(MP)]
    far = lax.ppermute(own, "mp", across)
    att, lse, tiles, counts = attend(limits, starts, queries, k, vt)
    vectors = (out_bias, norm1_gain, norm1_shift, down_bias, norm2_gain, norm2_shift, up_bias)
    post_mid, pre_mid, sum1, att_grad, keep, give, small = middle(
        att, post_stream, pre_stream, post_cotan, pre_cotan, own, far, vectors
    )
    given = lax.ppermute(give, "mp", across)
    dq, dk, dv, post_out, pre_out = attend_back(
        tiles, counts, starts, lse, queries, k, v, kt, att, att_grad, post_mid, pre_mid
    )
    post_sum, full, small = tail(dp_size, dq, dk, dv, tok_t, qkv3, sum1, keep, given, small)
    (
        post_grad, qkv_grad, up_grad, down_grad, out_grad,
        query_grad, value_grad, out_bias_grad, gain1, shift1, up_bias_grad, down_bias_grad, gain2, shift2,
    ) = finish(post_sum, full, small, hid, local)
    return (
        post_out, pre_out, post_grad, jnp.transpose(qkv_grad, (1, 0, 2)), query_grad, value_grad, out_grad,
        out_bias_grad, gain1, shift1, up_grad, up_bias_grad, down_grad, down_bias_grad, gain2, shift2,
    )


def solution(mesh):
    tokens = P(("dp", "mp"), None)
    vector = P()
    return jax.shard_map(
        functools.partial(body, mesh.shape["dp"]),
        mesh=mesh,
        in_specs=(
            tokens, tokens, P("dp", None), P(None, None, "mp"), P("mp"), P("mp"), P("mp", None),
            vector, vector, vector, P(None, "mp"), P("mp"), P("mp", None), vector, vector, vector,
            tokens, tokens,
        ),
        out_specs=(
            tokens, tokens, tokens, P(None, None, "mp"), P("mp"), P("mp"), P("mp", None),
            vector, vector, vector, P(None, "mp"), P("mp"), P("mp", None), vector, vector, vector,
        ),
        check_vma=False,
    )
```

```python
import functools

import jax
import jax.numpy as jnp
from jax import lax
from jax.experimental import pallas as pl
from jax.experimental.pallas import tpu as pltpu
from jax.sharding import PartitionSpec as P

HEAD_DIM = 64
EPSILON = 1e-05
MASKED = -1e30
MP = 4
TILE = 256
MESH = pl.DeviceIdType.MESH
BF16 = jnp.bfloat16
F32 = jnp.float32
ANY = pl.BlockSpec(memory_space=pl.ANY)
VMEM = pl.BlockSpec(memory_space=pltpu.VMEM)
SMEM = pl.BlockSpec(memory_space=pltpu.SMEM)
NT = (((1,), (1,)), ((), ()))
TN = (((0,), (0,)), ((), ()))
SQRT_2_OVER_PI = 0.7978845608028654


def ds(start, size):
    return pl.ds(pl.multiple_of(start, size), size)


def mp_peers():
    me = lax.axis_index("mp")
    sib = me + 1 - 2 * (me % 2)
    across = (me + 2) % MP
    diagonal = (sib + 2) % MP
    return me, sib, across, diagonal


def greet(devices):
    barrier = pltpu.get_barrier_semaphore()
    for device in devices:
        pl.semaphore_signal(barrier, inc=1, device_id=device, device_id_type=MESH)
    pl.semaphore_wait(barrier, len(devices))


def ds16(start, size):
    return pl.ds(pl.multiple_of(start, 16), size)


def remote(src, dst, send_sem, recv_sem, device):
    return pltpu.make_async_remote_copy(
        src_ref=src,
        dst_ref=dst,
        send_sem=send_sem,
        recv_sem=recv_sem,
        device_id=device,
        device_id_type=MESH,
    )


def dot(a, b, dims=(((1,), (0,)), ((), ()))):
    return lax.dot_general(a, b, dims, preferred_element_type=F32)


def column_sum(block):
    return jnp.sum(block, axis=0, keepdims=True)


def as_row(vector):
    return vector[...].astype(F32).reshape(1, vector.shape[0])


def dma_sems(*shape):
    return pltpu.SemaphoreType.DMA(shape)


def first_of_segment(bounds, place):
    start = jnp.zeros_like(place)
    for bound in bounds:
        start = jnp.where(place >= bound, bound, start)
    return jnp.where(place >= bounds[-1], place, start)


def head_masked(block, h):
    lane = lax.broadcasted_iota(jnp.int32, block.shape, 1)
    return jnp.where((lane >= h * HEAD_DIM) & (lane < (h + 1) * HEAD_DIM), block, jnp.zeros_like(block))


def dp_slices(dp_size):
    return min(dp_size, 8)


def project_kernel(
    dp_size,
    lengths, post, w_any, query_bias_ref, value_bias_ref, up, down, out,
    tok_t_out, q_out, k_out, v_out, kt_out, vt_out, starts, limits, own_out, line_out,
    stage, w, own_b, line_b, tok, tok_t, q_s, k_s, v_s, kt_s, vt_s,
    w_sem, line_send, line_recv, in_sem, send_x, recv_x, send_c, recv_c, send_f, recv_f, out_sem,
):
    me, sib, across, diagonal = mp_peers()
    dp = lax.axis_index("dp")
    rows = post.shape[0]
    width = post.shape[1]
    chunk = TILE // 2
    count = rows // chunk
    heads = w.shape[2] // HEAD_DIM
    hid = up.shape[1]
    packs = []
    for n, (src, start) in enumerate(((up, 0), (down, width), (out, width + hid))):
        packs.append(pltpu.make_async_copy(src, own_b.at[pl.ds(start, src.shape[0])], w_sem.at[1 + n]))
    packed = pltpu.make_async_copy(own_b, own_out, w_sem.at[4])
    w_load = pltpu.make_async_copy(w_any, w, w_sem.at[0])
    loads = [
        pltpu.make_async_copy(post.at[pl.ds(c * chunk, chunk)], stage.at[pl.ds(c * chunk, chunk)], in_sem.at[c])
        for c in range(count)
    ]
    for load in loads + [w_load] + packs:
        load.start()
    slices = dp_slices(dp_size)
    line = slices // 2
    spot = (dp // 2) % line
    part = own_b.shape[0] // slices
    line_peers = []
    for mask in range(1, line):
        peer = dp
        for b in range(line.bit_length() - 1):
            if mask >> b & 1:
                peer = peer + (2 << b) - 2 * (2 << b) * ((dp // (2 << b)) % 2)
        line_peers.append(peer)
    greet([(dp, sib), (dp, across)] + [(peer, me) for peer in line_peers])

    def slice_over():
        return remote(
            own_b.at[ds16(((dp % 2) * line + spot) * part, part)], line_b.at[ds16(spot * part, part)],
            line_send.at[0], line_recv.at[0], (dp, across),
        )

    def slice_along(n):
        here = ds16(spot * part, part)
        return remote(line_b.at[here], line_b.at[here], line_send.at[1 + n], line_recv.at[1 + n], (line_peers[n], me))

    def slice_arrived(n):
        here = ds16(((line_peers[n] // 2) % line) * part, part)
        return pltpu.make_async_copy(line_b.at[here], line_b.at[here], line_recv.at[1 + n])

    def piece(owner, c):
        return ds(owner * rows + c * chunk, chunk)

    def to_across(c):
        here = piece(me, c)
        return remote(tok.at[here], tok.at[here], send_x.at[c], recv_x.at[c], (dp, across))

    def to_sibling(c):
        here = piece(me, c)
        return remote(tok.at[here], tok.at[here], send_c.at[c], recv_c.at[c], (dp, sib))

    def forward(c):
        here = piece(across, c)
        return remote(tok.at[here], tok.at[here], send_f.at[c], recv_f.at[c], (dp, sib))

    def arrived(owner, sem, c):
        here = piece(owner, c)
        return pltpu.make_async_copy(tok.at[here], tok.at[here], sem.at[c])

    for c in range(count):
        loads[c].wait()
        tok[piece(me, c)] = stage[pl.ds(c * chunk, chunk)].astype(BF16)
        to_across(c).start()
        to_sibling(c).start()
        if c == 0:
            for pack in packs:
                pack.wait()
            slice_over().start()
            packed.start()

    query_bias = as_row(query_bias_ref)
    value_bias = as_row(value_bias_ref)

    def project(owner, c):
        here = piece(owner, c)
        block = tok[here]
        tok_t[:, here] = block.T
        query = (dot(block, w[0]) + query_bias).astype(BF16)
        query = (query.astype(F32) * HEAD_DIM ** (-0.5)).astype(BF16)
        for h in range(heads):
            q_s[owner * (rows // TILE) + c // 2, ds(h * TILE + (c % 2) * chunk, chunk)] = head_masked(query, h)
        keys = dot(block, w[1]).astype(BF16)
        k_s[here] = keys
        kt_s[:, here] = keys.T
        values = (dot(block, w[2]) + value_bias).astype(BF16)
        v_s[here] = values
        vt_s[:, here] = values.T

    def outs(g, owner, c):
        here = ds(owner * rows + c * TILE, TILE)
        block = owner * (rows // TILE) + c
        return [
            pltpu.make_async_copy(tok_t.at[:, here], tok_t_out.at[:, here], out_sem.at[g, c, 0]),
            pltpu.make_async_copy(q_s.at[block], q_out.at[block], out_sem.at[g, c, 1]),
            pltpu.make_async_copy(k_s.at[here], k_out.at[here], out_sem.at[g, c, 2]),
            pltpu.make_async_copy(v_s.at[here], v_out.at[here], out_sem.at[g, c, 3]),
            pltpu.make_async_copy(kt_s.at[:, here], kt_out.at[:, here], out_sem.at[g, c, 4]),
            pltpu.make_async_copy(vt_s.at[:, here], vt_out.at[:, here], out_sem.at[g, c, 5]),
        ]

    w_load.wait()
    bounds = [lengths[0, 0]]
    for s in range(1, lengths.shape[1] - 1):
        bounds.append(bounds[-1] + lengths[0, s])
    for i in range(starts.shape[0]):
        place = i * TILE + lax.broadcasted_iota(jnp.int32, (1, starts.shape[2]), 1) % TILE
        starts[i] = jnp.broadcast_to(first_of_segment(bounds, place), starts.shape[1:])
        limits[0, i] = first_of_segment(bounds, jnp.int32(i * TILE)) // TILE
        last = first_of_segment(bounds, jnp.int32(i * TILE + TILE - 1))
        limits[1, i] = jnp.minimum((last + TILE - 1) // TILE, i)

    def own_step(c, _):
        project(me, 2 * c)
        project(me, 2 * c + 1)
        for copy in outs(0, me, c):
            copy.start()
        return 0

    lax.fori_loop(0, count // 2, own_step, 0)

    def sibling_step(c, _):
        for n in (0, 1):
            arrived(sib, recv_c, 2 * c + n).wait()
            project(sib, 2 * c + n)
        for copy in outs(1, sib, c):
            copy.start()
        return 0

    lax.fori_loop(0, count // 2, sibling_step, 0)

    def slices_on(_):
        slice_over().wait_recv()
        for n in range(len(line_peers)):
            slice_along(n).start()

    slices_on(0)

    def across_step(c, _):
        for n in (0, 1):
            arrived(across, recv_x, 2 * c + n).wait()
            forward(2 * c + n).start()
            project(across, 2 * c + n)
        for copy in outs(2, across, c):
            copy.start()
        for n in (0, 1):
            arrived(diagonal, recv_f, 2 * c + n).wait()
            project(diagonal, 2 * c + n)
        for copy in outs(3, diagonal, c):
            copy.start()
        return 0

    lax.fori_loop(0, count // 2, across_step, 0)
    for c in range(count):
        to_across(c).wait_send()
        to_sibling(c).wait_send()
        forward(c).wait_send()
    packed.wait()
    slice_over().wait_send()
    for n in range(len(line_peers)):
        slice_along(n).wait_send()
        slice_arrived(n).wait()
    line_copy = pltpu.make_async_copy(line_b, line_out, w_sem.at[5])
    line_copy.start()
    for g, owner in enumerate((me, sib, across, diagonal)):
        for c in range(count // 2):
            for copy in outs(g, owner, c):
                copy.wait()
    line_copy.wait()


def gather_and_project(dp_size, lengths, post_stream, qkv3, query_bias, value_bias, own):
    rows, width = post_stream.shape
    group = rows * MP
    local = qkv3.shape[2]
    count = 2 * rows // TILE
    tall = jax.ShapeDtypeStruct((group, local), BF16)
    wide = jax.ShapeDtypeStruct((local, group), BF16)
    blocks = group // TILE
    across = TILE * (local // HEAD_DIM)
    tall_rows = sum(part.shape[0] for part in own)
    line = dp_slices(dp_size) // 2
    return pl.pallas_call(
        functools.partial(project_kernel, dp_size),
        out_shape=(
            jax.ShapeDtypeStruct((width, group), BF16),
            jax.ShapeDtypeStruct((blocks, across, local), BF16),
            tall, tall, wide, wide,
            jax.ShapeDtypeStruct((blocks, 8, across), jnp.int32),
            jax.ShapeDtypeStruct((2, blocks), jnp.int32),
            jax.ShapeDtypeStruct((tall_rows, width), BF16),
            jax.ShapeDtypeStruct((tall_rows // 2, width), BF16),
        ),
        in_specs=[SMEM, ANY, ANY, VMEM, VMEM, ANY, ANY, ANY],
        out_specs=(ANY,) * 6 + (VMEM, SMEM, ANY, ANY),
        scratch_shapes=[
            pltpu.VMEM((rows, width), F32),
            pltpu.VMEM(qkv3.shape, BF16),
            pltpu.VMEM((tall_rows, width), BF16),
            pltpu.VMEM((tall_rows // 2, width), BF16),
            pltpu.VMEM((group, width), BF16),
            pltpu.VMEM((width, group), BF16),
            pltpu.VMEM((blocks, across, local), BF16),
            pltpu.VMEM((group, local), BF16),
            pltpu.VMEM((group, local), BF16),
            pltpu.VMEM((local, group), BF16),
            pltpu.VMEM((local, group), BF16),
            dma_sems(6), dma_sems(line), dma_sems(line), dma_sems(count), dma_sems(count), dma_sems(count), dma_sems(count),
            dma_sems(count), dma_sems(count), dma_sems(count), dma_sems(4, count // 2, 6),
        ],
        compiler_params=pltpu.CompilerParams(
            collective_id=0, has_side_effects=True, vmem_limit_bytes=60 << 20
        ),
        cost_estimate=pl.CostEstimate(flops=2 * group * width * 3 * local, bytes_accessed=12 << 20, transcendentals=0),
        name="gather_project",
    )(lengths, post_stream, qkv3, query_bias, value_bias, *own)


UNROLL = 8


def list_tiles(limits, tiles, counts, blocks):
    spare = jnp.int32(blocks * 65536)
    tiles[0] = spare
    tiles[1] = spare

    def put(code, first, last, at):
        def step(j, at):
            tiles[at] = code + j
            return at + 1

        return lax.fori_loop(first, last, step, at)

    def diagonal(i, at):
        tiles[at] = i * 65536 + i * 257
        return at + 1

    def edge_row(i, at):
        return put(i * 65536 + i * 256, limits[0, i], limits[1, i], at)

    def whole_row(i, at):
        return put(i * 65536 + i * 256, jnp.maximum(limits[0, i], limits[1, i]), i, at)

    at = jnp.int32(2)
    for kind, row in enumerate((diagonal, edge_row, whole_row)):
        at = lax.fori_loop(0, blocks, row, at)
        counts[kind] = (at - 2 + (1 if kind < 2 else 2) + UNROLL - 1) // UNROLL
    for u in range(2 * UNROLL + 2):
        tiles[at + u] = spare


def for_tiles(tiles, counts, heads, products, probabilities, sums):
    for kind in range(3):

        def step(n, _):
            codes = [tiles[n * UNROLL + u] for u in range(UNROLL + 2)]
            entries = [(code // 65536, (code // 256) % 256, code % 256) for code in codes]
            for u in range(UNROLL):
                for h in range(heads):
                    if products is not None:
                        products(u % 2, h, *entries[u + 2])
                    sums(u % 2, h, *entries[u])
                    probabilities((u + 1) % 2, h, kind, *entries[u + 1])
            return 0

        lax.fori_loop(counts[kind - 1] if kind else 0, counts[kind], step, 0)


def masked_score(score, kind, starts, i, j, lanes):
    if kind == 2:
        return score
    keys, queries = score.shape
    score = score.reshape(keys // 8, 8, queries)
    row = 8 * lax.broadcasted_iota(jnp.int32, score.shape, 0)
    key = lax.broadcasted_iota(jnp.int32, (8, queries), 0) + j * TILE
    allowed = (key - starts[i, :, lanes])[None] >= -row
    if kind == 0:
        query = lax.broadcasted_iota(jnp.int32, (8, queries), 1) + i * TILE
        allowed = allowed & ((key - query)[None] <= -row)
    return jnp.where(allowed, score, MASKED).reshape(keys, queries)


def tile_limit(blocks):
    return blocks * (blocks + 1) // 2 + 4 * UNROLL


def attend_kernel(
    limits, starts_ref, q_ref, k_ref, vt_ref, att_ref, lse_ref, tiles, counts,
    queries, k, vt, top, total, acc, scores, probs, alphas, att_b, sem, out_sem,
):
    blocks, wide, local = queries.shape
    heads = local // HEAD_DIM
    one = pl.ds(0, 1)
    loads = [
        pltpu.make_async_copy(src, dst, sem.at[n])
        for n, (src, dst) in enumerate(((q_ref, queries), (k_ref, k), (vt_ref, vt)))
    ]
    for load in loads:
        load.start()
    list_tiles(limits, tiles, counts, blocks)
    top[...] = jnp.full_like(top, MASKED)
    total[...] = jnp.zeros_like(total)
    acc[...] = jnp.zeros_like(acc)
    for load in loads:
        load.wait()

    def products(b, h, slot, i, j):
        lanes = pl.ds(h * TILE, TILE)
        scores[b, :, lanes] = dot(k[ds(j * TILE, TILE)], queries[i, lanes], NT)

    def probabilities(b, h, kind, slot, i, j):
        lanes = pl.ds(h * TILE, TILE)
        score = scores[b, :, lanes]
        score = masked_score(score, kind, starts_ref, i, j, lanes)
        old = top[slot, one, lanes]
        new = jnp.maximum(old, jnp.max(score, axis=0, keepdims=True))
        top[slot, one, lanes] = new
        alpha = jnp.exp(old - new)
        prob = jnp.exp(score - new)
        total[slot, one, lanes] = total[slot, one, lanes] * alpha + jnp.sum(prob, axis=0, keepdims=True)
        probs[b, :, lanes] = prob.astype(BF16)
        alphas[b, one, lanes] = alpha

    def sums(b, h, slot, i, j):
        lanes = pl.ds(h * TILE, TILE)
        values_t = vt[pl.ds(h * HEAD_DIM, HEAD_DIM), ds(j * TILE, TILE)]
        acc[slot, :, lanes] = acc[slot, :, lanes] * alphas[b, one, lanes] + dot(values_t, probs[b, :, lanes])

    for_tiles(tiles, counts, heads, products, probabilities, sums)

    def finish(i, _):
        lse_ref[i, one] = top[i, one] + jnp.log(total[i, one])
        out_t = acc[i] / total[i, one]
        here = ds(i * TILE, TILE)
        parts = [out_t[:, h * TILE : (h + 1) * TILE] for h in range(heads)]
        att_b[here] = jnp.concatenate(parts, axis=0).T.astype(BF16)
        pltpu.make_async_copy(att_b.at[here], att_ref.at[here], out_sem.at[i]).start()
        return 0

    lax.fori_loop(0, blocks, finish, 0, unroll=4)
    for i in range(blocks):
        here = pl.ds(i * TILE, TILE)
        pltpu.make_async_copy(att_b.at[here], att_ref.at[here], out_sem.at[i]).wait()


def attend(limits, starts, queries, k, vt):
    group, local = k.shape
    blocks, wide, _ = queries.shape
    return pl.pallas_call(
        attend_kernel,
        in_specs=[SMEM, VMEM, ANY, ANY, ANY],
        out_specs=[ANY, VMEM, SMEM, SMEM],
        out_shape=(
            jax.ShapeDtypeStruct((group, local), BF16),
            jax.ShapeDtypeStruct((blocks, 8, wide), F32),
            jax.ShapeDtypeStruct((tile_limit(blocks),), jnp.int32),
            jax.ShapeDtypeStruct((3,), jnp.int32),
        ),
        scratch_shapes=[
            pltpu.VMEM((blocks, wide, local), BF16),
            pltpu.VMEM((group, local), BF16),
            pltpu.VMEM((local, group), BF16),
            pltpu.VMEM((blocks + 1, 8, wide), F32),
            pltpu.VMEM((blocks + 1, 8, wide), F32),
            pltpu.VMEM((blocks + 1, HEAD_DIM, wide), F32),
            pltpu.VMEM((2, TILE, wide), F32),
            pltpu.VMEM((2, TILE, wide), BF16),
            pltpu.VMEM((2, 8, wide), F32),
            pltpu.VMEM((group, local), BF16),
            dma_sems(3), dma_sems(blocks),
        ],
        compiler_params=pltpu.CompilerParams(vmem_limit_bytes=60 << 20),
        cost_estimate=pl.CostEstimate(flops=12 << 30, bytes_accessed=4 << 20, transcendentals=8 << 20),
        name="attend",
    )(limits, starts, queries, k, vt)


def attend_back_kernel(
    tiles, counts, starts_ref, lse, q_ref, do_ref, o_ref, k_ref, v_ref, kt_ref, post_mid, pre_mid,
    dq_ref, dk_ref, dv_ref, post_out, pre_out,
    queries, do, o, k, v, kt, grads, delta, dq_acc, dk_acc, dv_acc,
    probs, score_grads, passed_b, out_b, sem, out_sem,
):
    blocks, wide, local = queries.shape
    heads = local // HEAD_DIM
    one = pl.ds(0, 1)
    loads = [
        pltpu.make_async_copy(src, dst, sem.at[n])
        for n, (src, dst) in enumerate(((do_ref, do), (o_ref, o), (q_ref, queries), (k_ref, k), (v_ref, v), (kt_ref, kt)))
    ]
    passed_in = [
        pltpu.make_async_copy(src, passed_b.at[n], sem.at[6 + n]) for n, src in enumerate((post_mid, pre_mid))
    ]
    passed_out = [
        pltpu.make_async_copy(passed_b.at[n], dst, sem.at[8 + n]) for n, dst in enumerate((post_out, pre_out))
    ]
    for load in loads + passed_in:
        load.start()
    dq_acc[...] = jnp.zeros_like(dq_acc)
    dk_acc[...] = jnp.zeros_like(dk_acc)
    dv_acc[...] = jnp.zeros_like(dv_acc)
    for load in loads[:2]:
        load.wait()

    def prepare(i, _):
        here = ds(i * TILE, TILE)
        block = do[here]
        for h in range(heads):
            grads[i, pl.ds(h * TILE, TILE)] = head_masked(block, h)
        along = (block.astype(F32) * o[here].astype(F32)).T
        parts = [column_sum(along[h * HEAD_DIM : (h + 1) * HEAD_DIM]) for h in range(heads)]
        delta[i, one] = jnp.concatenate(parts, axis=1)
        return 0

    lax.fori_loop(0, blocks, prepare, 0, unroll=4)
    for load in loads[2:]:
        load.wait()
    for copy_in, copy_out in zip(passed_in, passed_out):
        copy_in.wait()
        copy_out.start()

    def probabilities(b, h, kind, slot, i, j):
        lanes = pl.ds(h * TILE, TILE)
        here = ds(j * TILE, TILE)
        score = dot(k[here], queries[i, lanes], NT)
        score = masked_score(score, kind, starts_ref, i, j, lanes)
        rise = dot(v[here], grads[i, lanes], NT)
        prob = jnp.exp(score - lse[i, one, lanes])
        probs[b, :, lanes] = prob.astype(BF16)
        score_grads[b, :, lanes] = (prob * (rise - delta[i, one, lanes])).astype(BF16)

    def sums(b, h, slot, i, j):
        lanes = pl.ds(h * TILE, TILE)
        spot = ds(jnp.where(slot == blocks, blocks, j) * TILE, TILE)
        if h == 0:
            dv_acc[spot] += dot(probs[b], grads[i])
        else:
            dk_acc[spot] += dot(score_grads[b], queries[i])
        keys_t = kt[pl.ds(h * HEAD_DIM, HEAD_DIM), ds(j * TILE, TILE)]
        dq_acc[slot, :, lanes] += dot(keys_t, score_grads[b, :, lanes])

    for_tiles(tiles, counts, heads, None, probabilities, sums)

    outs = (dq_ref, dk_ref, dv_ref)

    def out_copy(n, i):
        here = ds(i * TILE, TILE)
        return pltpu.make_async_copy(out_b.at[n, here], outs[n].at[here], out_sem.at[n, i])

    def finish(i, _):
        here = ds(i * TILE, TILE)
        dq_t = dq_acc[i] * HEAD_DIM ** (-0.5)
        parts = [dq_t[:, h * TILE : (h + 1) * TILE] for h in range(heads)]
        out_b[0, here] = jnp.concatenate(parts, axis=0).T.astype(BF16)
        out_b[1, here] = dk_acc[here].astype(BF16)
        out_b[2, here] = dv_acc[here].astype(BF16)
        for n in range(3):
            out_copy(n, i).start()
        return 0

    lax.fori_loop(0, blocks, finish, 0, unroll=4)
    for i in range(blocks):
        for n in range(3):
            out_copy(n, i).wait()
    for copy in passed_out:
        copy.wait()


def attend_back(tiles, counts, starts, lse, queries, k, v, kt, att, att_grad, post_mid, pre_mid):
    group, local = k.shape
    blocks, wide, _ = queries.shape
    shape = jax.ShapeDtypeStruct((group, local), BF16)
    tall = pltpu.VMEM((group, local), BF16)
    return pl.pallas_call(
        attend_back_kernel,
        in_specs=[SMEM, SMEM, VMEM, VMEM] + [ANY] * 8,
        out_specs=[ANY] * 5,
        out_shape=(shape, shape, shape, jax.ShapeDtypeStruct(post_mid.shape, F32), jax.ShapeDtypeStruct(pre_mid.shape, F32)),
        scratch_shapes=[
            pltpu.VMEM((blocks, wide, local), BF16),
            tall, tall, tall, tall,
            pltpu.VMEM((local, group), BF16),
            pltpu.VMEM((blocks, wide, local), BF16),
            pltpu.VMEM((blocks, 8, wide), F32),
            pltpu.VMEM((blocks + 1, HEAD_DIM, wide), F32),
            pltpu.VMEM((group + TILE, local), F32),
            pltpu.VMEM((group + TILE, local), F32),
            pltpu.VMEM((2, TILE, wide), BF16),
            pltpu.VMEM((2, TILE, wide), BF16),
            pltpu.VMEM((2,) + post_mid.shape, F32),
            pltpu.VMEM((3, group, local), BF16),
            dma_sems(10), dma_sems(3, blocks),
        ],
        compiler_params=pltpu.CompilerParams(vmem_limit_bytes=60 << 20),
        cost_estimate=pl.CostEstimate(flops=30 << 30, bytes_accessed=9 << 20, transcendentals=8 << 20),
        name="attend_back",
    )(tiles, counts, starts, lse, queries, att_grad, att, k, v, kt, post_mid, pre_mid)


def center_and_scale(summed):
    width = summed.shape[1]
    center = summed - jnp.sum(summed, axis=1, keepdims=True) * (1.0 / width)
    inverse = lax.rsqrt(jnp.sum(center * center, axis=1, keepdims=True) * (1.0 / width) + EPSILON)
    return center * inverse, inverse


def norm_backward(cotangent, normed, inverse, gain):
    width = normed.shape[1]
    scaled = cotangent * gain
    mean = jnp.sum(scaled, axis=1, keepdims=True) * (1.0 / width)
    along = jnp.sum(scaled * normed, axis=1, keepdims=True) * (1.0 / width)
    return inverse * (scaled - mean - normed * along)


def gelu_and_slope(value):
    square = value * value
    inner = value * (SQRT_2_OVER_PI + (SQRT_2_OVER_PI * 0.044715) * square)
    half = 0.5 + 0.5 * jnp.tanh(inner)
    rise = value * (2.0 * SQRT_2_OVER_PI + (6.0 * SQRT_2_OVER_PI * 0.044715) * square)
    return value * half, half * (1.0 + (1.0 - half) * rise)


def middle_kernel(
    att, post, pre, post_cot, pre_cot, own, far_line, far_side, out_bias_ref, gain1_ref, shift1_ref, down_bias_ref, gain2_ref, shift2_ref, up_bias_ref,
    post_out, pre_out, sum1_out, att_grad_out, keep_out, to_across_out, to_beside_out, to_corner_out, small_out,
    post_b, pre_b, post_cot_b, pre_cot_b, att_in, w_all, w_out, up_bias, up_bias_all,
    mid_low, hidden, act_grad, ffn_grad, branch_grad, att_grad_b, slope_b,
    post_out_b, pre_out_b, sum1_b, send_b, recv_b, keep_b, give_b, beside_b,
    in_sem, own_sem, weight_sem, send_w, recv_w, send_p, recv_p,
    send_a, recv_a, send_g, recv_g, send_r, recv_r, out_sem,
):
    me, sib, across, diagonal = mp_peers()
    dp = lax.axis_index("dp")
    rows, width = post.shape
    chunk = TILE
    count = rows // chunk
    local = att.shape[1]
    tall = own.shape[0]
    hid = tall - width - local
    up_rows, down_rows = pl.ds(0, width), pl.ds(width, hid)
    spans = (pl.ds(0, width), pl.ds(width, hid), pl.ds(width + hid, local))
    peers = (sib, across, diagonal)

    def stream(c):
        here = pl.ds(c * chunk, chunk)
        return [
            pltpu.make_async_copy(src.at[here], dst.at[here], in_sem.at[c, n])
            for n, (src, dst) in enumerate(
                ((post, post_b), (pre, pre_b), (post_cot, post_cot_b), (pre_cot, pre_cot_b))
            )
        ]

    def own_attended():
        return pltpu.make_async_copy(
            att.at[ds(me * rows, rows)], att_in.at[:, ds(me * local, local)], own_sem.at[0]
        )

    half = tall // 2
    line_at = ds16((dp % 2) * half, half)
    side_at = ds16((1 - dp % 2) * half, half)
    weight_parts = (
        (own, w_all.at[me]), (far_line, w_all.at[across, line_at]), (far_side, w_all.at[across, side_at])
    )

    def local_weights():
        return [pltpu.make_async_copy(src, dst, weight_sem.at[n]) for n, (src, dst) in enumerate(weight_parts)]

    def sent_weights():
        return [
            remote(src, dst, send_w.at[n], recv_w.at[n], (dp, sib)) for n, (src, dst) in enumerate(weight_parts)
        ]

    def arriving_weights():
        places = (w_all.at[sib], w_all.at[diagonal, line_at], w_all.at[diagonal, side_at])
        return [pltpu.make_async_copy(p, p, recv_w.at[n]) for n, p in enumerate(places)]

    def sent_prm(n):
        return remote(up_bias, up_bias_all.at[me], send_p.at[n], recv_p.at[n], (dp, peers[n]))

    def sent_attended(n, c):
        peer = peers[n]
        return remote(
            att.at[ds(peer * rows + c * chunk, chunk)],
            att_in.at[ds(c * chunk, chunk), ds(me * local, local)],
            send_a.at[n, c],
            recv_a.at[n, c],
            (dp, peer),
        )

    def arriving_attended(n, c):
        place = att_in.at[ds(c * chunk, chunk), ds(peers[n] * local, local)]
        return pltpu.make_async_copy(place, place, recv_a.at[n, c])

    def sent_grad(n, c):
        peer = peers[n]
        return remote(
            att_grad_b.at[ds(c * chunk, chunk), ds(peer * local, local)],
            att_grad_out.at[ds(me * rows + c * chunk, chunk)],
            send_g.at[n, c],
            recv_g.at[n, c],
            (dp, peer),
        )

    def arriving_grad(n, c):
        place = att_grad_out.at[ds(peers[n] * rows + c * chunk, chunk)]
        return pltpu.make_async_copy(place, place, recv_g.at[n, c])

    def own_grad(c):
        return pltpu.make_async_copy(
            att_grad_b.at[ds(c * chunk, chunk), ds(me * local, local)],
            att_grad_out.at[ds(me * rows + c * chunk, chunk)],
            out_sem.at[c, 3],
        )

    def stored(c):
        here = ds(c * chunk, chunk)
        return [
            pltpu.make_async_copy(src.at[here], dst.at[here], out_sem.at[c, n])
            for n, (src, dst) in enumerate(((post_out_b, post_out), (pre_out_b, pre_out), (sum1_b, sum1_out)))
        ]

    for copy in stream(0) + [own_attended()] + local_weights():
        copy.start()
    up_bias[...] = jnp.broadcast_to(as_row(up_bias_ref), up_bias.shape)
    greet([(dp, peer) for peer in peers])
    for n in range(3):
        sent_prm(n).start()
    for c in range(count):
        for n in (2, 1, 0):
            sent_attended(n, c).start()
    for copy in sent_weights():
        copy.start()
    for c in range(1, count):
        for copy in stream(c):
            copy.start()
    up_bias_all[ds(me, 1)] = up_bias[...][None]
    small_out[...] = jnp.zeros_like(small_out)
    own_attended().wait()
    for n in range(3):
        arrived = up_bias_all.at[peers[n]]
        pltpu.make_async_copy(arrived, arrived, recv_p.at[n]).wait()
    for copy in local_weights() + arriving_weights():
        copy.wait()
    for f in range(MP):
        w_out[pl.ds(f * local, local)] = w_all[f, pl.ds(width + hid, local)]

    out_bias, gain1, shift1 = as_row(out_bias_ref), as_row(gain1_ref), as_row(shift1_ref)
    down_bias, gain2, shift2 = as_row(down_bias_ref), as_row(gain2_ref), as_row(shift2_ref)

    def block_step(c, _):
        here = ds(c * chunk, chunk)
        for n in range(3):
            arriving_attended(n, c).wait()
        for n in range(4):
            pltpu.make_async_copy(post_b.at[here], post_b.at[here], in_sem.at[c, n]).wait()
        branch = dot(att_in[here], w_out[...]) + out_bias
        normed1, inverse1 = center_and_scale(post_b[here] + branch)
        mid = normed1 * gain1 + shift1
        pre_mid = pre_b[here] + branch
        low = mid.astype(BF16)
        mid_low[here] = low
        ffn = jnp.zeros((chunk, width), F32)
        for f in range(MP):
            pre_act = dot(low, w_all[f, up_rows]) + up_bias_all[f, 0:1]
            value, slope = gelu_and_slope(pre_act)
            value = value.astype(BF16)
            hidden[f, here] = value
            slope_b[f] = slope
            ffn = ffn + dot(value, w_all[f, down_rows])
        ffn = ffn + down_bias
        normed2, inverse2 = center_and_scale(mid + ffn)
        post_out_b[here] = normed2 * gain2 + shift2
        pre_out_b[here] = pre_mid + ffn
        cot = post_cot_b[here]
        small_out[4:5] += column_sum(cot * normed2)
        small_out[5:6] += column_sum(cot)
        sum2_grad = norm_backward(cot, normed2, inverse2, gain2)
        grad = (sum2_grad + pre_cot_b[here]).astype(BF16)
        ffn_grad[here] = grad
        small_out[3:4] += column_sum(grad.astype(F32))
        mid_grad = sum2_grad
        for f in range(MP):
            back = (dot(grad, w_all[f, down_rows], NT) * slope_b[f]).astype(BF16)
            act_grad[f, here] = back
            small_out[8 + f : 9 + f] += column_sum(back.astype(F32))
            mid_grad = mid_grad + dot(back, w_all[f, up_rows], NT)
        small_out[1:2] += column_sum(mid_grad * normed1)
        small_out[2:3] += column_sum(mid_grad)
        sum1 = norm_backward(mid_grad, normed1, inverse1, gain1)
        sum1_b[here] = sum1
        grad1 = (sum1 + pre_cot_b[here]).astype(BF16)
        branch_grad[here] = grad1
        small_out[0:1] += column_sum(grad1.astype(F32))
        att_grad_b[here] = dot(grad1, w_out[...], NT).astype(BF16)
        for n in (2, 1, 0):
            sent_grad(n, c).start()
        own_grad(c).start()
        for copy in stored(c):
            copy.start()
        return 0

    lax.fori_loop(0, count, block_step, 0)

    def weight_grads(s):
        up = dot(mid_low[...], act_grad[s], TN)
        down = dot(hidden[s], ffn_grad[...], TN)
        out = dot(att_in[:, ds(s * local, local)], branch_grad[...], TN)
        return up, down, out

    def sent_sums(n):
        return remote(send_b.at[n], recv_b.at[n], send_r.at[n], recv_r.at[n], (dp, sib))

    for n, owner in enumerate((diagonal, sib)):
        for span, part in zip(spans, weight_grads(owner)):
            send_b[n, span] = part.astype(BF16)
        sent_sums(n).start()
    for span, part in zip(spans, weight_grads(across)):
        keep_b[span] = part
    sent_sums(0).wait_recv()
    ours = ds((dp % 2) * (width // 2), width // 2)
    theirs = ds((1 - dp % 2) * (width // 2), width // 2)
    give_b[...] = (keep_b[...] + recv_b[0].astype(F32)).astype(BF16)
    gives = [
        pltpu.make_async_copy(give_b.at[:, ours], to_across_out, own_sem.at[1]),
        pltpu.make_async_copy(give_b.at[:, theirs], to_corner_out, own_sem.at[2]),
    ]
    for give in gives:
        give.start()
    for span, part in zip(spans, weight_grads(me)):
        keep_b[span] = part
    sent_sums(1).wait_recv()
    keep_b[...] = keep_b[...] + recv_b[1].astype(F32)
    beside_b[...] = keep_b[:, theirs].astype(BF16)
    gives += [
        pltpu.make_async_copy(keep_b.at[:, ours], keep_out, own_sem.at[3]),
        pltpu.make_async_copy(beside_b, to_beside_out, own_sem.at[4]),
    ]
    for give in gives[2:]:
        give.start()
    for c in range(count):
        for copy in stored(c) + [own_grad(c)]:
            copy.wait()
        for n in range(3):
            sent_attended(n, c).wait_send()
            sent_grad(n, c).wait_send()
            arriving_grad(n, c).wait()
    for copy in sent_weights():
        copy.wait_send()
    for n in range(3):
        sent_prm(n).wait_send()
    for n in range(2):
        sent_sums(n).wait_send()
    for give in gives:
        give.wait()


def middle(att, post, pre, post_cot, pre_cot, own, far_line, far_side, vectors):
    rows, width = post.shape
    local = att.shape[1]
    tall = own.shape[0]
    hid = tall - width - local
    count = rows // TILE
    f32 = jax.ShapeDtypeStruct((rows, width), F32)
    return pl.pallas_call(
        middle_kernel,
        out_shape=(
            f32, f32, f32,
            jax.ShapeDtypeStruct(att.shape, BF16),
            jax.ShapeDtypeStruct((tall, width // 2), F32),
            jax.ShapeDtypeStruct((tall, width // 2), BF16),
            jax.ShapeDtypeStruct((tall, width // 2), BF16),
            jax.ShapeDtypeStruct((tall, width // 2), BF16),
            jax.ShapeDtypeStruct((16, width), F32),
        ),
        in_specs=[ANY] * 8 + [VMEM] * len(vectors),
        out_specs=(ANY,) * 8 + (VMEM,),
        scratch_shapes=[
            pltpu.VMEM((rows, width), F32),
            pltpu.VMEM((rows, width), F32),
            pltpu.VMEM((rows, width), F32),
            pltpu.VMEM((rows, width), F32),
            pltpu.VMEM((rows, MP * local), BF16),
            pltpu.VMEM((MP, tall, width), BF16),
            pltpu.VMEM((MP * local, width), BF16),
            pltpu.VMEM((8, hid), F32),
            pltpu.VMEM((MP, 8, hid), F32),
            pltpu.VMEM((rows, width), BF16),
            pltpu.VMEM((MP, rows, hid), BF16),
            pltpu.VMEM((MP, rows, hid), BF16),
            pltpu.VMEM((rows, width), BF16),
            pltpu.VMEM((rows, width), BF16),
            pltpu.VMEM((rows, MP * local), BF16),
            pltpu.VMEM((MP, TILE, hid), F32),
            pltpu.VMEM((rows, width), F32),
            pltpu.VMEM((rows, width), F32),
            pltpu.VMEM((rows, width), F32),
            pltpu.VMEM((2, tall, width), BF16),
            pltpu.VMEM((2, tall, width), BF16),
            pltpu.VMEM((tall, width), F32),
            pltpu.VMEM((tall, width), BF16),
            pltpu.VMEM((tall, width // 2), BF16),
            dma_sems(count, 4), dma_sems(5), dma_sems(3), dma_sems(3), dma_sems(3),
            dma_sems(3), dma_sems(3), dma_sems(3, count), dma_sems(3, count),
            dma_sems(3, count), dma_sems(3, count), dma_sems(2), dma_sems(2), dma_sems(count, 4),
        ],
        compiler_params=pltpu.CompilerParams(
            collective_id=1, has_side_effects=True, vmem_limit_bytes=60 << 20
        ),
        cost_estimate=pl.CostEstimate(flops=15 << 30, bytes_accessed=20 << 20, transcendentals=4 << 20),
        name="middle",
    )(att, post, pre, post_cot, pre_cot, own, far_line, far_side, *vectors)


ROW_TIME = 0.0105
HOP_TIME = 2.8
HALF = 256


def sum_plan(dp_size, width, hid, local):
    bits = dp_size.bit_length() - 1
    rest = tuple((b,) for b in range(3, bits))

    def order(*groups):
        groups = tuple(tuple(b for b in group if b < bits) for group in groups)
        return tuple(group for group in groups if group) + rest

    below = hid + local
    rows = [
        (width // 2, order((0,), *PLANS[0]), 1.5, 1), (width // 2, order((0,), *PLANS[1]), 1.6, 1),
        (below // 2, order((0,), *PLANS[2]), 1.7, 1), (below // 2, order((0,), *PLANS[3]), 1.8, 1),
        (width // 2, order(*PLANS[4]), 3.2, 0), (width // 2, order(*PLANS[5]), 3.3, 0),
        (width // 2, order(*PLANS[6]), 3.4, 0),
    ]
    pieces, start = [], 0
    for size, groups, ready, done in rows:
        steps = []
        remaining = size
        for n, group in enumerate(groups):
            ways = 1 << len(group)
            if n < done:
                steps.append((group, ways * size, True))
            elif remaining % (16 * ways) == 0:
                steps.append((group, remaining, True))
                remaining //= ways
            else:
                steps += [((b,), remaining, False) for b in group]
        pieces.append((start, size, ready, steps, done))
        start += size
        if start == width + below:
            start *= 2
    return pieces, start


NEAR, SWAP, FAR = ((0,), (1,), (2,)), ((1,), (0,), (2,)), ((2,), (0,), (1,))
PAIR, ALL = ((0,), (1, 2)), ((0, 1, 2),)
LINE, BACK = ((1,), (2,)), ((2,), (1,))
BOTH = ((1, 2),)
PLANS = (BACK, LINE, BOTH, LINE, NEAR, NEAR, NEAR)
POST_TIME = (34.0, 34.1, 34.2, 38.0)
SMALL_TIME = (0.0, 2.0, 90.0)


def plan_length(steps):
    return len(steps) + sum(split for _, _, split in steps)


def step_times(pieces):
    free = {}
    waiting = [(piece[2], n, piece[4]) for n, piece in enumerate(pieces)]
    times = []
    while waiting:
        now, n, t = min(waiting)
        waiting.remove((now, n, t))
        times.append((now, n, t))
        steps = pieces[n][3]
        if t == plan_length(steps):
            continue
        back = [s for s in reversed(steps) if s[2]]
        group, size, split = steps[t] if t < len(steps) else back[t - len(steps)]
        begin = max([now] + [free.get(b, 0.0) for b in group])
        end = begin
        for b in group:
            cost = size * ROW_TIME * (0.5 if split else 1.0) * (1.0 if b == 0 else 1.5 if len(group) > 1 else b)
            free[b] = begin + cost
            end = max(end, free[b])
        waiting.append((end + HOP_TIME, n, t + 1))
    return times


def flipped(place, mask, bits):
    for b in range(bits):
        if mask >> b & 1:
            place = place + (1 << b) - 2 * (1 << b) * ((place // (1 << b)) % 2)
    return place


def tail_kernel(
    dp_size,
    dq, dk, dv, tok_t, w, sum1, keep, given0, given1, given2, small,
    post_out, full_out, small_out,
    grads, tok_b, w_t, sum1_b, keep_b, given_b, mine, far, send_far, recv_far, pass_far, land_far, send_near, recv_near,
    acc, flight, full, land, small_flight, small_land,
    in_sem, grad_sem, near_send, near_recv, far_send, far_recv, hop_send, hop_recv,
    step_send, step_recv, small_send, small_recv, out_sem, full_sem,
):
    me, sib, across, diagonal = mp_peers()
    dp = lax.axis_index("dp")
    rows, width = sum1.shape
    local = dq.shape[1]
    chunk = TILE
    count = rows // chunk
    tall = keep.shape[0]
    hid = tall - width - local
    bits = dp_size.bit_length() - 1
    pieces, total = sum_plan(dp_size, width, hid, local)

    loads = [
        pltpu.make_async_copy(keep, keep_b, in_sem.at[0]),
        pltpu.make_async_copy(given0, given_b.at[0], in_sem.at[1]),
        pltpu.make_async_copy(given1, given_b.at[1], in_sem.at[2]),
        pltpu.make_async_copy(given2, given_b.at[2], in_sem.at[5]),
        pltpu.make_async_copy(tok_t, tok_b, in_sem.at[3]),
        pltpu.make_async_copy(sum1, sum1_b, in_sem.at[4]),
    ]

    def grad_loads(g, owner):
        here = ds(owner * rows, rows)
        return [
            pltpu.make_async_copy(src.at[here], grads.at[here, pl.ds(n * local, local)], grad_sem.at[g, n])
            for n, src in enumerate((dq, dk, dv))
        ]

    owners = (diagonal, across, sib, me)
    for load in grad_loads(0, diagonal) + loads[:4] + grad_loads(1, across):
        load.start()
    for load in grad_loads(2, sib) + grad_loads(3, me) + loads[4:]:
        load.start()
    for n in range(3):
        w_t[pl.ds(n * local, local)] = w[n].T
    greet([(dp, sib), (dp, across), (dp, diagonal)] + [(flipped(dp, mask, bits), me) for mask in partner_masks(pieces, bits)])

    spots = {}
    ids = {}
    for n, (base, _, _, steps, done) in enumerate(pieces):
        base = jnp.int32(base)
        for t, (group, size, split) in enumerate(steps):
            ways = 1 << len(group)
            part = size // ways if split else size
            places = []
            for m in range(ways):
                mask = sum(1 << b for k, b in enumerate(group) if m >> k & 1)
                there = flipped(dp, mask, bits)
                rank = sum((there // (1 << b)) % 2 * (1 << k) for k, b in enumerate(group))
                places.append((there, base + rank * (tall if t < done else part) if split else base))
                ids[n, t, m] = len(ids)
            spots[n, t] = (places, part)
            base = places[0][1]

    def reduce_copy(n, t, m):
        places, part = spots[n, t]
        there, at = places[m]
        own = places[0][1]
        return remote(
            flight.at[ds16(at, part)], land.at[t, ds16(own, part)],
            step_send.at[0, ids[n, t, m]], step_recv.at[0, ids[n, t, m]], (there, me),
        )

    def reduce_start(n, t):
        places, part = spots[n, t]
        for m in range(1, len(places)):
            here = ds16(places[m][1], part)
            flight[here] = acc[here].astype(BF16)
            reduce_copy(n, t, m).start()

    def reduce_finish(n, t):
        places, part = spots[n, t]
        split = pieces[n][3][t][2]
        own = ds16(places[0][1], part)
        if split:
            value = acc[own]
        else:
            value = flight[own].astype(F32)
        for m in range(1, len(places)):
            there = ds16(places[m][1], part)
            pltpu.make_async_copy(land.at[t, there], land.at[t, there], step_recv.at[0, ids[n, t, m]]).wait()
            value = value + land[t, there].astype(F32)
        acc[own] = value
        for m in range(1, len(places)):
            reduce_copy(n, t, m).wait_send()

    def spread_copy(n, t, m):
        places, part = spots[n, t]
        own = ds16(places[0][1], part)
        return remote(
            full.at[own], full.at[own],
            step_send.at[1, ids[n, t, m]], step_recv.at[1, ids[n, t, m]], (places[m][0], me),
        )

    def spread_start(n, t):
        for m in range(1, len(spots[n, t][0])):
            spread_copy(n, t, m).start()

    def spread_done(n, t):
        places, part = spots[n, t]
        for m in range(1, len(places)):
            there = ds16(places[m][1], part)
            pltpu.make_async_copy(full.at[there], full.at[there], step_recv.at[1, ids[n, t, m]]).wait()
            spread_copy(n, t, m).wait_send()

    def full_copies(n):
        starts = [pieces[n][0] + s * tall for s in range(1 + pieces[n][4])]
        return [
            pltpu.make_async_copy(full.at[pl.ds(start, pieces[n][1])], full_out.at[pl.ds(start, pieces[n][1])], full_sem.at[n, s])
            for s, start in enumerate(starts)
        ]

    def stage(n, t):
        steps = pieces[n][3]
        back = [s for s in range(len(steps) - 1, -1, -1) if steps[s][2]]
        if pieces[n][4] < t <= len(steps):
            reduce_finish(n, t - 1)
        if t < len(steps):
            reduce_start(n, t)
            return
        if t == len(steps):
            places, part = spots[n, len(steps) - 1]
            here = ds16(places[0][1], part)
            full[here] = acc[here].astype(BF16)
        else:
            spread_done(n, back[t - len(steps) - 1])
        if t < plan_length(steps):
            spread_start(n, back[t - len(steps)])
        else:
            for copy in full_copies(n):
                copy.start()

    phases = [[(dp, peer) for peer in (sib, across, diagonal)]]
    for low in range(0, bits, 3):
        high = min(low + 3, bits)
        phases.append([(flipped(dp, mask << low, bits), me) for mask in range(1, 1 << (high - low))])

    def small_copy(s, n):
        return remote(small_flight.at[s], small_land.at[s, n], small_send.at[s, n], small_recv.at[s, n], phases[s][n])

    def ranked(own, arrived, place, ways):
        values = [own] + arrived
        total = None
        for rank in range(ways):
            value = values[0]
            for n in range(1, ways):
                value = jnp.where((place ^ n) == rank, values[n], value)
            total = value if total is None else total + value
        return total

    def small_stage(s):
        if s == 0:
            small_out[...] = small[...]
        else:
            for n in range(len(phases[s - 1])):
                small_copy(s - 1, n).wait()
            arrived = [small_land[s - 1, n] for n in range(len(phases[s - 1]))]
            place = me if s == 1 else (dp // (1 << (3 * (s - 2)))) % 8
            small_out[...] = ranked(small_out[...], arrived, place, len(arrived) + 1)
        if s == 1:
            sums = column_sum(grads[...].astype(F32))
            small_out[12:13] = jnp.concatenate(
                [sums[:, :local], sums[:, 2 * local :], jnp.zeros((1, width - 2 * local), F32)], axis=1
            )
        if s < len(phases):
            small_flight[s] = small_out[...]
            for n in range(len(phases[s])):
                small_copy(s, n).start()

    def far_copy(c):
        return remote(send_far.at[c], recv_far.at[c], far_send.at[c], far_recv.at[c], (dp, sib))

    def hop_copy(c):
        return remote(pass_far.at[c], land_far.at[c], hop_send.at[c], hop_recv.at[c], (dp, across))

    def near_copy(c):
        return remote(send_near.at[c], recv_near.at[c], near_send.at[c], near_recv.at[c], (dp, sib))

    def post_copy(c):
        here = pl.ds(c * chunk, chunk)
        return pltpu.make_async_copy(sum1_b.at[here], post_out.at[here], out_sem.at[c])

    def arrive(g):
        for load in grad_loads(g, owners[g]):
            load.wait()

    def part(g):
        if g < 2:
            arrive(g)
        return dot(grads[ds(owners[g] * rows, rows)], w_t[...]).reshape(count, chunk, width)

    def far_step(n):
        if n == 0:
            send_far[...] = part(0).astype(BF16)
            for c in range(count):
                far_copy(c).start()
        else:
            far[...] = part(1)

    def hop_step(c):
        far_copy(c).wait_recv()
        pass_far[c] = (far[c] + recv_far[c].astype(F32)).astype(BF16)
        hop_copy(c).start()

    def near_step(_):
        send_near[...] = part(2).astype(BF16)
        for c in range(count):
            near_copy(c).start()
        mine[...] = part(3)

    def post_step(c):
        if c == 0:
            loads[5].wait()
        near_copy(c).wait_recv()
        hop_copy(c).wait_recv()
        here = pl.ds(c * chunk, chunk)
        sum1_b[here] = sum1_b[here] + (mine[c] + recv_near[c].astype(F32)) + land_far[c].astype(F32)
        post_copy(c).start()

    def own_sums(_):
        for load in loads[:4]:
            load.wait()
        total = keep_b[...]
        for n in range(3):
            total = total + given_b[n].astype(F32)
        acc[ds16((dp % 2) * tall, tall)] = total

    def weight_step(_):
        loads[4].wait()
        block = dot(tok_b[...], grads[...])
        base = 2 * tall
        acc[pl.ds(base, width)] = block[:, : 2 * local]
        for s in range(2):
            acc[pl.ds(base + width, width // 2), pl.ds(s * local, local)] = block[
                s * width // 2 : (s + 1) * width // 2, 2 * local :
            ]

    events = [(now, 5, stage, (n, t)) for now, n, t in step_times(pieces)]
    events += [
        (1.0, 0, far_step, (0,)), (1.1, 0, own_sums, (0,)), (2.0, 0, far_step, (1,)),
        (2.8, 0, arrive, (2,)), (2.8, 0, arrive, (3,)),
        (3.2, 0, weight_step, (0,)), (3.3, 0, near_step, (0,)),
    ]
    for c in range(count):
        events.append((2.1 + 0.3 * c, 1, hop_step, (c,)))
        events.append((POST_TIME[c], 7, post_step, (c,)))
    for s in range(len(phases) + 1):
        events.append((SMALL_TIME[min(s, 2)] + s, 4, small_stage, (s,)))
    for _, _, act, where in sorted(events, key=lambda event: event[:2] + (event[3],)):
        act(*where)

    for c in range(count):
        far_copy(c).wait_send()
        hop_copy(c).wait_send()
        near_copy(c).wait_send()
        post_copy(c).wait()
    for n in range(len(pieces)):
        for copy in full_copies(n):
            copy.wait()


def ds1(start):
    return pl.ds(start, 1)


def partner_masks(pieces, bits):
    masks = {mask << low for low in range(0, bits, 3) for mask in range(1, 1 << min(3, bits - low))}
    for _, _, _, steps, _ in pieces:
        for group, _, _ in steps:
            for m in range(1, 1 << len(group)):
                masks.add(sum(1 << b for k, b in enumerate(group) if m >> k & 1))
            masks.update(1 << b for b in group)
    return sorted(masks)


def tail(dp_size, dq, dk, dv, tok_t, w, sum1, keep, given, small):
    rows, width = sum1.shape
    group, local = dq.shape
    tall = keep.shape[0]
    hid = tall - width - local
    count = rows // TILE
    bits = dp_size.bit_length() - 1
    assert 1 << bits == dp_size and bits > 0
    pieces, total = sum_plan(dp_size, width, hid, local)
    blocks = (count, TILE, width)
    phases = 1 + (bits + 2) // 3
    longest = max(len(piece[3]) for piece in pieces)
    copies = sum(1 << len(step[0]) for piece in pieces for step in piece[3])
    return pl.pallas_call(
        functools.partial(tail_kernel, dp_size),
        out_shape=(
            jax.ShapeDtypeStruct((rows, width), F32),
            jax.ShapeDtypeStruct((total, HALF), BF16),
            jax.ShapeDtypeStruct(small.shape, F32),
        ),
        in_specs=[ANY] * 4 + [VMEM] + [ANY] * 5 + [VMEM],
        out_specs=(ANY, ANY, VMEM),
        scratch_shapes=[
            pltpu.VMEM((group, 3 * local), BF16),
            pltpu.VMEM((width, group), BF16),
            pltpu.VMEM((3 * local, width), BF16),
            pltpu.VMEM((rows, width), F32),
            pltpu.VMEM((tall, HALF), F32),
            pltpu.VMEM((3, tall, HALF), BF16),
            pltpu.VMEM(blocks, F32),
            pltpu.VMEM(blocks, F32),
            pltpu.VMEM(blocks, BF16),
            pltpu.VMEM(blocks, BF16),
            pltpu.VMEM(blocks, BF16),
            pltpu.VMEM(blocks, BF16),
            pltpu.VMEM(blocks, BF16),
            pltpu.VMEM(blocks, BF16),
            pltpu.VMEM((total, HALF), F32),
            pltpu.VMEM((total, HALF), BF16),
            pltpu.VMEM((total, HALF), BF16),
            pltpu.VMEM((longest, total, HALF), BF16),
            pltpu.VMEM((phases,) + small.shape, F32),
            pltpu.VMEM((phases, 7) + small.shape, F32),
            dma_sems(6), dma_sems(4, 3), dma_sems(count), dma_sems(count), dma_sems(count), dma_sems(count),
            dma_sems(count), dma_sems(count), dma_sems(2, copies), dma_sems(2, copies),
            dma_sems(phases, 7), dma_sems(phases, 7), dma_sems(count), dma_sems(len(pieces), 2),
        ],
        compiler_params=pltpu.CompilerParams(
            collective_id=2, has_side_effects=True, vmem_limit_bytes=60 << 20
        ),
        cost_estimate=pl.CostEstimate(flops=4 << 30, bytes_accessed=20 << 20, transcendentals=0),
        name="tail",
    )(dq, dk, dv, tok_t, w, sum1, keep, *given, small)


def finish_kernel(
    post_sum, full, small,
    post_grad, qkv_grad, up_grad, down_grad, out_grad,
    query_grad, value_grad, out_bias, gain1, shift1, up_bias, down_bias, gain2, shift2,
    post_b, full_b, grad_b, qkv_b, sem, post_sem, out_sem,
):
    me = lax.axis_index("mp")
    total, _ = full.shape
    rows, width = post_sum.shape
    local = query_grad.shape[0]
    hid = down_grad.shape[0]
    tall = width + hid + local
    count = 4

    def post_in(c):
        here = pl.ds(c * rows // count, rows // count)
        return pltpu.make_async_copy(post_sum.at[here], post_b.at[here], post_sem.at[0, c])

    def post_out(c):
        here = pl.ds(c * rows // count, rows // count)
        return pltpu.make_async_copy(post_b.at[here], post_grad.at[here], post_sem.at[1, c])

    spans = ((0, width, up_grad), (width, hid, down_grad), (width + hid, local, out_grad))

    def full_in(s, n):
        start, size = (s * tall + spans[n][0], spans[n][1]) if n < 3 else (2 * tall, total - 2 * tall)
        here = pl.ds(start, size)
        return pltpu.make_async_copy(full.at[here], full_b.at[here], sem.at[s, n])

    parts = [(s, n) for n in range(3) for s in range(2)] + [(0, 3)]
    for c in range(count):
        post_in(c).start()
    for s, n in parts:
        full_in(s, n).start()
    for row, vector in enumerate((out_bias, gain1, shift1, down_bias, gain2, shift2)):
        vector[...] = small[row]
    own = small[12:13]
    query_grad[...] = own[0, :local]
    value_grad[...] = own[0, local : 2 * local]
    up_bias[...] = small[pl.ds(8 + me, 1), :][0]
    stores = []
    for c in range(count):
        post_in(c).wait()
        stores.append(post_out(c))
        stores[-1].start()
    for n, (start, size, dst) in enumerate(spans):
        for s in range(2):
            full_in(s, n).wait()
            grad_b[pl.ds(start, size), pl.ds(s * HALF, HALF)] = full_b[pl.ds(s * tall + start, size)].astype(F32)
        stores.append(pltpu.make_async_copy(grad_b.at[pl.ds(start, size)], dst, out_sem.at[n]))
        stores[-1].start()
    full_in(0, 3).wait()
    for m in range(2):
        qkv_b[m] = full_b[pl.ds(2 * tall, width), pl.ds(m * local, local)].astype(F32)
    for s in range(2):
        qkv_b[2, pl.ds(s * width // 2, width // 2)] = full_b[
            pl.ds(2 * tall + width, width // 2), pl.ds(s * local, local)
        ].astype(F32)
    stores.append(pltpu.make_async_copy(qkv_b, qkv_grad, out_sem.at[3]))
    stores[-1].start()
    for store in stores:
        store.wait()


def finish(post_sum, full, small, hid, local):
    rows, width = post_sum.shape
    total = full.shape[0]
    tall = width + hid + local
    vector = lambda size: jax.ShapeDtypeStruct((size,), F32)
    return pl.pallas_call(
        finish_kernel,
        out_shape=(
            jax.ShapeDtypeStruct((rows, width), F32),
            jax.ShapeDtypeStruct((3, width, local), F32),
            jax.ShapeDtypeStruct((width, hid), F32),
            jax.ShapeDtypeStruct((hid, width), F32),
            jax.ShapeDtypeStruct((local, width), F32),
            vector(local), vector(local), vector(width), vector(width), vector(width),
            vector(hid), vector(width), vector(width), vector(width),
        ),
        in_specs=[ANY, ANY, VMEM],
        out_specs=(ANY,) * 5 + (VMEM,) * 9,
        scratch_shapes=[
            pltpu.VMEM((rows, width), F32),
            pltpu.VMEM((total, HALF), BF16),
            pltpu.VMEM((tall, width), F32),
            pltpu.VMEM((3, width, local), F32),
            dma_sems(2, 4), dma_sems(2, 4), dma_sems(4),
        ],
        compiler_params=pltpu.CompilerParams(vmem_limit_bytes=60 << 20),
        name="results",
    )(post_sum, full, small)


def body(
    dp_size,
    post_stream,
    pre_stream,
    seq_lengths,
    qkv_weight,
    query_bias,
    value_bias,
    out_weight,
    out_bias,
    norm1_gain,
    norm1_shift,
    up_weight,
    up_bias,
    down_weight,
    down_bias,
    norm2_gain,
    norm2_shift,
    post_cotan,
    pre_cotan,
):
    local = out_weight.shape[0]
    hid = down_weight.shape[0]
    qkv3 = jnp.transpose(qkv_weight, (1, 0, 2))
    tok_t, queries, k, v, kt, vt, starts, limits, own, far_line = gather_and_project(
        dp_size, seq_lengths, post_stream, qkv3, query_bias, value_bias, (up_weight, down_weight, out_weight)
    )
    across = [(m, (m + 2) % MP) for m in range(MP)]
    beside = [(d, d + 1 - 2 * (d % 2)) for d in range(dp_size)]
    corner = [(d * MP + m, e * MP + n) for d, e in beside for m, n in across]
    far_side = lax.ppermute(far_line, "dp", beside)
    att, lse, tiles, counts = attend(limits, starts, queries, k, vt)
    vectors = (out_bias, norm1_gain, norm1_shift, down_bias, norm2_gain, norm2_shift, up_bias)
    post_mid, pre_mid, sum1, att_grad, keep, to_across, to_beside, to_corner, small = middle(
        att, post_stream, pre_stream, post_cotan, pre_cotan, own, far_line, far_side, vectors
    )
    given = (
        lax.ppermute(to_across, "mp", across),
        lax.ppermute(to_beside, "dp", beside),
        lax.ppermute(to_corner, ("dp", "mp"), corner),
    )
    dq, dk, dv, post_out, pre_out = attend_back(
        tiles, counts, starts, lse, queries, k, v, kt, att, att_grad, post_mid, pre_mid
    )
    post_sum, full, small = tail(dp_size, dq, dk, dv, tok_t, qkv3, sum1, keep, given, small)
    (
        post_grad, qkv_grad, up_grad, down_grad, out_grad,
        query_grad, value_grad, out_bias_grad, gain1, shift1, up_bias_grad, down_bias_grad, gain2, shift2,
    ) = finish(post_sum, full, small, hid, local)
    return (
        post_out, pre_out, post_grad, jnp.transpose(qkv_grad, (1, 0, 2)), query_grad, value_grad, out_grad,
        out_bias_grad, gain1, shift1, up_grad, up_bias_grad, down_grad, down_bias_grad, gain2, shift2,
    )


def solution(mesh):
    tokens = P(("dp", "mp"), None)
    vector = P()
    return jax.shard_map(
        functools.partial(body, mesh.shape["dp"]),
        mesh=mesh,
        in_specs=(
            tokens, tokens, P("dp", None), P(None, None, "mp"), P("mp"), P("mp"), P("mp", None),
            vector, vector, vector, P(None, "mp"), P("mp"), P("mp", None), vector, vector, vector,
            tokens, tokens,
        ),
        out_specs=(
            tokens, tokens, tokens, P(None, None, "mp"), P("mp"), P("mp"), P("mp", None),
            vector, vector, vector, P(None, "mp"), P("mp"), P("mp", None), vector, vector, vector,
        ),
        check_vma=False,
    )
```

```python
import functools

import jax
import jax.numpy as jnp
from jax import lax
from jax.experimental import pallas as pl
from jax.experimental.pallas import tpu as pltpu
from jax.sharding import PartitionSpec as P

HEAD_DIM = 64
EPSILON = 1e-05
MASKED = -1e30
MP = 4
TILE = 256
MESH = pl.DeviceIdType.MESH
BF16 = jnp.bfloat16
F32 = jnp.float32
ANY = pl.BlockSpec(memory_space=pl.ANY)
VMEM = pl.BlockSpec(memory_space=pltpu.VMEM)
SMEM = pl.BlockSpec(memory_space=pltpu.SMEM)
NT = (((1,), (1,)), ((), ()))
TN = (((0,), (0,)), ((), ()))
SQRT_2_OVER_PI = 0.7978845608028654


def ds(start, size):
    return pl.ds(pl.multiple_of(start, size), size)


def mp_peers():
    me = lax.axis_index("mp")
    sib = me + 1 - 2 * (me % 2)
    across = (me + 2) % MP
    diagonal = (sib + 2) % MP
    return me, sib, across, diagonal


def greet(devices):
    barrier = pltpu.get_barrier_semaphore()
    for device in devices:
        pl.semaphore_signal(barrier, inc=1, device_id=device, device_id_type=MESH)
    pl.semaphore_wait(barrier, len(devices))


def ds16(start, size):
    return pl.ds(pl.multiple_of(start, 16), size)


def remote(src, dst, send_sem, recv_sem, device):
    return pltpu.make_async_remote_copy(
        src_ref=src,
        dst_ref=dst,
        send_sem=send_sem,
        recv_sem=recv_sem,
        device_id=device,
        device_id_type=MESH,
    )


def dot(a, b, dims=(((1,), (0,)), ((), ()))):
    return lax.dot_general(a, b, dims, preferred_element_type=F32)


def column_sum(block):
    return jnp.sum(block, axis=0, keepdims=True)


def as_row(vector):
    return vector[...].astype(F32).reshape(1, vector.shape[0])


def dma_sems(*shape):
    return pltpu.SemaphoreType.DMA(shape)


def first_of_segment(bounds, place):
    start = jnp.zeros_like(place)
    for bound in bounds:
        start = jnp.where(place >= bound, bound, start)
    return jnp.where(place >= bounds[-1], place, start)


def head_masked(block, h):
    lane = lax.broadcasted_iota(jnp.int32, block.shape, 1)
    return jnp.where((lane >= h * HEAD_DIM) & (lane < (h + 1) * HEAD_DIM), block, jnp.zeros_like(block))


def dp_slices(dp_size):
    return min(dp_size, 8)


def project_kernel(
    dp_size,
    lengths, post, w_any, query_bias_ref, value_bias_ref, up, down, out,
    tok_t_out, q_out, k_out, v_out, kt_out, vt_out, starts, limits, own_out, line_out,
    stage, w, own_b, line_b, tok, tok_t, q_s, k_s, v_s, kt_s, vt_s,
    w_sem, line_send, line_recv, in_sem, send_x, recv_x, send_c, recv_c, send_f, recv_f, out_sem,
):
    me, sib, across, diagonal = mp_peers()
    dp = lax.axis_index("dp")
    rows = post.shape[0]
    width = post.shape[1]
    chunk = TILE // 2
    count = rows // chunk
    heads = w.shape[2] // HEAD_DIM
    hid = up.shape[1]
    packs = []
    for n, (src, start) in enumerate(((up, 0), (down, width), (out, width + hid))):
        packs.append(pltpu.make_async_copy(src, own_b.at[pl.ds(start, src.shape[0])], w_sem.at[1 + n]))
    packed = pltpu.make_async_copy(own_b, own_out, w_sem.at[4])
    w_load = pltpu.make_async_copy(w_any, w, w_sem.at[0])
    loads = [
        pltpu.make_async_copy(post.at[pl.ds(c * chunk, chunk)], stage.at[pl.ds(c * chunk, chunk)], in_sem.at[c])
        for c in range(count)
    ]
    for load in loads + [w_load] + packs:
        load.start()
    slices = dp_slices(dp_size)
    line = slices // 2
    spot = (dp // 2) % line
    part = own_b.shape[0] // slices
    line_peers = []
    for mask in range(1, line):
        peer = dp
        for b in range(line.bit_length() - 1):
            if mask >> b & 1:
                peer = peer + (2 << b) - 2 * (2 << b) * ((dp // (2 << b)) % 2)
        line_peers.append(peer)
    greet([(dp, sib), (dp, across)] + [(peer, me) for peer in line_peers])

    def slice_over():
        return remote(
            own_b.at[ds16(((dp % 2) * line + spot) * part, part)], line_b.at[ds16(spot * part, part)],
            line_send.at[0], line_recv.at[0], (dp, across),
        )

    def slice_along(n):
        here = ds16(spot * part, part)
        return remote(line_b.at[here], line_b.at[here], line_send.at[1 + n], line_recv.at[1 + n], (line_peers[n], me))

    def slice_arrived(n):
        here = ds16(((line_peers[n] // 2) % line) * part, part)
        return pltpu.make_async_copy(line_b.at[here], line_b.at[here], line_recv.at[1 + n])

    def piece(owner, c):
        return ds(owner * rows + c * chunk, chunk)

    def to_across(c):
        here = piece(me, c)
        return remote(tok.at[here], tok.at[here], send_x.at[c], recv_x.at[c], (dp, across))

    def to_sibling(c):
        here = piece(me, c)
        return remote(tok.at[here], tok.at[here], send_c.at[c], recv_c.at[c], (dp, sib))

    def forward(c):
        here = piece(across, c)
        return remote(tok.at[here], tok.at[here], send_f.at[c], recv_f.at[c], (dp, sib))

    def arrived(owner, sem, c):
        here = piece(owner, c)
        return pltpu.make_async_copy(tok.at[here], tok.at[here], sem.at[c])

    for c in range(count):
        loads[c].wait()
        tok[piece(me, c)] = stage[pl.ds(c * chunk, chunk)].astype(BF16)
        to_across(c).start()
        to_sibling(c).start()
        if c == 0:
            for pack in packs:
                pack.wait()
            slice_over().start()
            packed.start()

    query_bias = as_row(query_bias_ref)
    value_bias = as_row(value_bias_ref)

    def project(owner, c):
        here = piece(owner, c)
        block = tok[here]
        tok_t[:, here] = block.T
        query = (dot(block, w[0]) + query_bias).astype(BF16)
        query = (query.astype(F32) * HEAD_DIM ** (-0.5)).astype(BF16)
        for h in range(heads):
            q_s[owner * (rows // TILE) + c // 2, ds(h * TILE + (c % 2) * chunk, chunk)] = head_masked(query, h)
        keys = dot(block, w[1]).astype(BF16)
        k_s[here] = keys
        kt_s[:, here] = keys.T
        values = (dot(block, w[2]) + value_bias).astype(BF16)
        v_s[here] = values
        vt_s[:, here] = values.T

    def outs(g, owner, c):
        here = ds(owner * rows + c * TILE, TILE)
        block = owner * (rows // TILE) + c
        return [
            pltpu.make_async_copy(tok_t.at[:, here], tok_t_out.at[:, here], out_sem.at[g, c, 0]),
            pltpu.make_async_copy(q_s.at[block], q_out.at[block], out_sem.at[g, c, 1]),
            pltpu.make_async_copy(k_s.at[here], k_out.at[here], out_sem.at[g, c, 2]),
            pltpu.make_async_copy(v_s.at[here], v_out.at[here], out_sem.at[g, c, 3]),
            pltpu.make_async_copy(kt_s.at[:, here], kt_out.at[:, here], out_sem.at[g, c, 4]),
            pltpu.make_async_copy(vt_s.at[:, here], vt_out.at[:, here], out_sem.at[g, c, 5]),
        ]

    w_load.wait()
    bounds = [lengths[0, 0]]
    for s in range(1, lengths.shape[1] - 1):
        bounds.append(bounds[-1] + lengths[0, s])
    for i in range(starts.shape[0]):
        place = i * TILE + lax.broadcasted_iota(jnp.int32, (1, starts.shape[2]), 1) % TILE
        starts[i] = jnp.broadcast_to(first_of_segment(bounds, place), starts.shape[1:])
        limits[0, i] = first_of_segment(bounds, jnp.int32(i * TILE)) // TILE
        last = first_of_segment(bounds, jnp.int32(i * TILE + TILE - 1))
        limits[1, i] = jnp.minimum((last + TILE - 1) // TILE, i)

    def own_step(c, _):
        project(me, 2 * c)
        project(me, 2 * c + 1)
        for copy in outs(0, me, c):
            copy.start()
        return 0

    lax.fori_loop(0, count // 2, own_step, 0)

    def sibling_step(c, _):
        for n in (0, 1):
            arrived(sib, recv_c, 2 * c + n).wait()
            project(sib, 2 * c + n)
        for copy in outs(1, sib, c):
            copy.start()
        return 0

    lax.fori_loop(0, count // 2, sibling_step, 0)

    def slices_on(_):
        slice_over().wait_recv()
        for n in range(len(line_peers)):
            slice_along(n).start()

    slices_on(0)

    def across_step(c, _):
        for n in (0, 1):
            arrived(across, recv_x, 2 * c + n).wait()
            forward(2 * c + n).start()
            project(across, 2 * c + n)
        for copy in outs(2, across, c):
            copy.start()
        for n in (0, 1):
            arrived(diagonal, recv_f, 2 * c + n).wait()
            project(diagonal, 2 * c + n)
        for copy in outs(3, diagonal, c):
            copy.start()
        return 0

    lax.fori_loop(0, count // 2, across_step, 0)
    for c in range(count):
        to_across(c).wait_send()
        to_sibling(c).wait_send()
        forward(c).wait_send()
    packed.wait()
    slice_over().wait_send()
    for n in range(len(line_peers)):
        slice_along(n).wait_send()
        slice_arrived(n).wait()
    line_copy = pltpu.make_async_copy(line_b, line_out, w_sem.at[5])
    line_copy.start()
    for g, owner in enumerate((me, sib, across, diagonal)):
        for c in range(count // 2):
            for copy in outs(g, owner, c):
                copy.wait()
    line_copy.wait()


def gather_and_project(dp_size, lengths, post_stream, qkv3, query_bias, value_bias, own):
    rows, width = post_stream.shape
    group = rows * MP
    local = qkv3.shape[2]
    count = 2 * rows // TILE
    tall = jax.ShapeDtypeStruct((group, local), BF16)
    wide = jax.ShapeDtypeStruct((local, group), BF16)
    blocks = group // TILE
    across = TILE * (local // HEAD_DIM)
    tall_rows = sum(part.shape[0] for part in own)
    line = dp_slices(dp_size) // 2
    return pl.pallas_call(
        functools.partial(project_kernel, dp_size),
        out_shape=(
            jax.ShapeDtypeStruct((width, group), BF16),
            jax.ShapeDtypeStruct((blocks, across, local), BF16),
            tall, tall, wide, wide,
            jax.ShapeDtypeStruct((blocks, 8, across), jnp.int32),
            jax.ShapeDtypeStruct((2, blocks), jnp.int32),
            jax.ShapeDtypeStruct((tall_rows, width), BF16),
            jax.ShapeDtypeStruct((tall_rows // 2, width), BF16),
        ),
        in_specs=[SMEM, ANY, ANY, VMEM, VMEM, ANY, ANY, ANY],
        out_specs=(ANY,) * 6 + (VMEM, SMEM, ANY, ANY),
        scratch_shapes=[
            pltpu.VMEM((rows, width), F32),
            pltpu.VMEM(qkv3.shape, BF16),
            pltpu.VMEM((tall_rows, width), BF16),
            pltpu.VMEM((tall_rows // 2, width), BF16),
            pltpu.VMEM((group, width), BF16),
            pltpu.VMEM((width, group), BF16),
            pltpu.VMEM((blocks, across, local), BF16),
            pltpu.VMEM((group, local), BF16),
            pltpu.VMEM((group, local), BF16),
            pltpu.VMEM((local, group), BF16),
            pltpu.VMEM((local, group), BF16),
            dma_sems(6), dma_sems(line), dma_sems(line), dma_sems(count), dma_sems(count), dma_sems(count), dma_sems(count),
            dma_sems(count), dma_sems(count), dma_sems(count), dma_sems(4, count // 2, 6),
        ],
        compiler_params=pltpu.CompilerParams(
            collective_id=0, has_side_effects=True, vmem_limit_bytes=60 << 20
        ),
        cost_estimate=pl.CostEstimate(flops=2 * group * width * 3 * local, bytes_accessed=12 << 20, transcendentals=0),
        name="gather_project",
    )(lengths, post_stream, qkv3, query_bias, value_bias, *own)


UNROLL = 8


def list_tiles(limits, tiles, counts, blocks):
    spare = jnp.int32(blocks * 65536)
    tiles[0] = spare
    tiles[1] = spare

    def put(code, first, last, at):
        def step(j, at):
            tiles[at] = code + j
            return at + 1

        return lax.fori_loop(first, last, step, at)

    def diagonal(i, at):
        tiles[at] = i * 65536 + i * 257
        return at + 1

    def edge_row(i, at):
        return put(i * 65536 + i * 256, limits[0, i], limits[1, i], at)

    def whole_row(i, at):
        return put(i * 65536 + i * 256, jnp.maximum(limits[0, i], limits[1, i]), i, at)

    at = jnp.int32(2)
    for kind, row in enumerate((diagonal, edge_row, whole_row)):
        at = lax.fori_loop(0, blocks, row, at)
        counts[kind] = (at - 2 + (1 if kind < 2 else 2) + UNROLL - 1) // UNROLL
    for u in range(2 * UNROLL + 2):
        tiles[at + u] = spare


def for_tiles(tiles, counts, heads, products, probabilities, sums):
    for kind in range(3):

        def step(n, _):
            codes = [tiles[n * UNROLL + u] for u in range(UNROLL + 2)]
            entries = [(code // 65536, (code // 256) % 256, code % 256) for code in codes]
            for u in range(UNROLL):
                for h in range(heads):
                    if products is not None:
                        products(u % 2, h, *entries[u + 2])
                    sums(u % 2, h, *entries[u])
                    probabilities((u + 1) % 2, h, kind, *entries[u + 1])
            return 0

        lax.fori_loop(counts[kind - 1] if kind else 0, counts[kind], step, 0)


def masked_score(score, kind, starts, i, j, lanes):
    if kind == 2:
        return score
    keys, queries = score.shape
    score = score.reshape(keys // 8, 8, queries)
    row = 8 * lax.broadcasted_iota(jnp.int32, score.shape, 0)
    key = lax.broadcasted_iota(jnp.int32, (8, queries), 0) + j * TILE
    allowed = (key - starts[i, :, lanes])[None] >= -row
    if kind == 0:
        query = lax.broadcasted_iota(jnp.int32, (8, queries), 1) + i * TILE
        allowed = allowed & ((key - query)[None] <= -row)
    return jnp.where(allowed, score, MASKED).reshape(keys, queries)


def tile_limit(blocks):
    return blocks * (blocks + 1) // 2 + 4 * UNROLL


def attend_kernel(
    limits, starts_ref, q_ref, k_ref, vt_ref, att_ref, lse_ref, tiles, counts,
    queries, k, vt, top, total, acc, scores, probs, alphas, att_b, sem, out_sem,
):
    blocks, wide, local = queries.shape
    heads = local // HEAD_DIM
    one = pl.ds(0, 1)
    loads = [
        pltpu.make_async_copy(src, dst, sem.at[n])
        for n, (src, dst) in enumerate(((q_ref, queries), (k_ref, k), (vt_ref, vt)))
    ]
    for load in loads:
        load.start()
    list_tiles(limits, tiles, counts, blocks)
    top[...] = jnp.full_like(top, MASKED)
    total[...] = jnp.zeros_like(total)
    acc[...] = jnp.zeros_like(acc)
    for load in loads:
        load.wait()

    def products(b, h, slot, i, j):
        lanes = pl.ds(h * TILE, TILE)
        scores[b, :, lanes] = dot(k[ds(j * TILE, TILE)], queries[i, lanes], NT)

    def probabilities(b, h, kind, slot, i, j):
        lanes = pl.ds(h * TILE, TILE)
        score = scores[b, :, lanes]
        score = masked_score(score, kind, starts_ref, i, j, lanes)
        old = top[slot, one, lanes]
        new = jnp.maximum(old, jnp.max(score, axis=0, keepdims=True))
        top[slot, one, lanes] = new
        alpha = jnp.exp(old - new)
        prob = jnp.exp(score - new)
        total[slot, one, lanes] = total[slot, one, lanes] * alpha + jnp.sum(prob, axis=0, keepdims=True)
        probs[b, :, lanes] = prob.astype(BF16)
        alphas[b, one, lanes] = alpha

    def sums(b, h, slot, i, j):
        lanes = pl.ds(h * TILE, TILE)
        values_t = vt[pl.ds(h * HEAD_DIM, HEAD_DIM), ds(j * TILE, TILE)]
        acc[slot, :, lanes] = acc[slot, :, lanes] * alphas[b, one, lanes] + dot(values_t, probs[b, :, lanes])

    for_tiles(tiles, counts, heads, products, probabilities, sums)

    def finish(i, _):
        lse_ref[i, one] = top[i, one] + jnp.log(total[i, one])
        out_t = acc[i] / total[i, one]
        here = ds(i * TILE, TILE)
        parts = [out_t[:, h * TILE : (h + 1) * TILE] for h in range(heads)]
        att_b[here] = jnp.concatenate(parts, axis=0).T.astype(BF16)
        pltpu.make_async_copy(att_b.at[here], att_ref.at[here], out_sem.at[i]).start()
        return 0

    lax.fori_loop(0, blocks, finish, 0, unroll=4)
    for i in range(blocks):
        here = pl.ds(i * TILE, TILE)
        pltpu.make_async_copy(att_b.at[here], att_ref.at[here], out_sem.at[i]).wait()


def attend(limits, starts, queries, k, vt):
    group, local = k.shape
    blocks, wide, _ = queries.shape
    return pl.pallas_call(
        attend_kernel,
        in_specs=[SMEM, VMEM, ANY, ANY, ANY],
        out_specs=[ANY, VMEM, SMEM, SMEM],
        out_shape=(
            jax.ShapeDtypeStruct((group, local), BF16),
            jax.ShapeDtypeStruct((blocks, 8, wide), F32),
            jax.ShapeDtypeStruct((tile_limit(blocks),), jnp.int32),
            jax.ShapeDtypeStruct((3,), jnp.int32),
        ),
        scratch_shapes=[
            pltpu.VMEM((blocks, wide, local), BF16),
            pltpu.VMEM((group, local), BF16),
            pltpu.VMEM((local, group), BF16),
            pltpu.VMEM((blocks + 1, 8, wide), F32),
            pltpu.VMEM((blocks + 1, 8, wide), F32),
            pltpu.VMEM((blocks + 1, HEAD_DIM, wide), F32),
            pltpu.VMEM((2, TILE, wide), F32),
            pltpu.VMEM((2, TILE, wide), BF16),
            pltpu.VMEM((2, 8, wide), F32),
            pltpu.VMEM((group, local), BF16),
            dma_sems(3), dma_sems(blocks),
        ],
        compiler_params=pltpu.CompilerParams(vmem_limit_bytes=60 << 20),
        cost_estimate=pl.CostEstimate(flops=12 << 30, bytes_accessed=4 << 20, transcendentals=8 << 20),
        name="attend",
    )(limits, starts, queries, k, vt)


def attend_back_kernel(
    tiles, counts, starts_ref, lse, q_ref, do_ref, o_ref, k_ref, v_ref, kt_ref, post_mid, pre_mid,
    dq_ref, dk_ref, dv_ref, post_out, pre_out,
    queries, do, o, k, v, kt, grads, delta, dq_acc, dk_acc, dv_acc,
    probs, score_grads, passed_b, out_b, sem, out_sem,
):
    blocks, wide, local = queries.shape
    heads = local // HEAD_DIM
    one = pl.ds(0, 1)
    loads = [
        pltpu.make_async_copy(src, dst, sem.at[n])
        for n, (src, dst) in enumerate(((do_ref, do), (o_ref, o), (q_ref, queries), (k_ref, k), (v_ref, v), (kt_ref, kt)))
    ]
    passed_in = [
        pltpu.make_async_copy(src, passed_b.at[n], sem.at[6 + n]) for n, src in enumerate((post_mid, pre_mid))
    ]
    passed_out = [
        pltpu.make_async_copy(passed_b.at[n], dst, sem.at[8 + n]) for n, dst in enumerate((post_out, pre_out))
    ]
    for load in loads + passed_in:
        load.start()
    dq_acc[...] = jnp.zeros_like(dq_acc)
    dk_acc[...] = jnp.zeros_like(dk_acc)
    dv_acc[...] = jnp.zeros_like(dv_acc)
    for load in loads[:2]:
        load.wait()

    def prepare(i, _):
        here = ds(i * TILE, TILE)
        block = do[here]
        for h in range(heads):
            grads[i, pl.ds(h * TILE, TILE)] = head_masked(block, h)
        along = (block.astype(F32) * o[here].astype(F32)).T
        parts = [column_sum(along[h * HEAD_DIM : (h + 1) * HEAD_DIM]) for h in range(heads)]
        delta[i, one] = jnp.concatenate(parts, axis=1)
        return 0

    lax.fori_loop(0, blocks, prepare, 0, unroll=4)
    for load in loads[2:]:
        load.wait()
    for copy_in, copy_out in zip(passed_in, passed_out):
        copy_in.wait()
        copy_out.start()

    def probabilities(b, h, kind, slot, i, j):
        lanes = pl.ds(h * TILE, TILE)
        here = ds(j * TILE, TILE)
        score = dot(k[here], queries[i, lanes], NT)
        score = masked_score(score, kind, starts_ref, i, j, lanes)
        rise = dot(v[here], grads[i, lanes], NT)
        prob = jnp.exp(score - lse[i, one, lanes])
        probs[b, :, lanes] = prob.astype(BF16)
        score_grads[b, :, lanes] = (prob * (rise - delta[i, one, lanes])).astype(BF16)

    def sums(b, h, slot, i, j):
        lanes = pl.ds(h * TILE, TILE)
        spot = ds(jnp.where(slot == blocks, blocks, j) * TILE, TILE)
        if h == 0:
            dv_acc[spot] += dot(probs[b], grads[i])
        else:
            dk_acc[spot] += dot(score_grads[b], queries[i])
        keys_t = kt[pl.ds(h * HEAD_DIM, HEAD_DIM), ds(j * TILE, TILE)]
        dq_acc[slot, :, lanes] += dot(keys_t, score_grads[b, :, lanes])

    for_tiles(tiles, counts, heads, None, probabilities, sums)

    outs = (dq_ref, dk_ref, dv_ref)

    def out_copy(n, i):
        here = ds(i * TILE, TILE)
        return pltpu.make_async_copy(out_b.at[n, here], outs[n].at[here], out_sem.at[n, i])

    def finish(i, _):
        here = ds(i * TILE, TILE)
        dq_t = dq_acc[i] * HEAD_DIM ** (-0.5)
        parts = [dq_t[:, h * TILE : (h + 1) * TILE] for h in range(heads)]
        out_b[0, here] = jnp.concatenate(parts, axis=0).T.astype(BF16)
        out_b[1, here] = dk_acc[here].astype(BF16)
        out_b[2, here] = dv_acc[here].astype(BF16)
        for n in range(3):
            out_copy(n, i).start()
        return 0

    lax.fori_loop(0, blocks, finish, 0, unroll=4)
    for i in range(blocks):
        for n in range(3):
            out_copy(n, i).wait()
    for copy in passed_out:
        copy.wait()


def attend_back(tiles, counts, starts, lse, queries, k, v, kt, att, att_grad, post_mid, pre_mid):
    group, local = k.shape
    blocks, wide, _ = queries.shape
    shape = jax.ShapeDtypeStruct((group, local), BF16)
    tall = pltpu.VMEM((group, local), BF16)
    return pl.pallas_call(
        attend_back_kernel,
        in_specs=[SMEM, SMEM, VMEM, VMEM] + [ANY] * 8,
        out_specs=[ANY] * 5,
        out_shape=(shape, shape, shape, jax.ShapeDtypeStruct(post_mid.shape, F32), jax.ShapeDtypeStruct(pre_mid.shape, F32)),
        scratch_shapes=[
            pltpu.VMEM((blocks, wide, local), BF16),
            tall, tall, tall, tall,
            pltpu.VMEM((local, group), BF16),
            pltpu.VMEM((blocks, wide, local), BF16),
            pltpu.VMEM((blocks, 8, wide), F32),
            pltpu.VMEM((blocks + 1, HEAD_DIM, wide), F32),
            pltpu.VMEM((group + TILE, local), F32),
            pltpu.VMEM((group + TILE, local), F32),
            pltpu.VMEM((2, TILE, wide), BF16),
            pltpu.VMEM((2, TILE, wide), BF16),
            pltpu.VMEM((2,) + post_mid.shape, F32),
            pltpu.VMEM((3, group, local), BF16),
            dma_sems(10), dma_sems(3, blocks),
        ],
        compiler_params=pltpu.CompilerParams(vmem_limit_bytes=60 << 20),
        cost_estimate=pl.CostEstimate(flops=30 << 30, bytes_accessed=9 << 20, transcendentals=8 << 20),
        name="attend_back",
    )(tiles, counts, starts, lse, queries, att_grad, att, k, v, kt, post_mid, pre_mid)


BLOCK_LAG = 30


def center_and_scale(summed):
    width = summed.shape[1]
    center = summed - jnp.sum(summed, axis=1, keepdims=True) * (1.0 / width)
    inverse = lax.rsqrt(jnp.sum(center * center, axis=1, keepdims=True) * (1.0 / width) + EPSILON)
    return center * inverse, inverse


def norm_backward(cotangent, normed, inverse, gain):
    width = normed.shape[1]
    scaled = cotangent * gain
    mean = jnp.sum(scaled, axis=1, keepdims=True) * (1.0 / width)
    along = jnp.sum(scaled * normed, axis=1, keepdims=True) * (1.0 / width)
    return inverse * (scaled - mean - normed * along)


def gelu_and_slope(value):
    square = value * value
    inner = value * (SQRT_2_OVER_PI + (SQRT_2_OVER_PI * 0.044715) * square)
    half = 0.5 + 0.5 * jnp.tanh(inner)
    rise = value * (2.0 * SQRT_2_OVER_PI + (6.0 * SQRT_2_OVER_PI * 0.044715) * square)
    return value * half, half * (1.0 + (1.0 - half) * rise)


def middle_kernel(
    att, post, pre, post_cot, pre_cot, own, far_line, far_side, out_bias_ref, gain1_ref, shift1_ref, down_bias_ref, gain2_ref, shift2_ref, up_bias_ref,
    post_out, pre_out, sum1_out, att_grad_out, keep_out, to_across_out, to_beside_out, to_corner_out, small_out,
    post_b, pre_b, post_cot_b, pre_cot_b, att_in, w_all, w_out, up_bias, up_bias_all,
    mid_low, hidden, act_grad, ffn_grad, branch_grad, att_grad_b, wide_b, rise_b,
    branch_b, normed_b, sum_b, send_b, recv_b, keep_b, give_b, beside_b,
    in_sem, own_sem, weight_sem, send_w, recv_w, send_p, recv_p,
    send_a, recv_a, send_g, recv_g, send_r, recv_r, out_sem,
):
    me, sib, across, diagonal = mp_peers()
    dp = lax.axis_index("dp")
    rows, width = post.shape
    chunk = TILE
    count = rows // chunk
    local = att.shape[1]
    tall = own.shape[0]
    hid = tall - width - local
    up_rows, down_rows = pl.ds(0, width), pl.ds(width, hid)
    spans = (pl.ds(0, width), pl.ds(width, hid), pl.ds(width + hid, local))
    peers = (sib, across, diagonal)

    def stream(c):
        here = ds(c * chunk, chunk)
        return [
            pltpu.make_async_copy(src.at[here], dst.at[here], in_sem.at[c, n])
            for n, (src, dst) in enumerate(
                ((post, post_b), (pre, pre_b), (post_cot, post_cot_b), (pre_cot, pre_cot_b))
            )
        ]

    def own_attended():
        return pltpu.make_async_copy(
            att.at[ds(me * rows, rows)], att_in.at[:, ds(me * local, local)], own_sem.at[0]
        )

    half = tall // 2
    line_at = ds16((dp % 2) * half, half)
    side_at = ds16((1 - dp % 2) * half, half)
    weight_parts = (
        (own, w_all.at[me]), (far_line, w_all.at[across, line_at]), (far_side, w_all.at[across, side_at])
    )

    def local_weights():
        return [pltpu.make_async_copy(src, dst, weight_sem.at[n]) for n, (src, dst) in enumerate(weight_parts)]

    def sent_weights():
        return [
            remote(src, dst, send_w.at[n], recv_w.at[n], (dp, sib)) for n, (src, dst) in enumerate(weight_parts)
        ]

    def arriving_weights():
        places = (w_all.at[sib], w_all.at[diagonal, line_at], w_all.at[diagonal, side_at])
        return [pltpu.make_async_copy(p, p, recv_w.at[n]) for n, p in enumerate(places)]

    def sent_prm(n):
        return remote(up_bias, up_bias_all.at[me], send_p.at[n], recv_p.at[n], (dp, peers[n]))

    def sent_attended(n, c):
        peer = peers[n]
        return remote(
            att.at[ds(peer * rows + c * chunk, chunk)],
            att_in.at[ds(c * chunk, chunk), ds(me * local, local)],
            send_a.at[n, c],
            recv_a.at[n, c],
            (dp, peer),
        )

    def arriving_attended(n, c):
        place = att_in.at[ds(c * chunk, chunk), ds(peers[n] * local, local)]
        return pltpu.make_async_copy(place, place, recv_a.at[n, c])

    def sent_grad(n, c):
        peer = peers[n]
        return remote(
            att_grad_b.at[ds(c * chunk, chunk), ds(peer * local, local)],
            att_grad_out.at[ds(me * rows + c * chunk, chunk)],
            send_g.at[n, c],
            recv_g.at[n, c],
            (dp, peer),
        )

    def arriving_grad(n, c):
        place = att_grad_out.at[ds(peers[n] * rows + c * chunk, chunk)]
        return pltpu.make_async_copy(place, place, recv_g.at[n, c])

    def own_grad(c):
        return pltpu.make_async_copy(
            att_grad_b.at[ds(c * chunk, chunk), ds(me * local, local)],
            att_grad_out.at[ds(me * rows + c * chunk, chunk)],
            out_sem.at[c, 3],
        )

    def stored(c):
        here = ds(c * chunk, chunk)
        return [
            pltpu.make_async_copy(src.at[here], dst.at[here], out_sem.at[c, n])
            for n, (src, dst) in enumerate(((post_b, post_out), (pre_b, pre_out), (post_cot_b, sum1_out)))
        ]

    for copy in stream(0) + [own_attended()] + local_weights():
        copy.start()
    up_bias[...] = jnp.broadcast_to(as_row(up_bias_ref), up_bias.shape)
    greet([(dp, peer) for peer in peers])
    for n in range(3):
        sent_prm(n).start()
    for c in range(count):
        for n in (2, 1, 0):
            sent_attended(n, c).start()
    for copy in sent_weights():
        copy.start()
    for c in range(1, count):
        for copy in stream(c):
            copy.start()
    up_bias_all[ds(me, 1)] = up_bias[...][None]
    small_out[...] = jnp.zeros_like(small_out)
    own_attended().wait()
    for n in range(3):
        arrived = up_bias_all.at[peers[n]]
        pltpu.make_async_copy(arrived, arrived, recv_p.at[n]).wait()
    for copy in local_weights() + arriving_weights():
        copy.wait()
    for f in range(MP):
        w_out[pl.ds(f * local, local)] = w_all[f, pl.ds(width + hid, local)]

    out_bias, gain1, shift1 = as_row(out_bias_ref), as_row(gain1_ref), as_row(shift1_ref)
    down_bias, gain2, shift2 = as_row(down_bias_ref), as_row(gain2_ref), as_row(shift2_ref)

    def block_steps(c, b):
        here = ds(c * chunk, chunk)
        one = pl.ds(0, 1)
        kept = {}

        def branch_step():
            for n in range(3):
                arriving_attended(n, c).wait()
            for copy in stream(c):
                copy.wait()
            branch_b[b] = dot(att_in[here], w_out[...])

        def norm1_step():
            branch = branch_b[b] + out_bias
            pre_b[here] = pre_b[here] + branch
            normed, inverse = center_and_scale(post_b[here] + branch)
            kept["inverse1"] = inverse
            normed_b[b] = normed
            mid = normed * gain1 + shift1
            branch_b[b] = mid
            mid_low[here] = mid.astype(BF16)

        def up_step(f):
            wide_b[b, f] = dot(mid_low[here], w_all[f, up_rows])

        def gelu_step(f):
            value, slope = gelu_and_slope(wide_b[b, f] + up_bias_all[f, 0:1])
            hidden[f, here] = value.astype(BF16)
            wide_b[b, f] = slope

        def down_step(f):
            part = dot(hidden[f, here], w_all[f, down_rows])
            sum_b[b] = part if f == 0 else sum_b[b] + part

        def norm2_step():
            ffn = sum_b[b] + down_bias
            pre_b[here] = pre_b[here] + ffn
            normed2, inverse2 = center_and_scale(branch_b[b] + ffn)
            post_b[here] = normed2 * gain2 + shift2
            for copy in stored(c)[:2]:
                copy.start()
            cot = post_cot_b[here]
            small_out[4:5] += column_sum(cot * normed2)
            small_out[5:6] += column_sum(cot)
            sum2_grad = norm_backward(cot, normed2, inverse2, gain2)
            sum_b[b] = sum2_grad
            grad = (sum2_grad + pre_cot_b[here]).astype(BF16)
            ffn_grad[here] = grad
            small_out[3:4] += column_sum(grad.astype(F32))

        def rise_step(f):
            rise_b[b, f % 2] = dot(ffn_grad[here], w_all[f, down_rows], NT)

        def act_step(f):
            back = (rise_b[b, f % 2] * wide_b[b, f]).astype(BF16)
            act_grad[f, here] = back
            small_out[8 + f : 9 + f] += column_sum(back.astype(F32))

        def mid_step(f):
            sum_b[b] = sum_b[b] + dot(act_grad[f, here], w_all[f, up_rows], NT)

        def norm1_back_step():
            mid_grad = sum_b[b]
            normed = normed_b[b]
            small_out[1:2] += column_sum(mid_grad * normed)
            small_out[2:3] += column_sum(mid_grad)
            sum1 = norm_backward(mid_grad, normed, kept["inverse1"], gain1)
            post_cot_b[here] = sum1
            grad = (sum1 + pre_cot_b[here]).astype(BF16)
            branch_grad[here] = grad
            small_out[0:1] += column_sum(grad.astype(F32))

        def attended_step():
            att_grad_b[here] = dot(branch_grad[here], w_out[...], NT).astype(BF16)
            for n in (2, 1, 0):
                sent_grad(n, c).start()
            own_grad(c).start()
            stored(c)[2].start()

        steps = [branch_step, norm1_step]
        for t in range(MP + 2):
            for act, f in ((down_step, t - 2), (gelu_step, t - 1), (up_step, t)):
                if 0 <= f < MP:
                    steps.append(functools.partial(act, f))
        steps.append(norm2_step)
        for t in range(MP + 2):
            for act, f in ((mid_step, t - 2), (act_step, t - 1), (rise_step, t)):
                if 0 <= f < MP:
                    steps.append(functools.partial(act, f))
        return steps + [norm1_back_step, attended_step]

    def block_pair(p, _):
        pair = [block_steps(2 * p + b, b) for b in range(2)]
        length = len(pair[0])
        for t in range(length + BLOCK_LAG):
            for b in range(2):
                if 0 <= t - b * BLOCK_LAG < length:
                    pair[b][t - b * BLOCK_LAG]()
        return 0

    lax.fori_loop(0, count // 2, block_pair, 0)

    def weight_grads(s):
        up = dot(mid_low[...], act_grad[s], TN)
        down = dot(hidden[s], ffn_grad[...], TN)
        out = dot(att_in[:, ds(s * local, local)], branch_grad[...], TN)
        return up, down, out

    def sent_sums(n):
        return remote(send_b.at[n], recv_b.at[n], send_r.at[n], recv_r.at[n], (dp, sib))

    for n, owner in enumerate((diagonal, sib)):
        for span, part in zip(spans, weight_grads(owner)):
            send_b[n, span] = part.astype(BF16)
        sent_sums(n).start()
    for span, part in zip(spans, weight_grads(across)):
        keep_b[span] = part
    sent_sums(0).wait_recv()
    ours = ds((dp % 2) * (width // 2), width // 2)
    theirs = ds((1 - dp % 2) * (width // 2), width // 2)
    give_b[...] = (keep_b[...] + recv_b[0].astype(F32)).astype(BF16)
    gives = [
        pltpu.make_async_copy(give_b.at[:, ours], to_across_out, own_sem.at[1]),
        pltpu.make_async_copy(give_b.at[:, theirs], to_corner_out, own_sem.at[2]),
    ]
    for give in gives:
        give.start()
    for span, part in zip(spans, weight_grads(me)):
        keep_b[span] = part
    sent_sums(1).wait_recv()
    keep_b[...] = keep_b[...] + recv_b[1].astype(F32)
    beside_b[...] = keep_b[:, theirs].astype(BF16)
    gives += [
        pltpu.make_async_copy(keep_b.at[:, ours], keep_out, own_sem.at[3]),
        pltpu.make_async_copy(beside_b, to_beside_out, own_sem.at[4]),
    ]
    for give in gives[2:]:
        give.start()
    for c in range(count):
        for copy in stored(c) + [own_grad(c)]:
            copy.wait()
        for n in range(3):
            sent_attended(n, c).wait_send()
            sent_grad(n, c).wait_send()
            arriving_grad(n, c).wait()
    for copy in sent_weights():
        copy.wait_send()
    for n in range(3):
        sent_prm(n).wait_send()
    for n in range(2):
        sent_sums(n).wait_send()
    for give in gives:
        give.wait()


def middle(att, post, pre, post_cot, pre_cot, own, far_line, far_side, vectors):
    rows, width = post.shape
    local = att.shape[1]
    tall = own.shape[0]
    hid = tall - width - local
    count = rows // TILE
    f32 = jax.ShapeDtypeStruct((rows, width), F32)
    return pl.pallas_call(
        middle_kernel,
        out_shape=(
            f32, f32, f32,
            jax.ShapeDtypeStruct(att.shape, BF16),
            jax.ShapeDtypeStruct((tall, width // 2), F32),
            jax.ShapeDtypeStruct((tall, width // 2), BF16),
            jax.ShapeDtypeStruct((tall, width // 2), BF16),
            jax.ShapeDtypeStruct((tall, width // 2), BF16),
            jax.ShapeDtypeStruct((16, width), F32),
        ),
        in_specs=[ANY] * 8 + [VMEM] * len(vectors),
        out_specs=(ANY,) * 8 + (VMEM,),
        scratch_shapes=[
            pltpu.VMEM((rows, width), F32),
            pltpu.VMEM((rows, width), F32),
            pltpu.VMEM((rows, width), F32),
            pltpu.VMEM((rows, width), F32),
            pltpu.VMEM((rows, MP * local), BF16),
            pltpu.VMEM((MP, tall, width), BF16),
            pltpu.VMEM((MP * local, width), BF16),
            pltpu.VMEM((8, hid), F32),
            pltpu.VMEM((MP, 8, hid), F32),
            pltpu.VMEM((rows, width), BF16),
            pltpu.VMEM((MP, rows, hid), BF16),
            pltpu.VMEM((MP, rows, hid), BF16),
            pltpu.VMEM((rows, width), BF16),
            pltpu.VMEM((rows, width), BF16),
            pltpu.VMEM((rows, MP * local), BF16),
            pltpu.VMEM((2, MP, TILE, hid), F32),
            pltpu.VMEM((2, 2, TILE, hid), F32),
            pltpu.VMEM((2, TILE, width), F32),
            pltpu.VMEM((2, TILE, width), F32),
            pltpu.VMEM((2, TILE, width), F32),
            pltpu.VMEM((2, tall, width), BF16),
            pltpu.VMEM((2, tall, width), BF16),
            pltpu.VMEM((tall, width), F32),
            pltpu.VMEM((tall, width), BF16),
            pltpu.VMEM((tall, width // 2), BF16),
            dma_sems(count, 4), dma_sems(5), dma_sems(3), dma_sems(3), dma_sems(3),
            dma_sems(3), dma_sems(3), dma_sems(3, count), dma_sems(3, count),
            dma_sems(3, count), dma_sems(3, count), dma_sems(2), dma_sems(2), dma_sems(count, 4),
        ],
        compiler_params=pltpu.CompilerParams(
            collective_id=1, has_side_effects=True, vmem_limit_bytes=60 << 20
        ),
        cost_estimate=pl.CostEstimate(flops=15 << 30, bytes_accessed=20 << 20, transcendentals=4 << 20),
        name="middle",
    )(att, post, pre, post_cot, pre_cot, own, far_line, far_side, *vectors)


ROW_TIME = 0.0105
HOP_TIME = 2.8
HALF = 256


def sum_plan(dp_size, width, hid, local):
    bits = dp_size.bit_length() - 1
    rest = tuple((b,) for b in range(3, bits))

    def order(*groups):
        groups = tuple(tuple(b for b in group if b < bits) for group in groups)
        return tuple(group for group in groups if group) + rest

    below = hid + local
    rows = [
        (width // 2, order((0,), *PLANS[0]), 1.5, 1), (width // 2, order((0,), *PLANS[1]), 1.6, 1),
        (below // 2, order((0,), *PLANS[2]), 1.7, 1), (below // 2, order((0,), *PLANS[3]), 1.8, 1),
        (width // 2, order(*PLANS[4]), 2.0, 0), (width // 2, order(*PLANS[5]), 2.01, 0),
        (width // 2, order(*PLANS[6]), 2.02, 0),
    ]
    pieces, start = [], 0
    for size, groups, ready, done in rows:
        steps = []
        remaining = size
        for n, group in enumerate(groups):
            ways = 1 << len(group)
            if n < done:
                steps.append((group, ways * size, True))
            elif remaining % (16 * ways) == 0:
                steps.append((group, remaining, True))
                remaining //= ways
            else:
                steps += [((b,), remaining, False) for b in group]
        pieces.append((start, size, ready, steps, done))
        start += size
        if start == width + below:
            start *= 2
    return pieces, start


NEAR, SWAP, FAR = ((0,), (1,), (2,)), ((1,), (0,), (2,)), ((2,), (0,), (1,))
PAIR, ALL = ((0,), (1, 2)), ((0, 1, 2),)
LINE, BACK = ((1,), (2,)), ((2,), (1,))
BOTH = ((1, 2),)
PLANS = (BACK, LINE, BOTH, LINE, NEAR, NEAR, NEAR)
POST_TIME = (34.0, 34.1, 34.2, 38.0)
SMALL_TIME = (0.0, 2.0, 90.0)


def plan_length(steps):
    return len(steps) + sum(split for _, _, split in steps)


def step_times(pieces):
    free = {}
    waiting = [(piece[2], n, piece[4]) for n, piece in enumerate(pieces)]
    times = []
    while waiting:
        now, n, t = min(waiting)
        waiting.remove((now, n, t))
        times.append((now, n, t))
        steps = pieces[n][3]
        if t == plan_length(steps):
            continue
        back = [s for s in reversed(steps) if s[2]]
        group, size, split = steps[t] if t < len(steps) else back[t - len(steps)]
        begin = max([now] + [free.get(b, 0.0) for b in group])
        end = begin
        for b in group:
            cost = size * ROW_TIME * (0.5 if split else 1.0) * (1.0 if b == 0 else 1.5 if len(group) > 1 else b)
            free[b] = begin + cost
            end = max(end, free[b])
        waiting.append((end + HOP_TIME, n, t + 1))
    return times


def flipped(place, mask, bits):
    for b in range(bits):
        if mask >> b & 1:
            place = place + (1 << b) - 2 * (1 << b) * ((place // (1 << b)) % 2)
    return place


def tail_kernel(
    dp_size,
    dq, dk, dv, tok_t, w, sum1, keep, given0, given1, given2, small,
    post_out, full_out, small_out,
    grads, tok_b, w_t, sum1_b, keep_b, given_b, mine, far, send_far, recv_far, pass_far, land_far, send_near, recv_near,
    acc, flight, full, land, small_flight, small_land,
    in_sem, grad_sem, near_send, near_recv, far_send, far_recv, hop_send, hop_recv,
    step_send, step_recv, small_send, small_recv, out_sem, full_sem,
):
    me, sib, across, diagonal = mp_peers()
    dp = lax.axis_index("dp")
    rows, width = sum1.shape
    local = dq.shape[1]
    chunk = TILE
    count = rows // chunk
    tall = keep.shape[0]
    hid = tall - width - local
    bits = dp_size.bit_length() - 1
    pieces, total = sum_plan(dp_size, width, hid, local)

    loads = [
        pltpu.make_async_copy(keep, keep_b, in_sem.at[0]),
        pltpu.make_async_copy(given0, given_b.at[0], in_sem.at[1]),
        pltpu.make_async_copy(given1, given_b.at[1], in_sem.at[2]),
        pltpu.make_async_copy(given2, given_b.at[2], in_sem.at[5]),
        pltpu.make_async_copy(tok_t, tok_b, in_sem.at[3]),
        pltpu.make_async_copy(sum1, sum1_b, in_sem.at[4]),
    ]

    def grad_loads(g, owner):
        here = ds(owner * rows, rows)
        return [
            pltpu.make_async_copy(src.at[here], grads.at[here, pl.ds(n * local, local)], grad_sem.at[g, n])
            for n, src in enumerate((dq, dk, dv))
        ]

    owners = (diagonal, across, sib, me)
    for load in grad_loads(0, diagonal) + loads[:4] + grad_loads(1, across) + grad_loads(2, sib) + grad_loads(3, me):
        load.start()
    for load in loads[4:]:
        load.start()
    for n in range(3):
        w_t[pl.ds(n * local, local)] = w[n].T
    greet([(dp, sib), (dp, across), (dp, diagonal)] + [(flipped(dp, mask, bits), me) for mask in partner_masks(pieces, bits)])

    spots = {}
    ids = {}
    for n, (base, _, _, steps, done) in enumerate(pieces):
        base = jnp.int32(base)
        for t, (group, size, split) in enumerate(steps):
            ways = 1 << len(group)
            part = size // ways if split else size
            places = []
            for m in range(ways):
                mask = sum(1 << b for k, b in enumerate(group) if m >> k & 1)
                there = flipped(dp, mask, bits)
                rank = sum((there // (1 << b)) % 2 * (1 << k) for k, b in enumerate(group))
                places.append((there, base + rank * (tall if t < done else part) if split else base))
                ids[n, t, m] = len(ids)
            spots[n, t] = (places, part)
            base = places[0][1]

    def reduce_copy(n, t, m):
        places, part = spots[n, t]
        there, at = places[m]
        own = places[0][1]
        return remote(
            flight.at[ds16(at, part)], land.at[t, ds16(own, part)],
            step_send.at[0, ids[n, t, m]], step_recv.at[0, ids[n, t, m]], (there, me),
        )

    def reduce_start(n, t):
        places, part = spots[n, t]
        for m in range(1, len(places)):
            here = ds16(places[m][1], part)
            flight[here] = acc[here].astype(BF16)
            reduce_copy(n, t, m).start()

    def reduce_finish(n, t):
        places, part = spots[n, t]
        split = pieces[n][3][t][2]
        own = ds16(places[0][1], part)
        if split:
            value = acc[own]
        else:
            value = flight[own].astype(F32)
        for m in range(1, len(places)):
            there = ds16(places[m][1], part)
            pltpu.make_async_copy(land.at[t, there], land.at[t, there], step_recv.at[0, ids[n, t, m]]).wait()
            value = value + land[t, there].astype(F32)
        acc[own] = value
        for m in range(1, len(places)):
            reduce_copy(n, t, m).wait_send()

    def spread_copy(n, t, m):
        places, part = spots[n, t]
        own = ds16(places[0][1], part)
        return remote(
            full.at[own], full.at[own],
            step_send.at[1, ids[n, t, m]], step_recv.at[1, ids[n, t, m]], (places[m][0], me),
        )

    def spread_start(n, t):
        for m in range(1, len(spots[n, t][0])):
            spread_copy(n, t, m).start()

    def spread_done(n, t):
        places, part = spots[n, t]
        for m in range(1, len(places)):
            there = ds16(places[m][1], part)
            pltpu.make_async_copy(full.at[there], full.at[there], step_recv.at[1, ids[n, t, m]]).wait()
            spread_copy(n, t, m).wait_send()

    def full_copies(n):
        starts = [pieces[n][0] + s * tall for s in range(1 + pieces[n][4])]
        return [
            pltpu.make_async_copy(full.at[pl.ds(start, pieces[n][1])], full_out.at[pl.ds(start, pieces[n][1])], full_sem.at[n, s])
            for s, start in enumerate(starts)
        ]

    def stage(n, t):
        steps = pieces[n][3]
        back = [s for s in range(len(steps) - 1, -1, -1) if steps[s][2]]
        if pieces[n][4] < t <= len(steps):
            reduce_finish(n, t - 1)
        if t < len(steps):
            reduce_start(n, t)
            return
        if t == len(steps):
            places, part = spots[n, len(steps) - 1]
            here = ds16(places[0][1], part)
            full[here] = acc[here].astype(BF16)
        else:
            spread_done(n, back[t - len(steps) - 1])
        if t < plan_length(steps):
            spread_start(n, back[t - len(steps)])
        else:
            for copy in full_copies(n):
                copy.start()

    phases = [[(dp, peer) for peer in (sib, across, diagonal)]]
    for low in range(0, bits, 3):
        high = min(low + 3, bits)
        phases.append([(flipped(dp, mask << low, bits), me) for mask in range(1, 1 << (high - low))])

    def small_copy(s, n):
        return remote(small_flight.at[s], small_land.at[s, n], small_send.at[s, n], small_recv.at[s, n], phases[s][n])

    def ranked(own, arrived, place, ways):
        values = [own] + arrived
        total = None
        for rank in range(ways):
            value = values[0]
            for n in range(1, ways):
                value = jnp.where((place ^ n) == rank, values[n], value)
            total = value if total is None else total + value
        return total

    def small_stage(s):
        if s == 0:
            small_out[...] = small[...]
        else:
            for n in range(len(phases[s - 1])):
                small_copy(s - 1, n).wait()
            arrived = [small_land[s - 1, n] for n in range(len(phases[s - 1]))]
            place = me if s == 1 else (dp // (1 << (3 * (s - 2)))) % 8
            small_out[...] = ranked(small_out[...], arrived, place, len(arrived) + 1)
        if s == 1:
            sums = column_sum(grads[...].astype(F32))
            small_out[12:13] = jnp.concatenate(
                [sums[:, :local], sums[:, 2 * local :], jnp.zeros((1, width - 2 * local), F32)], axis=1
            )
        if s < len(phases):
            small_flight[s] = small_out[...]
            for n in range(len(phases[s])):
                small_copy(s, n).start()

    def far_copy(c):
        return remote(send_far.at[c], recv_far.at[c], far_send.at[c], far_recv.at[c], (dp, sib))

    def hop_copy(c):
        return remote(pass_far.at[c], land_far.at[c], hop_send.at[c], hop_recv.at[c], (dp, across))

    def near_copy(c):
        return remote(send_near.at[c], recv_near.at[c], near_send.at[c], near_recv.at[c], (dp, sib))

    def post_copy(c):
        here = pl.ds(c * chunk, chunk)
        return pltpu.make_async_copy(sum1_b.at[here], post_out.at[here], out_sem.at[c])

    def arrive(g):
        for load in grad_loads(g, owners[g]):
            load.wait()

    def part(g):
        if g < 1:
            arrive(g)
        return dot(grads[ds(owners[g] * rows, rows)], w_t[...]).reshape(count, chunk, width)

    def far_step(n):
        if n == 0:
            send_far[...] = part(0).astype(BF16)
            for c in range(count):
                far_copy(c).start()
        else:
            far[...] = part(1)

    def hop_step(c):
        far_copy(c).wait_recv()
        pass_far[c] = (far[c] + recv_far[c].astype(F32)).astype(BF16)
        hop_copy(c).start()

    def near_step(_):
        send_near[...] = part(2).astype(BF16)
        for c in range(count):
            near_copy(c).start()
        mine[...] = part(3)

    def post_step(c):
        if c == 0:
            loads[5].wait()
        near_copy(c).wait_recv()
        hop_copy(c).wait_recv()
        here = pl.ds(c * chunk, chunk)
        sum1_b[here] = sum1_b[here] + (mine[c] + recv_near[c].astype(F32)) + land_far[c].astype(F32)
        post_copy(c).start()

    def own_sums(_):
        for load in loads[:4]:
            load.wait()
        total = keep_b[...]
        for n in range(3):
            total = total + given_b[n].astype(F32)
        acc[ds16((dp % 2) * tall, tall)] = total

    def weight_step(_):
        loads[4].wait()
        block = dot(tok_b[...], grads[...])
        base = 2 * tall
        acc[pl.ds(base, width)] = block[:, : 2 * local]
        for s in range(2):
            acc[pl.ds(base + width, width // 2), pl.ds(s * local, local)] = block[
                s * width // 2 : (s + 1) * width // 2, 2 * local :
            ]

    events = [(now, 5, stage, (n, t)) for now, n, t in step_times(pieces)]
    events += [
        (1.0, 0, far_step, (0,)), (1.1, 0, own_sums, (0,)),
        (1.9, 0, arrive, (1,)), (1.9, 0, arrive, (2,)), (1.9, 0, arrive, (3,)), (1.95, 0, weight_step, (0,)),
        (2.1, 0, far_step, (1,)), (3.3, 0, near_step, (0,)),
    ]
    for c in range(count):
        events.append((2.2 + 0.1 * c, 1, hop_step, (c,)))
        events.append((POST_TIME[c], 7, post_step, (c,)))
    for s in range(len(phases) + 1):
        events.append((SMALL_TIME[min(s, 2)] + s, 4, small_stage, (s,)))
    for _, _, act, where in sorted(events, key=lambda event: event[:2] + (event[3],)):
        act(*where)

    for c in range(count):
        far_copy(c).wait_send()
        hop_copy(c).wait_send()
        near_copy(c).wait_send()
        post_copy(c).wait()
    for n in range(len(pieces)):
        for copy in full_copies(n):
            copy.wait()


def ds1(start):
    return pl.ds(start, 1)


def partner_masks(pieces, bits):
    masks = {mask << low for low in range(0, bits, 3) for mask in range(1, 1 << min(3, bits - low))}
    for _, _, _, steps, _ in pieces:
        for group, _, _ in steps:
            for m in range(1, 1 << len(group)):
                masks.add(sum(1 << b for k, b in enumerate(group) if m >> k & 1))
            masks.update(1 << b for b in group)
    return sorted(masks)


def tail(dp_size, dq, dk, dv, tok_t, w, sum1, keep, given, small):
    rows, width = sum1.shape
    group, local = dq.shape
    tall = keep.shape[0]
    hid = tall - width - local
    count = rows // TILE
    bits = dp_size.bit_length() - 1
    assert 1 << bits == dp_size and bits > 0
    pieces, total = sum_plan(dp_size, width, hid, local)
    blocks = (count, TILE, width)
    phases = 1 + (bits + 2) // 3
    longest = max(len(piece[3]) for piece in pieces)
    copies = sum(1 << len(step[0]) for piece in pieces for step in piece[3])
    return pl.pallas_call(
        functools.partial(tail_kernel, dp_size),
        out_shape=(
            jax.ShapeDtypeStruct((rows, width), F32),
            jax.ShapeDtypeStruct((total, HALF), BF16),
            jax.ShapeDtypeStruct(small.shape, F32),
        ),
        in_specs=[ANY] * 4 + [VMEM] + [ANY] * 5 + [VMEM],
        out_specs=(ANY, ANY, VMEM),
        scratch_shapes=[
            pltpu.VMEM((group, 3 * local), BF16),
            pltpu.VMEM((width, group), BF16),
            pltpu.VMEM((3 * local, width), BF16),
            pltpu.VMEM((rows, width), F32),
            pltpu.VMEM((tall, HALF), F32),
            pltpu.VMEM((3, tall, HALF), BF16),
            pltpu.VMEM(blocks, F32),
            pltpu.VMEM(blocks, F32),
            pltpu.VMEM(blocks, BF16),
            pltpu.VMEM(blocks, BF16),
            pltpu.VMEM(blocks, BF16),
            pltpu.VMEM(blocks, BF16),
            pltpu.VMEM(blocks, BF16),
            pltpu.VMEM(blocks, BF16),
            pltpu.VMEM((total, HALF), F32),
            pltpu.VMEM((total, HALF), BF16),
            pltpu.VMEM((total, HALF), BF16),
            pltpu.VMEM((longest, total, HALF), BF16),
            pltpu.VMEM((phases,) + small.shape, F32),
            pltpu.VMEM((phases, 7) + small.shape, F32),
            dma_sems(6), dma_sems(4, 3), dma_sems(count), dma_sems(count), dma_sems(count), dma_sems(count),
            dma_sems(count), dma_sems(count), dma_sems(2, copies), dma_sems(2, copies),
            dma_sems(phases, 7), dma_sems(phases, 7), dma_sems(count), dma_sems(len(pieces), 2),
        ],
        compiler_params=pltpu.CompilerParams(
            collective_id=2, has_side_effects=True, vmem_limit_bytes=60 << 20
        ),
        cost_estimate=pl.CostEstimate(flops=4 << 30, bytes_accessed=20 << 20, transcendentals=0),
        name="tail",
    )(dq, dk, dv, tok_t, w, sum1, keep, *given, small)


def finish_kernel(
    post_sum, full, small,
    post_grad, qkv_grad, up_grad, down_grad, out_grad,
    query_grad, value_grad, out_bias, gain1, shift1, up_bias, down_bias, gain2, shift2,
    post_b, full_b, grad_b, qkv_b, sem, post_sem, out_sem,
):
    me = lax.axis_index("mp")
    total, _ = full.shape
    rows, width = post_sum.shape
    local = query_grad.shape[0]
    hid = down_grad.shape[0]
    tall = width + hid + local
    count = 4

    def post_in(c):
        here = pl.ds(c * rows // count, rows // count)
        return pltpu.make_async_copy(post_sum.at[here], post_b.at[here], post_sem.at[0, c])

    def post_out(c):
        here = pl.ds(c * rows // count, rows // count)
        return pltpu.make_async_copy(post_b.at[here], post_grad.at[here], post_sem.at[1, c])

    spans = ((0, width, up_grad), (width, hid, down_grad), (width + hid, local, out_grad))

    def full_in(s, n):
        start, size = (s * tall + spans[n][0], spans[n][1]) if n < 3 else (2 * tall, total - 2 * tall)
        here = pl.ds(start, size)
        return pltpu.make_async_copy(full.at[here], full_b.at[here], sem.at[s, n])

    parts = [(s, n) for n in range(3) for s in range(2)] + [(0, 3)]
    for c in range(count):
        post_in(c).start()
    for s, n in parts:
        full_in(s, n).start()
    for row, vector in enumerate((out_bias, gain1, shift1, down_bias, gain2, shift2)):
        vector[...] = small[row]
    own = small[12:13]
    query_grad[...] = own[0, :local]
    value_grad[...] = own[0, local : 2 * local]
    up_bias[...] = small[pl.ds(8 + me, 1), :][0]
    stores = []
    for c in range(count):
        post_in(c).wait()
        stores.append(post_out(c))
        stores[-1].start()
    for n, (start, size, dst) in enumerate(spans):
        for s in range(2):
            full_in(s, n).wait()
            grad_b[pl.ds(start, size), pl.ds(s * HALF, HALF)] = full_b[pl.ds(s * tall + start, size)].astype(F32)
        stores.append(pltpu.make_async_copy(grad_b.at[pl.ds(start, size)], dst, out_sem.at[n]))
        stores[-1].start()
    full_in(0, 3).wait()
    for m in range(2):
        qkv_b[m] = full_b[pl.ds(2 * tall, width), pl.ds(m * local, local)].astype(F32)
    for s in range(2):
        qkv_b[2, pl.ds(s * width // 2, width // 2)] = full_b[
            pl.ds(2 * tall + width, width // 2), pl.ds(s * local, local)
        ].astype(F32)
    stores.append(pltpu.make_async_copy(qkv_b, qkv_grad, out_sem.at[3]))
    stores[-1].start()
    for store in stores:
        store.wait()


def finish(post_sum, full, small, hid, local):
    rows, width = post_sum.shape
    total = full.shape[0]
    tall = width + hid + local
    vector = lambda size: jax.ShapeDtypeStruct((size,), F32)
    return pl.pallas_call(
        finish_kernel,
        out_shape=(
            jax.ShapeDtypeStruct((rows, width), F32),
            jax.ShapeDtypeStruct((3, width, local), F32),
            jax.ShapeDtypeStruct((width, hid), F32),
            jax.ShapeDtypeStruct((hid, width), F32),
            jax.ShapeDtypeStruct((local, width), F32),
            vector(local), vector(local), vector(width), vector(width), vector(width),
            vector(hid), vector(width), vector(width), vector(width),
        ),
        in_specs=[ANY, ANY, VMEM],
        out_specs=(ANY,) * 5 + (VMEM,) * 9,
        scratch_shapes=[
            pltpu.VMEM((rows, width), F32),
            pltpu.VMEM((total, HALF), BF16),
            pltpu.VMEM((tall, width), F32),
            pltpu.VMEM((3, width, local), F32),
            dma_sems(2, 4), dma_sems(2, 4), dma_sems(4),
        ],
        compiler_params=pltpu.CompilerParams(vmem_limit_bytes=60 << 20),
        name="results",
    )(post_sum, full, small)


def body(
    dp_size,
    post_stream,
    pre_stream,
    seq_lengths,
    qkv_weight,
    query_bias,
    value_bias,
    out_weight,
    out_bias,
    norm1_gain,
    norm1_shift,
    up_weight,
    up_bias,
    down_weight,
    down_bias,
    norm2_gain,
    norm2_shift,
    post_cotan,
    pre_cotan,
):
    local = out_weight.shape[0]
    hid = down_weight.shape[0]
    qkv3 = jnp.transpose(qkv_weight, (1, 0, 2))
    tok_t, queries, k, v, kt, vt, starts, limits, own, far_line = gather_and_project(
        dp_size, seq_lengths, post_stream, qkv3, query_bias, value_bias, (up_weight, down_weight, out_weight)
    )
    across = [(m, (m + 2) % MP) for m in range(MP)]
    beside = [(d, d + 1 - 2 * (d % 2)) for d in range(dp_size)]
    corner = [(d * MP + m, e * MP + n) for d, e in beside for m, n in across]
    far_side = lax.ppermute(far_line, "dp", beside)
    att, lse, tiles, counts = attend(limits, starts, queries, k, vt)
    vectors = (out_bias, norm1_gain, norm1_shift, down_bias, norm2_gain, norm2_shift, up_bias)
    post_mid, pre_mid, sum1, att_grad, keep, to_across, to_beside, to_corner, small = middle(
        att, post_stream, pre_stream, post_cotan, pre_cotan, own, far_line, far_side, vectors
    )
    given = (
        lax.ppermute(to_across, "mp", across),
        lax.ppermute(to_beside, "dp", beside),
        lax.ppermute(to_corner, ("dp", "mp"), corner),
    )
    dq, dk, dv, post_out, pre_out = attend_back(
        tiles, counts, starts, lse, queries, k, v, kt, att, att_grad, post_mid, pre_mid
    )
    post_sum, full, small = tail(dp_size, dq, dk, dv, tok_t, qkv3, sum1, keep, given, small)
    (
        post_grad, qkv_grad, up_grad, down_grad, out_grad,
        query_grad, value_grad, out_bias_grad, gain1, shift1, up_bias_grad, down_bias_grad, gain2, shift2,
    ) = finish(post_sum, full, small, hid, local)
    return (
        post_out, pre_out, post_grad, jnp.transpose(qkv_grad, (1, 0, 2)), query_grad, value_grad, out_grad,
        out_bias_grad, gain1, shift1, up_grad, up_bias_grad, down_grad, down_bias_grad, gain2, shift2,
    )


def solution(mesh):
    tokens = P(("dp", "mp"), None)
    vector = P()
    return jax.shard_map(
        functools.partial(body, mesh.shape["dp"]),
        mesh=mesh,
        in_specs=(
            tokens, tokens, P("dp", None), P(None, None, "mp"), P("mp"), P("mp"), P("mp", None),
            vector, vector, vector, P(None, "mp"), P("mp"), P("mp", None), vector, vector, vector,
            tokens, tokens,
        ),
        out_specs=(
            tokens, tokens, tokens, P(None, None, "mp"), P("mp"), P("mp"), P("mp", None),
            vector, vector, vector, P(None, "mp"), P("mp"), P("mp", None), vector, vector, vector,
        ),
        check_vma=False,
    )
```
